32 devices in a mesh: groups: 2 (over y), blk: 4 (over z), shard: 2 (over x), sub: 2 (over core).
Axes of the slice: x: 2, y: 2, z: 4, core: 2. Of those that a mesh axis runs over, the one named last changes fastest.
Arguments:
- embeddings: bfloat16 [4096, 1024], P(('groups', 'blk', 'shard', 'sub')), parts along dimension 0, may hold values from -100 to 100
- assignment: int32 [4096, 1], P(('groups', 'blk', 'shard', 'sub')), parts along dimension 0, may hold values from 0 to 15, as said below
Outputs:
- best_similarity: float32 [4096], P(('groups', 'blk', 'shard', 'sub')), parts along dimension 0
The draws below stay inside these ranges and needn't reach their ends.
There are 2 independent parts, one for each index of `groups`. The reference program is written for one: setup_inputs(seed, part) draws one part's arguments, and reference() takes and returns one part's arrays. A program takes and returns all parts, laid end to end along the dimension named above; each array names one. Nothing has to cross between parts.
Inputs may be any that keep to these rules, and one draw needn't show every extreme that they name: `assignment`: among the 128 rows of one device at most 16 belong to one cluster; one cluster has exactly 16 rows on every device; every cluster has at least one row in the group.
All inputs are finite; a program needn't handle non-finite values.
Results may differ from the reference program's by a relative error of at most 0.0013.
Values may be sent and summed in bfloat16 or wider, within the bound.
No kernel may reach another device: no remote copies, remote signals or barrier semaphores. Data moves between devices by JAX's collectives and lax.ppermute only.
A program may use at most 64 MiB of HBM per device.

```python
import math
import jax
import jax.numpy as jnp
from jax import lax

D = 1024
CLUSTERS = 16
CAP = 16
ROWS_DEV = 128
ROWS = 2048


def draw_embeddings(key, part):
    key = jax.random.fold_in(key, 11)
    key_pool, key_pick, key_twin, key_twinpick, key_fresh, key_weight = jax.random.split(key, 6)
    coarse_count = 8
    twin_count = max(ROWS // 64, 1)
    coarse = jax.random.normal(key_pool, (coarse_count, D), jnp.float32)
    coarse_pick = jax.random.randint(key_pick, (ROWS,), 0, coarse_count)
    twins = jax.random.normal(key_twin, (twin_count, D), jnp.float32)
    twin_pick = jax.random.randint(key_twinpick, (ROWS,), 0, twin_count)
    tail_start = D // 4
    tail_mask = (jnp.arange(D) >= tail_start).astype(jnp.float32)[None, :]
    tail_boost = float(D) / float(D - tail_start)
    weights = jax.random.uniform(key_weight, (ROWS, 2), jnp.float32, 0.0, 1.0)
    alpha = 0.15 + 0.3 * weights[:, 0:1]
    beta = 0.3 + 0.2 * weights[:, 1:2]
    rest = 1.0 - alpha - beta
    fresh = jax.random.normal(key_fresh, (ROWS, D), jnp.float32)
    rows_out = jnp.sqrt(alpha) * coarse[coarse_pick] + jnp.sqrt(beta * tail_boost) * twins[twin_pick] * tail_mask + jnp.sqrt(rest) * fresh
    rows_out = jnp.clip(rows_out, -100.0, 100.0)
    return rows_out.astype(jnp.bfloat16)


def draw_assignment(key, part):
    key = jax.random.fold_in(key, 23)
    key_order, key_score, key_lone, key_row = jax.random.split(key, 4)
    device_count = ROWS // ROWS_DEV
    slot_total = CLUSTERS * CAP
    order = jax.random.permutation(key_order, CLUSTERS).astype(jnp.int32)
    lonely = order[CLUSTERS - 1]
    common = order[0]
    labels = jnp.arange(CLUSTERS, dtype=jnp.int32)
    ranks_of = jnp.sum(jnp.where(order[None, :] == labels[:, None], labels[None, :], 0), axis=1)
    slot_ids = jnp.arange(slot_total, dtype=jnp.int32)
    slot_cluster = slot_ids // CAP
    slot_place = slot_ids % CAP
    device_ids = jnp.arange(device_count, dtype=jnp.int32)
    rotating = order[1 + device_ids % (CLUSTERS - 2)]
    base = jax.random.randint(key_score, (device_count, slot_total), 0, 2 ** 20, dtype=jnp.int32)
    base = base // (1 + ranks_of[slot_cluster])[None, :]
    forced = (slot_cluster == common)[None, :] | (slot_cluster[None, :] == rotating[:, None]) & (slot_place[None, :] == 0)
    score = jnp.where(forced, 2 ** 21, base)
    score = jnp.where((slot_cluster == lonely)[None, :], -1, score)
    ranked = score * slot_total + slot_ids[None, :]
    top_values, picked = lax.top_k(ranked, ROWS_DEV)
    chosen = (picked // CAP).astype(jnp.int32)
    lone_device = jax.random.randint(key_lone, (), 0, device_count, dtype=jnp.int32)
    last_column = jnp.arange(ROWS_DEV, dtype=jnp.int32) == ROWS_DEV - 1
    chosen = jnp.where((device_ids[:, None] == lone_device) & last_column[None, :], lonely, chosen)
    shuffle_keys = jax.random.randint(key_row, (device_count, ROWS_DEV), 0, 2 ** 20, dtype=jnp.int32) * ROWS_DEV + jnp.arange(ROWS_DEV, dtype=jnp.int32)[None, :]
    row_order = jnp.argsort(shuffle_keys, axis=1, stable=True)
    chosen = jnp.take_along_axis(chosen, row_order, axis=1)
    return chosen.reshape(ROWS, 1).astype(jnp.int32)


def setup_inputs(seed: int = 0, part: int = 0) -> dict:
    arg_keys = jax.random.split(jax.random.key(seed), 3)
    part_splits = jax.random.split(jax.random.fold_in(arg_keys[2], part), 3)
    embeddings = draw_embeddings(jax.random.fold_in(jax.random.fold_in(arg_keys[2], part), 71), part)
    assignment = draw_assignment(jax.random.fold_in(jax.random.fold_in(arg_keys[2], part), 71), part)
    return dict(embeddings=embeddings, assignment=assignment)


def normalize(embeddings):
    values = embeddings.astype(jnp.float32)
    scaled = values * lax.rsqrt(lax.optimization_barrier(jnp.mean(values * values, axis=1, keepdims=True)) + 1e-06)
    return (scaled * (1.0 / math.sqrt(values.shape[1]))).astype(jnp.bfloat16)

def reference(embeddings, assignment):
    unit = normalize(embeddings)
    cluster = assignment[:, 0]
    row_ids = jnp.arange(ROWS, dtype=jnp.int32)
    span_rows = math.gcd(ROWS, 1024)

    def one_block(begin_at):
        block_rows = lax.dynamic_slice_in_dim(unit, begin_at, span_rows, 0)
        block_cluster = lax.dynamic_slice_in_dim(cluster, begin_at, span_rows, 0)
        block_ids = lax.dynamic_slice_in_dim(row_ids, begin_at, span_rows, 0)
        similar = lax.dot_general(block_rows, unit, (((1,), (1,)), ((), ())), preferred_element_type=jnp.float32)
        allowed = (block_cluster[:, None] == cluster[None, :]) & (block_ids[:, None] != row_ids[None, :])
        return lax.optimization_barrier(jnp.max(jnp.where(allowed, similar, -2.0), axis=1))
    block_starts = (jnp.arange(ROWS // span_rows) * span_rows).astype(jnp.int32)
    return lax.map(one_block, block_starts).reshape(ROWS)
```

```python
import functools
import math

import jax
import jax.numpy as jnp
from jax import lax
from jax.experimental import pallas as pl
from jax.experimental.pallas import tpu as pltpu
from jax.sharding import PartitionSpec as P

CLUSTERS = 16
CAP = 16
SLOTS = CLUSTERS * CAP
LANES = 128
EMPTY = 4.0
NONE = -2.0

VMEM = pl.BlockSpec(memory_space=pltpu.VMEM)


def placement(cluster):
    rows = cluster.shape[1]
    label = lax.broadcasted_iota(jnp.int32, (CLUSTERS, rows), 0)
    member = (cluster == label).astype(jnp.float32)
    before = lax.broadcasted_iota(jnp.int32, (rows, rows), 0) < lax.broadcasted_iota(
        jnp.int32, (rows, rows), 1
    )
    earlier = jnp.dot(
        member.astype(jnp.bfloat16),
        before.astype(jnp.float32).astype(jnp.bfloat16),
        preferred_element_type=jnp.float32,
    )
    within = jnp.sum(earlier * member, axis=0, keepdims=True).astype(jnp.int32)
    target = cluster * CAP + within
    return lax.broadcasted_iota(jnp.int32, (SLOTS, rows), 0) == target


def pack_kernel(rows_ref, cluster_ref, out_ref):
    values = rows_ref[...].astype(jnp.float32)
    width = values.shape[1]
    scaled = values * lax.rsqrt(jnp.mean(values * values, axis=1, keepdims=True) + 1e-06)
    unit = (scaled * (1.0 / math.sqrt(width))).astype(jnp.bfloat16)
    placed = placement(cluster_ref[...]).astype(jnp.float32)
    slots = jnp.dot(placed.astype(jnp.bfloat16), unit, preferred_element_type=jnp.float32)
    used = jnp.sum(placed, axis=1, keepdims=True)
    first = lax.broadcasted_iota(jnp.int32, slots.shape, 1) == 0
    slots = jnp.where(first & (used < 0.5), EMPTY, slots)
    out_ref[...] = slots.astype(jnp.bfloat16)


def pack(embeddings, assignment):
    rows, width = embeddings.shape
    return pl.pallas_call(
        pack_kernel,
        out_shape=jax.ShapeDtypeStruct((SLOTS, width), jnp.bfloat16),
        in_specs=[VMEM] * 2,
        out_specs=VMEM,
        name="pack",
    )(embeddings, assignment.reshape(1, rows))


def best_kernel(count, slots_ref, others_ref, first_ref, out_ref, best_ref):
    step = pl.program_id(0)
    slots, others = slots_ref[...], others_ref[...]
    similar = lax.dot_general(
        others, slots, (((1,), (1,)), ((), ())), preferred_element_type=jnp.float32
    )
    used = others[:, :1].astype(jnp.float32) < 2.0
    row = lax.broadcasted_iota(jnp.int32, similar.shape, 0)
    column = lax.broadcasted_iota(jnp.int32, similar.shape, 1)
    kept = used & (row + step * slots.shape[0] != column + first_ref[0, 0])
    if count > CAP:
        kept = kept & (row % count // CAP == column % count // CAP)
    best = jnp.max(jnp.where(kept, similar, NONE), axis=0, keepdims=True)

    @pl.when(step == 0)
    def _():
        best_ref[...] = best

    @pl.when(step > 0)
    def _():
        best_ref[...] = jnp.maximum(best_ref[...], best)

    @pl.when(step == pl.num_programs(0) - 1)
    def _():
        for source in range(out_ref.shape[0]):
            piece = best_ref[:, source * count : (source + 1) * count]
            out_ref[source, :, :count] = jnp.broadcast_to(piece, (8, count))
            if count < LANES:
                out_ref[source, :, count:] = jnp.full((8, LANES - count), NONE)


def best_of(slots, others, first, owners):
    size, width = slots.shape
    count = size // owners
    return pl.pallas_call(
        functools.partial(best_kernel, count),
        grid=(others.shape[0] // size,),
        out_shape=jax.ShapeDtypeStruct((owners, 8, LANES), jnp.float32),
        in_specs=[
            pl.BlockSpec((size, width), lambda i: (0, 0)),
            pl.BlockSpec((size, width), lambda i: (i, 0)),
            pl.BlockSpec((1, 1), lambda i: (0, 0), memory_space=pltpu.SMEM),
        ],
        out_specs=pl.BlockSpec((owners, 8, LANES), lambda i: (0, 0, 0)),
        scratch_shapes=[pltpu.VMEM((1, size), jnp.float32)],
        name="best",
    )(slots, others, first)


def unpack_kernel(returned_ref, cluster_ref, out_ref):
    owners = returned_ref.shape[0]
    count = SLOTS // owners
    placed = placement(cluster_ref[...])
    returned = jnp.broadcast_to(returned_ref[:, :1, :], (owners, count, LANES)).reshape(SLOTS, LANES)
    slot = lax.broadcasted_iota(jnp.int32, (SLOTS, LANES), 0) % count
    lane = lax.broadcasted_iota(jnp.int32, (SLOTS, LANES), 1)
    by_slot = jnp.max(jnp.where(slot == lane, returned, NONE), axis=1, keepdims=True)
    out_ref[...] = jnp.max(jnp.where(placed, by_slot, NONE), axis=0, keepdims=True)


def unpack(returned, assignment):
    rows = assignment.shape[0]
    return pl.pallas_call(
        unpack_kernel,
        out_shape=jax.ShapeDtypeStruct((1, rows), jnp.float32),
        in_specs=[VMEM] * 2,
        out_specs=VMEM,
        name="unpack",
    )(returned, assignment.reshape(1, rows))


def local(route, gather, embeddings, assignment):
    send = pack(embeddings, assignment)
    got = lax.all_to_all(send, route, split_axis=0, concat_axis=0, tiled=True)
    owners = lax.axis_size(route)
    if gather:
        others = lax.all_gather(got, gather, axis=0, tiled=True)
        first = (lax.axis_index(gather) * SLOTS).astype(jnp.int32).reshape(1, 1)
    else:
        others, first = got, jnp.zeros((1, 1), jnp.int32)
    best = best_of(got, others, first, owners)
    returned = lax.all_to_all(best, route, split_axis=0, concat_axis=0, tiled=True)
    return unpack(returned, assignment).reshape(-1)


def solution(mesh):
    placed = (
        P(("groups", "blk", "shard", "sub"), None),
        P(("groups", "blk", "shard", "sub"), None),
    )
    axes = ("blk", "shard", "sub")
    split = 3 if CLUSTERS % math.prod(mesh.shape[a] for a in axes) == 0 else 1
    return jax.shard_map(
        functools.partial(local, axes[:split], axes[split:]),
        mesh=mesh,
        in_specs=placed,
        out_specs=P(("groups", "blk", "shard", "sub")),
        check_vma=False,
    )
```

```python
import functools
import math

import jax
import jax.numpy as jnp
from jax import lax
from jax.experimental import pallas as pl
from jax.experimental.pallas import tpu as pltpu
from jax.sharding import PartitionSpec as P

CLUSTERS = 16
CAP = 16
SLOTS = CLUSTERS * CAP
LANES = 128
EMPTY = 4.0
NONE = -2.0
AXES = ("blk", "shard", "sub")

VMEM = pl.BlockSpec(memory_space=pltpu.VMEM)
SMEM = pl.BlockSpec(memory_space=pltpu.SMEM)


def placement(cluster, flip):
    rows = cluster.shape[1]
    label = lax.broadcasted_iota(jnp.int32, (CLUSTERS, rows), 0)
    member = (cluster == label).astype(jnp.float32)
    before = lax.broadcasted_iota(jnp.int32, (rows, rows), 0) < lax.broadcasted_iota(
        jnp.int32, (rows, rows), 1
    )
    earlier = jnp.dot(
        member.astype(jnp.bfloat16),
        before.astype(jnp.float32).astype(jnp.bfloat16),
        preferred_element_type=jnp.float32,
    )
    within = jnp.sum(earlier * member, axis=0, keepdims=True).astype(jnp.int32)
    target = (cluster ^ flip) * CAP + within
    return lax.broadcasted_iota(jnp.int32, (SLOTS, rows), 0) == target


def pack_kernel(flip_ref, rows_ref, cluster_ref, *out_refs):
    values = rows_ref[...].astype(jnp.float32)
    width = values.shape[1]
    scaled = values * lax.rsqrt(jnp.mean(values * values, axis=1, keepdims=True) + 1e-06)
    unit = (scaled * (1.0 / math.sqrt(width))).astype(jnp.bfloat16)
    placed = placement(cluster_ref[...], flip_ref[0, 0]).astype(jnp.float32)
    slots = jnp.dot(placed.astype(jnp.bfloat16), unit, preferred_element_type=jnp.float32)
    used = jnp.sum(placed, axis=1, keepdims=True)
    first = lax.broadcasted_iota(jnp.int32, slots.shape, 1) == 0
    slots = jnp.where(first & (used < 0.5), EMPTY, slots).astype(jnp.bfloat16)
    count = SLOTS // len(out_refs)
    for block, out_ref in enumerate(out_refs):
        out_ref[...] = slots[block * count : (block + 1) * count]


def pack(flip, embeddings, assignment, blocks):
    rows, width = embeddings.shape
    return pl.pallas_call(
        pack_kernel,
        out_shape=[jax.ShapeDtypeStruct((SLOTS // blocks, width), jnp.bfloat16)] * blocks,
        in_specs=[SMEM, VMEM, VMEM],
        out_specs=[VMEM] * blocks,
        name="pack",
    )(flip, embeddings, assignment.reshape(1, rows))


def best_kernel(*refs):
    half = len(refs) // 2
    slots = jnp.concatenate([ref[...] for ref in refs[:half]], axis=0)
    similar = lax.dot_general(
        slots, slots, (((1,), (1,)), ((), ())), preferred_element_type=jnp.float32
    )
    used = slots[:, :1].astype(jnp.float32) < 2.0
    row = lax.broadcasted_iota(jnp.int32, similar.shape, 0)
    column = lax.broadcasted_iota(jnp.int32, similar.shape, 1)
    best = jnp.max(jnp.where(used & (row != column), similar, NONE), axis=0, keepdims=True)
    for block, out_ref in enumerate(refs[half:]):
        piece = best[:, block * CAP : (block + 1) * CAP]
        out_ref[:, :CAP] = jnp.broadcast_to(piece, (8, CAP))
        out_ref[:, CAP:] = jnp.full((8, LANES - CAP), NONE)


def best_of(blocks):
    return pl.pallas_call(
        best_kernel,
        out_shape=[jax.ShapeDtypeStruct((8, LANES), jnp.float32)] * len(blocks),
        in_specs=[VMEM] * len(blocks),
        out_specs=[VMEM] * len(blocks),
        name="best",
    )(*blocks)


def shared_best_kernel(count, first_ref, slots_ref, others_ref, out_ref, best_ref):
    step = pl.program_id(0)
    slots, others = slots_ref[...], others_ref[...]
    similar = lax.dot_general(
        others, slots, (((1,), (1,)), ((), ())), preferred_element_type=jnp.float32
    )
    used = others[:, :1].astype(jnp.float32) < 2.0
    row = lax.broadcasted_iota(jnp.int32, similar.shape, 0)
    column = lax.broadcasted_iota(jnp.int32, similar.shape, 1)
    kept = used & (row + step * slots.shape[0] != column + first_ref[0, 0])
    kept = kept & (row % count // CAP == column % count // CAP)
    best = jnp.max(jnp.where(kept, similar, NONE), axis=0, keepdims=True)

    @pl.when(step == 0)
    def _():
        best_ref[...] = best

    @pl.when(step > 0)
    def _():
        best_ref[...] = jnp.maximum(best_ref[...], best)

    @pl.when(step == pl.num_programs(0) - 1)
    def _():
        for source in range(out_ref.shape[0]):
            piece = best_ref[:, source * count : (source + 1) * count]
            out_ref[source, :, :count] = jnp.broadcast_to(piece, (8, count))
            if count < LANES:
                out_ref[source, :, count:] = jnp.full((8, LANES - count), NONE)


def shared_best_of(slots, others, first, owners):
    size, width = slots.shape
    return pl.pallas_call(
        functools.partial(shared_best_kernel, size // owners),
        grid=(others.shape[0] // size,),
        out_shape=jax.ShapeDtypeStruct((owners, 8, LANES), jnp.float32),
        in_specs=[
            pl.BlockSpec((1, 1), lambda i: (0, 0), memory_space=pltpu.SMEM),
            pl.BlockSpec((size, width), lambda i: (0, 0)),
            pl.BlockSpec((size, width), lambda i: (i, 0)),
        ],
        out_specs=pl.BlockSpec((owners, 8, LANES), lambda i: (0, 0, 0)),
        scratch_shapes=[pltpu.VMEM((1, size), jnp.float32)],
        name="shared_best",
    )(first, slots, others)


def unpack_kernel(flip_ref, cluster_ref, *refs):
    returned_refs, out_ref = refs[:-1], refs[-1]
    count = SLOTS // len(returned_refs)
    placed = placement(cluster_ref[...], flip_ref[0, 0])
    returned = jnp.concatenate(
        [jnp.broadcast_to(ref[:1, :], (count, LANES)) for ref in returned_refs], axis=0
    )
    slot = lax.broadcasted_iota(jnp.int32, (SLOTS, LANES), 0) % count
    lane = lax.broadcasted_iota(jnp.int32, (SLOTS, LANES), 1)
    by_slot = jnp.max(jnp.where(slot == lane, returned, NONE), axis=1, keepdims=True)
    out_ref[...] = jnp.max(jnp.where(placed, by_slot, NONE), axis=0, keepdims=True)


def unpack(flip, returned, assignment):
    rows = assignment.shape[0]
    return pl.pallas_call(
        unpack_kernel,
        out_shape=jax.ShapeDtypeStruct((1, rows), jnp.float32),
        in_specs=[SMEM, VMEM] + [VMEM] * len(returned),
        out_specs=VMEM,
        name="unpack",
    )(flip, assignment.reshape(1, rows), *returned).reshape(-1)


def exchange(blocks):
    size = len(blocks)
    return [blocks[0]] + [
        lax.ppermute(blocks[r], AXES, [(i, i ^ r) for i in range(size)]) for r in range(1, size)
    ]


def one_owner(embeddings, assignment):
    flip = lax.axis_index(AXES).astype(jnp.int32).reshape(1, 1)
    sent = pack(flip, embeddings, assignment, CLUSTERS)
    best = best_of(exchange(sent))
    return unpack(flip, exchange(best), assignment)


def shared_owner(embeddings, assignment):
    route, gather = AXES[:1], AXES[1:]
    owners = lax.axis_size(route)
    flip = jnp.zeros((1, 1), jnp.int32)
    (sent,) = pack(flip, embeddings, assignment, 1)
    got = lax.all_to_all(sent, route, split_axis=0, concat_axis=0, tiled=True)
    others = lax.all_gather(got, gather, axis=0, tiled=True)
    first = (lax.axis_index(gather) * SLOTS).astype(jnp.int32).reshape(1, 1)
    best = shared_best_of(got, others, first, owners)
    returned = lax.all_to_all(best, route, split_axis=0, concat_axis=0, tiled=True)
    return unpack(flip, [returned[i] for i in range(owners)], assignment)


def solution(mesh):
    placed = (
        P(("groups", "blk", "shard", "sub"), None),
        P(("groups", "blk", "shard", "sub"), None),
    )
    one = math.prod(mesh.shape[axis] for axis in AXES) == CLUSTERS
    return jax.shard_map(
        one_owner if one else shared_owner,
        mesh=mesh,
        in_specs=placed,
        out_specs=P(("groups", "blk", "shard", "sub")),
        check_vma=False,
    )
```

```python
import functools
import math

import jax
import jax.numpy as jnp
from jax import lax
from jax.experimental import pallas as pl
from jax.experimental.pallas import tpu as pltpu
from jax.sharding import PartitionSpec as P

CLUSTERS = 16
CAP = 16
SLOTS = CLUSTERS * CAP
LANES = 128
EMPTY = 4.0
NONE = -2.0
TAIL = 8
AXES = ("blk", "shard", "sub")

VMEM = pl.BlockSpec(memory_space=pltpu.VMEM)
SMEM = pl.BlockSpec(memory_space=pltpu.SMEM)


def placement(cluster, flip):
    rows = cluster.shape[1]
    label = lax.broadcasted_iota(jnp.int32, (CLUSTERS, rows), 0)
    member = (cluster == label).astype(jnp.float32)
    before = lax.broadcasted_iota(jnp.int32, (rows, rows), 0) < lax.broadcasted_iota(
        jnp.int32, (rows, rows), 1
    )
    earlier = jnp.dot(
        member.astype(jnp.bfloat16),
        before.astype(jnp.float32).astype(jnp.bfloat16),
        preferred_element_type=jnp.float32,
    )
    within = jnp.sum(earlier * member, axis=0, keepdims=True).astype(jnp.int32)
    target = (cluster ^ flip) * CAP + within
    return lax.broadcasted_iota(jnp.int32, (SLOTS, rows), 0) == target


def pack_kernel(flip_ref, rows_ref, cluster_ref, *out_refs):
    values = rows_ref[...].astype(jnp.float32)
    width = values.shape[1]
    scaled = values * lax.rsqrt(jnp.mean(values * values, axis=1, keepdims=True) + 1e-06)
    unit = (scaled * (1.0 / math.sqrt(width))).astype(jnp.bfloat16)
    placed = placement(cluster_ref[...], flip_ref[0, 0]).astype(jnp.float32)
    slots = jnp.dot(placed.astype(jnp.bfloat16), unit, preferred_element_type=jnp.float32)
    used = jnp.sum(placed, axis=1, keepdims=True)
    first = lax.broadcasted_iota(jnp.int32, slots.shape, 1) == 0
    slots = jnp.where(first & (used < 0.5), EMPTY, slots).astype(jnp.bfloat16)
    count = SLOTS // len(out_refs)
    for block, out_ref in enumerate(out_refs):
        out_ref[...] = slots[block * count : (block + 1) * count]


def pack(flip, embeddings, assignment, blocks):
    rows, width = embeddings.shape
    return pl.pallas_call(
        pack_kernel,
        out_shape=[jax.ShapeDtypeStruct((SLOTS // blocks, width), jnp.bfloat16)] * blocks,
        in_specs=[SMEM, VMEM, VMEM],
        out_specs=[VMEM] * blocks,
        name="pack",
    )(flip, embeddings, assignment.reshape(1, rows))


def shared_best_kernel(count, first_ref, slots_ref, others_ref, out_ref, best_ref):
    step = pl.program_id(0)
    slots, others = slots_ref[...], others_ref[...]
    similar = lax.dot_general(
        others, slots, (((1,), (1,)), ((), ())), preferred_element_type=jnp.float32
    )
    used = others[:, :1].astype(jnp.float32) < 2.0
    row = lax.broadcasted_iota(jnp.int32, similar.shape, 0)
    column = lax.broadcasted_iota(jnp.int32, similar.shape, 1)
    kept = used & (row + step * slots.shape[0] != column + first_ref[0, 0])
    kept = kept & (row % count // CAP == column % count // CAP)
    best = jnp.max(jnp.where(kept, similar, NONE), axis=0, keepdims=True)

    @pl.when(step == 0)
    def _():
        best_ref[...] = best

    @pl.when(step > 0)
    def _():
        best_ref[...] = jnp.maximum(best_ref[...], best)

    @pl.when(step == pl.num_programs(0) - 1)
    def _():
        for source in range(out_ref.shape[0]):
            piece = best_ref[:, source * count : (source + 1) * count]
            out_ref[source, :, :count] = jnp.broadcast_to(piece, (8, count))
            if count < LANES:
                out_ref[source, :, count:] = jnp.full((8, LANES - count), NONE)


def shared_best_of(slots, others, first, owners):
    size, width = slots.shape
    return pl.pallas_call(
        functools.partial(shared_best_kernel, size // owners),
        grid=(others.shape[0] // size,),
        out_shape=jax.ShapeDtypeStruct((owners, 8, LANES), jnp.float32),
        in_specs=[
            pl.BlockSpec((1, 1), lambda i: (0, 0), memory_space=pltpu.SMEM),
            pl.BlockSpec((size, width), lambda i: (0, 0)),
            pl.BlockSpec((size, width), lambda i: (i, 0)),
        ],
        out_specs=pl.BlockSpec((owners, 8, LANES), lambda i: (0, 0, 0)),
        scratch_shapes=[pltpu.VMEM((1, size), jnp.float32)],
        name="shared_best",
    )(first, slots, others)


def unpack_kernel(flip_ref, cluster_ref, *refs):
    returned_refs, out_ref = refs[:-1], refs[-1]
    count = SLOTS // len(returned_refs)
    placed = placement(cluster_ref[...], flip_ref[0, 0])
    returned = jnp.concatenate(
        [jnp.broadcast_to(ref[:1, :], (count, LANES)) for ref in returned_refs], axis=0
    )
    slot = lax.broadcasted_iota(jnp.int32, (SLOTS, LANES), 0) % count
    lane = lax.broadcasted_iota(jnp.int32, (SLOTS, LANES), 1)
    by_slot = jnp.max(jnp.where(slot == lane, returned, NONE), axis=1, keepdims=True)
    out_ref[...] = jnp.max(jnp.where(placed, by_slot, NONE), axis=0, keepdims=True)


def unpack(flip, returned, assignment):
    rows = assignment.shape[0]
    return pl.pallas_call(
        unpack_kernel,
        out_shape=jax.ShapeDtypeStruct((1, rows), jnp.float32),
        in_specs=[SMEM, VMEM] + [VMEM] * len(returned),
        out_specs=VMEM,
        name="unpack",
    )(flip, assignment.reshape(1, rows), *returned).reshape(-1)


def unit_of(values):
    values = values.astype(jnp.float32)
    scaled = values * lax.rsqrt(jnp.mean(values * values, axis=1, keepdims=True) + 1e-06)
    return (scaled * (1.0 / math.sqrt(values.shape[1]))).astype(jnp.bfloat16)


def normalize_kernel(rows_ref, cluster_ref, out_ref):
    rows, width = rows_ref.shape
    out_ref[:rows] = unit_of(rows_ref[...])
    cluster = jnp.broadcast_to(cluster_ref[...].astype(jnp.float32), (TAIL, rows))
    tail = jnp.concatenate([cluster, jnp.zeros((TAIL, width - rows), jnp.float32)], axis=1)
    out_ref[rows:] = tail.astype(jnp.bfloat16)


def normalize(embeddings, assignment):
    rows, width = embeddings.shape
    return pl.pallas_call(
        normalize_kernel,
        out_shape=jax.ShapeDtypeStruct((rows + TAIL, width), jnp.bfloat16),
        in_specs=[VMEM, VMEM],
        out_specs=VMEM,
        name="normalize",
    )(embeddings, assignment.reshape(1, rows))


def split(block):
    rows = block.shape[0] - TAIL
    return block[:rows], block[rows : rows + 1, :rows].astype(jnp.float32)


def best_against(own, others, same_rows):
    rows, clusters = zip(*[split(block) for block in own])
    rows, clusters = jnp.concatenate(rows, axis=0), jnp.concatenate(clusters, axis=1)
    best = None
    for place, other in enumerate(others):
        other_rows, other_clusters = split(other)
        count = other_rows.shape[0]
        similar = lax.dot_general(
            other_rows, rows, (((1,), (1,)), ((), ())), preferred_element_type=jnp.float32
        )
        down = jnp.broadcast_to(other_clusters, (count, count)).T[:, :1]
        kept = down == clusters
        if same_rows and place == 0:
            row = lax.broadcasted_iota(jnp.int32, similar.shape, 0)
            column = lax.broadcasted_iota(jnp.int32, similar.shape, 1)
            kept = kept & (row != column)
        found = jnp.max(jnp.where(kept, similar, NONE), axis=0, keepdims=True)
        best = found if best is None else jnp.maximum(best, found)
    return best


def early_kernel(*refs):
    *own_refs, other_ref, out_ref = refs
    own = [ref[...] for ref in own_refs]
    best = best_against(own, [own[0], other_ref[...]], True)
    out_ref[...] = jnp.broadcast_to(best, out_ref.shape)


def early(own, other):
    rows = own[0].shape[0] - TAIL
    return pl.pallas_call(
        early_kernel,
        out_shape=jax.ShapeDtypeStruct((8, len(own) * rows), jnp.float32),
        in_specs=[VMEM] * (len(own) + 1),
        out_specs=VMEM,
        name="early",
    )(*own, other)


def late_kernel(edge_ref, best_ref, *refs):
    own_refs, far_refs, out_refs = refs[:4], refs[4:8], refs[8:]
    edge = edge_ref[0, 0] > 0
    m1, m2, e2, e3 = [ref[...] for ref in far_refs]
    others = [jnp.where(edge, e2, m1), jnp.where(edge, e3, m2)]
    best = best_against([ref[...] for ref in own_refs], others, False)
    best = jnp.maximum(best, best_ref[:1, :])
    for place, out_ref in enumerate(out_refs):
        rows = out_ref.shape[1]
        out_ref[...] = jnp.broadcast_to(best[:, place * rows : (place + 1) * rows], out_ref.shape)


def late(edge, best, own, far):
    rows = own[0].shape[0] - TAIL
    return pl.pallas_call(
        late_kernel,
        out_shape=[jax.ShapeDtypeStruct((8, rows), jnp.float32)] * len(own),
        in_specs=[SMEM] + [VMEM] * (1 + len(own) + len(far)),
        out_specs=[VMEM] * len(own),
        name="late",
    )(edge, best, *own, *far)


def line(blk, plane):
    size = 4 * plane

    def within(flip, array):
        return lax.ppermute(array, AXES, [(i, i ^ flip) for i in range(size)])

    def outer(array):
        return within(plane, array)

    def inner(array):
        swapped = [0, 2, 1, 3]
        return lax.ppermute(
            array, AXES, [(i, swapped[i // plane] * plane + i % plane) for i in range(size)]
        )

    def local(embeddings, assignment):
        mine = normalize(embeddings, assignment)
        e1 = outer(mine)
        m1 = inner(mine)
        others = [within(flip, mine) for flip in range(1, plane)]
        m2 = inner(e1)
        e2 = outer(m1)
        e3 = outer(m2)
        own = [mine] + others
        best = early(own, e1)
        place = lax.axis_index(blk)
        edge = ((place == 0) | (place == 3)).astype(jnp.int32).reshape(1, 1)
        bests = late(edge, best, own, [m1, m2, e2, e3])
        found = bests[0]
        for flip in range(1, plane):
            found = jnp.maximum(found, within(flip, bests[flip]))
        return found[0]

    return local


def shared_owner(embeddings, assignment):
    route, gather = AXES[:1], AXES[1:]
    owners = lax.axis_size(route)
    flip = jnp.zeros((1, 1), jnp.int32)
    (sent,) = pack(flip, embeddings, assignment, 1)
    got = lax.all_to_all(sent, route, split_axis=0, concat_axis=0, tiled=True)
    others = lax.all_gather(got, gather, axis=0, tiled=True)
    first = (lax.axis_index(gather) * SLOTS).astype(jnp.int32).reshape(1, 1)
    best = shared_best_of(got, others, first, owners)
    returned = lax.all_to_all(best, route, split_axis=0, concat_axis=0, tiled=True)
    return unpack(flip, [returned[i] for i in range(owners)], assignment)


def solution(mesh):
    placed = (
        P(("groups", "blk", "shard", "sub"), None),
        P(("groups", "blk", "shard", "sub"), None),
    )
    plane = mesh.shape["shard"] * mesh.shape["sub"]
    program = line("blk", plane) if mesh.shape["blk"] == 4 and plane == 4 else shared_owner
    return jax.shard_map(
        program,
        mesh=mesh,
        in_specs=placed,
        out_specs=P(("groups", "blk", "shard", "sub")),
        check_vma=False,
    )
```

```python
import functools
import math

import jax
import jax.numpy as jnp
from jax import lax
from jax.experimental import pallas as pl
from jax.experimental.pallas import tpu as pltpu
from jax.sharding import PartitionSpec as P

CLUSTERS = 16
CAP = 16
SLOTS = CLUSTERS * CAP
LANES = 128
EMPTY = 4.0
NONE = -2.0
TAIL = 8
HIGH, LOW, SHARD, SUB = 8, 4, 2, 1
LIMIT = pltpu.CompilerParams(vmem_limit_bytes=12 << 20)
AXES = ("blk", "shard", "sub")

VMEM = pl.BlockSpec(memory_space=pltpu.VMEM)
SMEM = pl.BlockSpec(memory_space=pltpu.SMEM)


def placement(cluster, flip):
    rows = cluster.shape[1]
    label = lax.broadcasted_iota(jnp.int32, (CLUSTERS, rows), 0)
    member = (cluster == label).astype(jnp.float32)
    before = lax.broadcasted_iota(jnp.int32, (rows, rows), 0) < lax.broadcasted_iota(
        jnp.int32, (rows, rows), 1
    )
    earlier = jnp.dot(
        member.astype(jnp.bfloat16),
        before.astype(jnp.float32).astype(jnp.bfloat16),
        preferred_element_type=jnp.float32,
    )
    within = jnp.sum(earlier * member, axis=0, keepdims=True).astype(jnp.int32)
    target = (cluster ^ flip) * CAP + within
    return lax.broadcasted_iota(jnp.int32, (SLOTS, rows), 0) == target


def pack_kernel(flip_ref, rows_ref, cluster_ref, *out_refs):
    values = rows_ref[...].astype(jnp.float32)
    width = values.shape[1]
    scaled = values * lax.rsqrt(jnp.mean(values * values, axis=1, keepdims=True) + 1e-06)
    unit = (scaled * (1.0 / math.sqrt(width))).astype(jnp.bfloat16)
    placed = placement(cluster_ref[...], flip_ref[0, 0]).astype(jnp.float32)
    slots = jnp.dot(placed.astype(jnp.bfloat16), unit, preferred_element_type=jnp.float32)
    used = jnp.sum(placed, axis=1, keepdims=True)
    first = lax.broadcasted_iota(jnp.int32, slots.shape, 1) == 0
    slots = jnp.where(first & (used < 0.5), EMPTY, slots).astype(jnp.bfloat16)
    count = SLOTS // len(out_refs)
    for block, out_ref in enumerate(out_refs):
        out_ref[...] = slots[block * count : (block + 1) * count]


def pack(flip, embeddings, assignment, blocks):
    rows, width = embeddings.shape
    return pl.pallas_call(
        pack_kernel,
        out_shape=[jax.ShapeDtypeStruct((SLOTS // blocks, width), jnp.bfloat16)] * blocks,
        in_specs=[SMEM, VMEM, VMEM],
        out_specs=[VMEM] * blocks,
        name="pack",
    )(flip, embeddings, assignment.reshape(1, rows))


def shared_best_kernel(count, first_ref, slots_ref, others_ref, out_ref, best_ref):
    step = pl.program_id(0)
    slots, others = slots_ref[...], others_ref[...]
    similar = lax.dot_general(
        others, slots, (((1,), (1,)), ((), ())), preferred_element_type=jnp.float32
    )
    used = others[:, :1].astype(jnp.float32) < 2.0
    row = lax.broadcasted_iota(jnp.int32, similar.shape, 0)
    column = lax.broadcasted_iota(jnp.int32, similar.shape, 1)
    kept = used & (row + step * slots.shape[0] != column + first_ref[0, 0])
    kept = kept & (row % count // CAP == column % count // CAP)
    best = jnp.max(jnp.where(kept, similar, NONE), axis=0, keepdims=True)

    @pl.when(step == 0)
    def _():
        best_ref[...] = best

    @pl.when(step > 0)
    def _():
        best_ref[...] = jnp.maximum(best_ref[...], best)

    @pl.when(step == pl.num_programs(0) - 1)
    def _():
        for source in range(out_ref.shape[0]):
            piece = best_ref[:, source * count : (source + 1) * count]
            out_ref[source, :, :count] = jnp.broadcast_to(piece, (8, count))
            if count < LANES:
                out_ref[source, :, count:] = jnp.full((8, LANES - count), NONE)


def shared_best_of(slots, others, first, owners):
    size, width = slots.shape
    return pl.pallas_call(
        functools.partial(shared_best_kernel, size // owners),
        grid=(others.shape[0] // size,),
        out_shape=jax.ShapeDtypeStruct((owners, 8, LANES), jnp.float32),
        in_specs=[
            pl.BlockSpec((1, 1), lambda i: (0, 0), memory_space=pltpu.SMEM),
            pl.BlockSpec((size, width), lambda i: (0, 0)),
            pl.BlockSpec((size, width), lambda i: (i, 0)),
        ],
        out_specs=pl.BlockSpec((owners, 8, LANES), lambda i: (0, 0, 0)),
        scratch_shapes=[pltpu.VMEM((1, size), jnp.float32)],
        name="shared_best",
    )(first, slots, others)


def unpack_kernel(flip_ref, cluster_ref, *refs):
    returned_refs, out_ref = refs[:-1], refs[-1]
    count = SLOTS // len(returned_refs)
    placed = placement(cluster_ref[...], flip_ref[0, 0])
    returned = jnp.concatenate(
        [jnp.broadcast_to(ref[:1, :], (count, LANES)) for ref in returned_refs], axis=0
    )
    slot = lax.broadcasted_iota(jnp.int32, (SLOTS, LANES), 0) % count
    lane = lax.broadcasted_iota(jnp.int32, (SLOTS, LANES), 1)
    by_slot = jnp.max(jnp.where(slot == lane, returned, NONE), axis=1, keepdims=True)
    out_ref[...] = jnp.max(jnp.where(placed, by_slot, NONE), axis=0, keepdims=True)


def unpack(flip, returned, assignment):
    rows = assignment.shape[0]
    return pl.pallas_call(
        unpack_kernel,
        out_shape=jax.ShapeDtypeStruct((1, rows), jnp.float32),
        in_specs=[SMEM, VMEM] + [VMEM] * len(returned),
        out_specs=VMEM,
        name="unpack",
    )(flip, assignment.reshape(1, rows), *returned).reshape(-1)


def unit_of(values):
    values = values.astype(jnp.float32)
    scaled = values * lax.rsqrt(jnp.mean(values * values, axis=1, keepdims=True) + 1e-06)
    return (scaled * (1.0 / math.sqrt(values.shape[1]))).astype(jnp.bfloat16)


def normalize_kernel(rows_ref, cluster_ref, out_ref):
    rows, width = rows_ref.shape
    out_ref[:rows] = unit_of(rows_ref[...])
    cluster = jnp.broadcast_to(cluster_ref[...].astype(jnp.float32), (TAIL, rows))
    tail = jnp.concatenate([cluster, jnp.zeros((TAIL, width - rows), jnp.float32)], axis=1)
    out_ref[rows:] = tail.astype(jnp.bfloat16)


def normalize(embeddings, assignment):
    rows, width = embeddings.shape
    return pl.pallas_call(
        normalize_kernel,
        out_shape=jax.ShapeDtypeStruct((rows + TAIL, width), jnp.bfloat16),
        in_specs=[VMEM, VMEM],
        out_specs=VMEM,
        compiler_params=LIMIT,
        name="normalize",
    )(embeddings, assignment.reshape(1, rows))


def split(block):
    rows = block.shape[0] - TAIL
    return block[:rows], block[rows : rows + 1, :rows].astype(jnp.float32)


def best_of(own, others, same_rows=False):
    rows, clusters = zip(*[split(block) for block in own])
    rows, clusters = jnp.concatenate(rows, axis=0), jnp.concatenate(clusters, axis=1)
    best = None
    for place, other in enumerate(others):
        other_rows, other_clusters = split(other)
        count = other_rows.shape[0]
        similar = lax.dot_general(
            other_rows, rows, (((1,), (1,)), ((), ())), preferred_element_type=jnp.float32
        )
        down = jnp.broadcast_to(other_clusters, (count, count)).T[:, :1]
        kept = down == clusters
        if same_rows and place == 0:
            row = lax.broadcasted_iota(jnp.int32, similar.shape, 0)
            column = lax.broadcasted_iota(jnp.int32, similar.shape, 1)
            kept = kept & (row != column)
        found = jnp.max(jnp.where(kept, similar, NONE), axis=0, keepdims=True)
        best = found if best is None else jnp.maximum(best, found)
    return best


def early_kernel(x_ref, e_ref, mine_ref, c_ref, out_ref):
    mine = mine_ref[...]
    best = best_of([mine, x_ref[...], e_ref[...]], [mine, c_ref[...]], True)
    out_ref[...] = jnp.broadcast_to(best, out_ref.shape)


def early(x, e, mine, c):
    rows = mine.shape[0] - TAIL
    return pl.pallas_call(
        early_kernel,
        out_shape=jax.ShapeDtypeStruct((8, 3 * rows), jnp.float32),
        in_specs=[VMEM] * 4,
        out_specs=VMEM,
        compiler_params=LIMIT,
        name="early",
    )(x, e, mine, c)


def late_kernel(best_ref, x_ref, e_ref, xe_ref, mine_ref, c_ref, h_ref, ch_ref, *out_refs):
    mine, h, ch = mine_ref[...], h_ref[...], ch_ref[...]
    best = best_of([mine, x_ref[...], e_ref[...]], [h, ch])
    best = jnp.maximum(best, best_ref[:1, :])
    last = best_of([xe_ref[...]], [mine, c_ref[...], h, ch])
    best = jnp.concatenate([best, last], axis=1)
    for place, out_ref in enumerate(out_refs):
        rows = out_ref.shape[1]
        out_ref[...] = jnp.broadcast_to(best[:, place * rows : (place + 1) * rows], out_ref.shape)


def late(best, x, e, xe, mine, c, h, ch):
    rows = mine.shape[0] - TAIL
    return pl.pallas_call(
        late_kernel,
        out_shape=[jax.ShapeDtypeStruct((8, rows), jnp.float32)] * 4,
        in_specs=[VMEM] * 8,
        out_specs=[VMEM] * 4,
        compiler_params=LIMIT,
        name="late",
    )(best, x, e, xe, mine, c, h, ch)


def square(embeddings, assignment):
    def swap(flip, array):
        return lax.ppermute(array, AXES, [(i, i ^ flip) for i in range(16)])

    mine = normalize(embeddings, assignment)
    e = swap(LOW, mine)
    x = swap(SHARD, mine)
    c = swap(SUB, mine)
    then, c = lax.optimization_barrier((mine, c))
    h = swap(HIGH, then)
    xe = swap(SHARD, e)
    ch = swap(SUB, h)
    best = early(x, e, mine, c)
    found, *others = late(best, x, e, xe, mine, c, h, ch)
    for flip, other in zip((SHARD, LOW, LOW | SHARD), others):
        found = jnp.maximum(found, swap(flip, other))
    return found[0]


def shared_owner(embeddings, assignment):
    route, gather = AXES[:1], AXES[1:]
    owners = lax.axis_size(route)
    flip = jnp.zeros((1, 1), jnp.int32)
    (sent,) = pack(flip, embeddings, assignment, 1)
    got = lax.all_to_all(sent, route, split_axis=0, concat_axis=0, tiled=True)
    others = lax.all_gather(got, gather, axis=0, tiled=True)
    first = (lax.axis_index(gather) * SLOTS).astype(jnp.int32).reshape(1, 1)
    best = shared_best_of(got, others, first, owners)
    returned = lax.all_to_all(best, route, split_axis=0, concat_axis=0, tiled=True)
    return unpack(flip, [returned[i] for i in range(owners)], assignment)


def solution(mesh):
    placed = (
        P(("groups", "blk", "shard", "sub"), None),
        P(("groups", "blk", "shard", "sub"), None),
    )
    four_bits = [mesh.shape[axis] for axis in AXES] == [4, 2, 2]
    program = square if four_bits else shared_owner
    return jax.shard_map(
        program,
        mesh=mesh,
        in_specs=placed,
        out_specs=P(("groups", "blk", "shard", "sub")),
        check_vma=False,
    )
```

```python
import functools
import math

import jax
import jax.numpy as jnp
from jax import lax
from jax.experimental import pallas as pl
from jax.experimental.pallas import tpu as pltpu
from jax.sharding import PartitionSpec as P

CLUSTERS = 16
CAP = 16
SLOTS = CLUSTERS * CAP
LANES = 128
EMPTY = 4.0
NONE = -2.0
TAIL = 8
HIGH, LOW, SHARD, SUB = 8, 4, 2, 1
LIMIT = pltpu.CompilerParams(vmem_limit_bytes=12 << 20)
AXES = ("blk", "shard", "sub")

VMEM = pl.BlockSpec(memory_space=pltpu.VMEM)
SMEM = pl.BlockSpec(memory_space=pltpu.SMEM)


def placement(cluster, flip):
    rows = cluster.shape[1]
    label = lax.broadcasted_iota(jnp.int32, (CLUSTERS, rows), 0)
    member = (cluster == label).astype(jnp.float32)
    before = lax.broadcasted_iota(jnp.int32, (rows, rows), 0) < lax.broadcasted_iota(
        jnp.int32, (rows, rows), 1
    )
    earlier = jnp.dot(
        member.astype(jnp.bfloat16),
        before.astype(jnp.float32).astype(jnp.bfloat16),
        preferred_element_type=jnp.float32,
    )
    within = jnp.sum(earlier * member, axis=0, keepdims=True).astype(jnp.int32)
    target = (cluster ^ flip) * CAP + within
    return lax.broadcasted_iota(jnp.int32, (SLOTS, rows), 0) == target


def pack_kernel(flip_ref, rows_ref, cluster_ref, *out_refs):
    values = rows_ref[...].astype(jnp.float32)
    width = values.shape[1]
    scaled = values * lax.rsqrt(jnp.mean(values * values, axis=1, keepdims=True) + 1e-06)
    unit = (scaled * (1.0 / math.sqrt(width))).astype(jnp.bfloat16)
    placed = placement(cluster_ref[...], flip_ref[0, 0]).astype(jnp.float32)
    slots = jnp.dot(placed.astype(jnp.bfloat16), unit, preferred_element_type=jnp.float32)
    used = jnp.sum(placed, axis=1, keepdims=True)
    first = lax.broadcasted_iota(jnp.int32, slots.shape, 1) == 0
    slots = jnp.where(first & (used < 0.5), EMPTY, slots).astype(jnp.bfloat16)
    count = SLOTS // len(out_refs)
    for block, out_ref in enumerate(out_refs):
        out_ref[...] = slots[block * count : (block + 1) * count]


def pack(flip, embeddings, assignment, blocks):
    rows, width = embeddings.shape
    return pl.pallas_call(
        pack_kernel,
        out_shape=[jax.ShapeDtypeStruct((SLOTS // blocks, width), jnp.bfloat16)] * blocks,
        in_specs=[SMEM, VMEM, VMEM],
        out_specs=[VMEM] * blocks,
        name="pack",
    )(flip, embeddings, assignment.reshape(1, rows))


def shared_best_kernel(count, first_ref, slots_ref, others_ref, out_ref, best_ref):
    step = pl.program_id(0)
    slots, others = slots_ref[...], others_ref[...]
    similar = lax.dot_general(
        others, slots, (((1,), (1,)), ((), ())), preferred_element_type=jnp.float32
    )
    used = others[:, :1].astype(jnp.float32) < 2.0
    row = lax.broadcasted_iota(jnp.int32, similar.shape, 0)
    column = lax.broadcasted_iota(jnp.int32, similar.shape, 1)
    kept = used & (row + step * slots.shape[0] != column + first_ref[0, 0])
    kept = kept & (row % count // CAP == column % count // CAP)
    best = jnp.max(jnp.where(kept, similar, NONE), axis=0, keepdims=True)

    @pl.when(step == 0)
    def _():
        best_ref[...] = best

    @pl.when(step > 0)
    def _():
        best_ref[...] = jnp.maximum(best_ref[...], best)

    @pl.when(step == pl.num_programs(0) - 1)
    def _():
        for source in range(out_ref.shape[0]):
            piece = best_ref[:, source * count : (source + 1) * count]
            out_ref[source, :, :count] = jnp.broadcast_to(piece, (8, count))
            if count < LANES:
                out_ref[source, :, count:] = jnp.full((8, LANES - count), NONE)


def shared_best_of(slots, others, first, owners):
    size, width = slots.shape
    return pl.pallas_call(
        functools.partial(shared_best_kernel, size // owners),
        grid=(others.shape[0] // size,),
        out_shape=jax.ShapeDtypeStruct((owners, 8, LANES), jnp.float32),
        in_specs=[
            pl.BlockSpec((1, 1), lambda i: (0, 0), memory_space=pltpu.SMEM),
            pl.BlockSpec((size, width), lambda i: (0, 0)),
            pl.BlockSpec((size, width), lambda i: (i, 0)),
        ],
        out_specs=pl.BlockSpec((owners, 8, LANES), lambda i: (0, 0, 0)),
        scratch_shapes=[pltpu.VMEM((1, size), jnp.float32)],
        name="shared_best",
    )(first, slots, others)


def unpack_kernel(flip_ref, cluster_ref, *refs):
    returned_refs, out_ref = refs[:-1], refs[-1]
    count = SLOTS // len(returned_refs)
    placed = placement(cluster_ref[...], flip_ref[0, 0])
    returned = jnp.concatenate(
        [jnp.broadcast_to(ref[:1, :], (count, LANES)) for ref in returned_refs], axis=0
    )
    slot = lax.broadcasted_iota(jnp.int32, (SLOTS, LANES), 0) % count
    lane = lax.broadcasted_iota(jnp.int32, (SLOTS, LANES), 1)
    by_slot = jnp.max(jnp.where(slot == lane, returned, NONE), axis=1, keepdims=True)
    out_ref[...] = jnp.max(jnp.where(placed, by_slot, NONE), axis=0, keepdims=True)


def unpack(flip, returned, assignment):
    rows = assignment.shape[0]
    return pl.pallas_call(
        unpack_kernel,
        out_shape=jax.ShapeDtypeStruct((1, rows), jnp.float32),
        in_specs=[SMEM, VMEM] + [VMEM] * len(returned),
        out_specs=VMEM,
        name="unpack",
    )(flip, assignment.reshape(1, rows), *returned).reshape(-1)


def unit_of(values):
    values = values.astype(jnp.float32)
    scaled = values * lax.rsqrt(jnp.mean(values * values, axis=1, keepdims=True) + 1e-06)
    return (scaled * (1.0 / math.sqrt(values.shape[1]))).astype(jnp.bfloat16)


def normalize_kernel(rows_ref, cluster_ref, out_ref, front_ref, back_ref):
    rows, width = rows_ref.shape
    unit = unit_of(rows_ref[...])
    cluster = jnp.broadcast_to(cluster_ref[...].astype(jnp.float32), (TAIL, rows))
    tail = jnp.concatenate([cluster, jnp.zeros((TAIL, width - rows), jnp.float32)], axis=1)
    tail = tail.astype(jnp.bfloat16)
    out_ref[:rows] = unit
    out_ref[rows:] = tail
    front_ref[: rows // 2] = unit[: rows // 2]
    front_ref[rows // 2 :] = tail
    back_ref[...] = unit[rows // 2 :]


def normalize(embeddings, assignment):
    rows, width = embeddings.shape
    return pl.pallas_call(
        normalize_kernel,
        out_shape=[
            jax.ShapeDtypeStruct((size, width), jnp.bfloat16)
            for size in (rows + TAIL, rows // 2 + TAIL, rows // 2)
        ],
        in_specs=[VMEM, VMEM],
        out_specs=[VMEM] * 3,
        compiler_params=LIMIT,
        name="normalize",
    )(embeddings, assignment.reshape(1, rows))


def whole(ref):
    rows = ref.shape[0] - TAIL
    return ref[:rows], ref[rows:, :rows][:1].astype(jnp.float32)


def halves(front_ref, back_ref):
    half, rows = back_ref.shape[0], 2 * back_ref.shape[0]
    joined = jnp.concatenate([front_ref[:half], back_ref[...]], axis=0)
    return joined, front_ref[half:, :rows][:1].astype(jnp.float32)


def best_of(own, others, same_rows=False):
    rows, clusters = zip(*own)
    rows, clusters = jnp.concatenate(rows, axis=0), jnp.concatenate(clusters, axis=1)
    best = None
    for place, (other_rows, other_clusters) in enumerate(others):
        count = other_rows.shape[0]
        similar = lax.dot_general(
            other_rows, rows, (((1,), (1,)), ((), ())), preferred_element_type=jnp.float32
        )
        down = jnp.broadcast_to(other_clusters, (count, count)).T[:, :1]
        kept = down == clusters
        if same_rows and place == 0:
            row = lax.broadcasted_iota(jnp.int32, similar.shape, 0)
            column = lax.broadcasted_iota(jnp.int32, similar.shape, 1)
            kept = kept & (row != column)
        found = jnp.max(jnp.where(kept, similar, NONE), axis=0, keepdims=True)
        best = found if best is None else jnp.maximum(best, found)
    return best


def early_kernel(c_ref, e_ref, mine_ref, x_ref, out_ref):
    mine = whole(mine_ref)
    best = best_of([mine, whole(c_ref), whole(e_ref)], [mine, whole(x_ref)], True)
    out_ref[...] = jnp.broadcast_to(best, out_ref.shape)


def early(c, e, mine, x):
    rows = mine.shape[0] - TAIL
    return pl.pallas_call(
        early_kernel,
        out_shape=jax.ShapeDtypeStruct((8, 3 * rows), jnp.float32),
        in_specs=[VMEM] * 4,
        out_specs=VMEM,
        compiler_params=LIMIT,
        name="early",
    )(c, e, mine, x)


def late_kernel(best_ref, c_ref, e_ref, ce_ref, mine_ref, x_ref, *refs):
    h, xh, out_refs = halves(*refs[:2]), halves(*refs[2:4]), refs[4:]
    mine = whole(mine_ref)
    best = best_of([mine, whole(c_ref), whole(e_ref)], [h, xh])
    best = jnp.maximum(best, best_ref[:1, :])
    last = best_of([whole(ce_ref)], [mine, whole(x_ref), h, xh])
    best = jnp.concatenate([best, last], axis=1)
    for place, out_ref in enumerate(out_refs):
        rows = out_ref.shape[1]
        out_ref[...] = jnp.broadcast_to(best[:, place * rows : (place + 1) * rows], out_ref.shape)


def late(best, c, e, ce, mine, x, h, xh):
    rows = mine.shape[0] - TAIL
    return pl.pallas_call(
        late_kernel,
        out_shape=[jax.ShapeDtypeStruct((8, rows), jnp.float32)] * 4,
        in_specs=[VMEM] * 10,
        out_specs=[VMEM] * 4,
        compiler_params=LIMIT,
        name="late",
    )(best, c, e, ce, mine, x, *h, *xh)


def square(embeddings, assignment):
    def swap(flip, array):
        return lax.ppermute(array, AXES, [(i, i ^ flip) for i in range(16)])

    mine, front, back = normalize(embeddings, assignment)
    h_front = swap(HIGH, front)
    h_back = swap(HIGH, back)
    x = swap(SHARD, mine)
    e = swap(LOW, mine)
    c = swap(SUB, mine)
    xh_front = swap(SHARD, h_front)
    xh_back = swap(SHARD, h_back)
    ce = swap(SUB, e)
    best = early(c, e, mine, x)
    found, *others = late(best, c, e, ce, mine, x, (h_front, h_back), (xh_front, xh_back))
    for flip, other in zip((SUB, LOW, LOW | SUB), others):
        found = jnp.maximum(found, swap(flip, other))
    return found[0]


def shared_owner(embeddings, assignment):
    route, gather = AXES[:1], AXES[1:]
    owners = lax.axis_size(route)
    flip = jnp.zeros((1, 1), jnp.int32)
    (sent,) = pack(flip, embeddings, assignment, 1)
    got = lax.all_to_all(sent, route, split_axis=0, concat_axis=0, tiled=True)
    others = lax.all_gather(got, gather, axis=0, tiled=True)
    first = (lax.axis_index(gather) * SLOTS).astype(jnp.int32).reshape(1, 1)
    best = shared_best_of(got, others, first, owners)
    returned = lax.all_to_all(best, route, split_axis=0, concat_axis=0, tiled=True)
    return unpack(flip, [returned[i] for i in range(owners)], assignment)


def solution(mesh):
    placed = (
        P(("groups", "blk", "shard", "sub"), None),
        P(("groups", "blk", "shard", "sub"), None),
    )
    four_bits = [mesh.shape[axis] for axis in AXES] == [4, 2, 2]
    program = square if four_bits else shared_owner
    return jax.shard_map(
        program,
        mesh=mesh,
        in_specs=placed,
        out_specs=P(("groups", "blk", "shard", "sub")),
        check_vma=False,
    )
```

```python
import functools
import math

import jax
import jax.numpy as jnp
from jax import lax
from jax.experimental import pallas as pl
from jax.experimental.pallas import tpu as pltpu
from jax.sharding import PartitionSpec as P

CLUSTERS = 16
CAP = 16
SLOTS = CLUSTERS * CAP
LANES = 128
EMPTY = 4.0
NONE = -2.0
HIGH, LOW, SHARD, SUB = 8, 4, 2, 1
LIMIT = pltpu.CompilerParams(vmem_limit_bytes=12 << 20)
AXES = ("blk", "shard", "sub")

VMEM = pl.BlockSpec(memory_space=pltpu.VMEM)
SMEM = pl.BlockSpec(memory_space=pltpu.SMEM)


def placement(cluster, flip):
    rows = cluster.shape[1]
    label = lax.broadcasted_iota(jnp.int32, (CLUSTERS, rows), 0)
    member = (cluster == label).astype(jnp.float32)
    before = lax.broadcasted_iota(jnp.int32, (rows, rows), 0) < lax.broadcasted_iota(
        jnp.int32, (rows, rows), 1
    )
    earlier = jnp.dot(
        member.astype(jnp.bfloat16),
        before.astype(jnp.float32).astype(jnp.bfloat16),
        preferred_element_type=jnp.float32,
    )
    within = jnp.sum(earlier * member, axis=0, keepdims=True).astype(jnp.int32)
    target = (cluster ^ flip) * CAP + within
    return lax.broadcasted_iota(jnp.int32, (SLOTS, rows), 0) == target


def pack_kernel(flip_ref, rows_ref, cluster_ref, *out_refs):
    values = rows_ref[...].astype(jnp.float32)
    width = values.shape[1]
    scaled = values * lax.rsqrt(jnp.mean(values * values, axis=1, keepdims=True) + 1e-06)
    unit = (scaled * (1.0 / math.sqrt(width))).astype(jnp.bfloat16)
    placed = placement(cluster_ref[...], flip_ref[0, 0]).astype(jnp.float32)
    slots = jnp.dot(placed.astype(jnp.bfloat16), unit, preferred_element_type=jnp.float32)
    used = jnp.sum(placed, axis=1, keepdims=True)
    first = lax.broadcasted_iota(jnp.int32, slots.shape, 1) == 0
    slots = jnp.where(first & (used < 0.5), EMPTY, slots).astype(jnp.bfloat16)
    count = SLOTS // len(out_refs)
    for block, out_ref in enumerate(out_refs):
        out_ref[...] = slots[block * count : (block + 1) * count]


def pack(flip, embeddings, assignment, blocks):
    rows, width = embeddings.shape
    return pl.pallas_call(
        pack_kernel,
        out_shape=[jax.ShapeDtypeStruct((SLOTS // blocks, width), jnp.bfloat16)] * blocks,
        in_specs=[SMEM, VMEM, VMEM],
        out_specs=[VMEM] * blocks,
        name="pack",
    )(flip, embeddings, assignment.reshape(1, rows))


def shared_best_kernel(count, first_ref, slots_ref, others_ref, out_ref, best_ref):
    step = pl.program_id(0)
    slots, others = slots_ref[...], others_ref[...]
    similar = lax.dot_general(
        others, slots, (((1,), (1,)), ((), ())), preferred_element_type=jnp.float32
    )
    used = others[:, :1].astype(jnp.float32) < 2.0
    row = lax.broadcasted_iota(jnp.int32, similar.shape, 0)
    column = lax.broadcasted_iota(jnp.int32, similar.shape, 1)
    kept = used & (row + step * slots.shape[0] != column + first_ref[0, 0])
    kept = kept & (row % count // CAP == column % count // CAP)
    best = jnp.max(jnp.where(kept, similar, NONE), axis=0, keepdims=True)

    @pl.when(step == 0)
    def _():
        best_ref[...] = best

    @pl.when(step > 0)
    def _():
        best_ref[...] = jnp.maximum(best_ref[...], best)

    @pl.when(step == pl.num_programs(0) - 1)
    def _():
        for source in range(out_ref.shape[0]):
            piece = best_ref[:, source * count : (source + 1) * count]
            out_ref[source, :, :count] = jnp.broadcast_to(piece, (8, count))
            if count < LANES:
                out_ref[source, :, count:] = jnp.full((8, LANES - count), NONE)


def shared_best_of(slots, others, first, owners):
    size, width = slots.shape
    return pl.pallas_call(
        functools.partial(shared_best_kernel, size // owners),
        grid=(others.shape[0] // size,),
        out_shape=jax.ShapeDtypeStruct((owners, 8, LANES), jnp.float32),
        in_specs=[
            pl.BlockSpec((1, 1), lambda i: (0, 0), memory_space=pltpu.SMEM),
            pl.BlockSpec((size, width), lambda i: (0, 0)),
            pl.BlockSpec((size, width), lambda i: (i, 0)),
        ],
        out_specs=pl.BlockSpec((owners, 8, LANES), lambda i: (0, 0, 0)),
        scratch_shapes=[pltpu.VMEM((1, size), jnp.float32)],
        name="shared_best",
    )(first, slots, others)


def unpack_kernel(flip_ref, cluster_ref, *refs):
    returned_refs, out_ref = refs[:-1], refs[-1]
    count = SLOTS // len(returned_refs)
    placed = placement(cluster_ref[...], flip_ref[0, 0])
    returned = jnp.concatenate(
        [jnp.broadcast_to(ref[:1, :], (count, LANES)) for ref in returned_refs], axis=0
    )
    slot = lax.broadcasted_iota(jnp.int32, (SLOTS, LANES), 0) % count
    lane = lax.broadcasted_iota(jnp.int32, (SLOTS, LANES), 1)
    by_slot = jnp.max(jnp.where(slot == lane, returned, NONE), axis=1, keepdims=True)
    out_ref[...] = jnp.max(jnp.where(placed, by_slot, NONE), axis=0, keepdims=True)


def unpack(flip, returned, assignment):
    rows = assignment.shape[0]
    return pl.pallas_call(
        unpack_kernel,
        out_shape=jax.ShapeDtypeStruct((1, rows), jnp.float32),
        in_specs=[SMEM, VMEM] + [VMEM] * len(returned),
        out_specs=VMEM,
        name="unpack",
    )(flip, assignment.reshape(1, rows), *returned).reshape(-1)


def unit_of(values):
    values = values.astype(jnp.float32)
    scaled = values * lax.rsqrt(jnp.mean(values * values, axis=1, keepdims=True) + 1e-06)
    return (scaled * (1.0 / math.sqrt(values.shape[1]))).astype(jnp.bfloat16)


def best_of(own, own_clusters, others, other_clusters, same_rows=False):
    best = None
    for place, (rows, clusters) in enumerate(zip(others, other_clusters)):
        count = rows.shape[0]
        similar = lax.dot_general(
            rows, own, (((1,), (1,)), ((), ())), preferred_element_type=jnp.float32
        )
        down = jnp.broadcast_to(clusters, (count, count)).T[:, :1]
        kept = down == own_clusters
        if same_rows and place == 0:
            row = lax.broadcasted_iota(jnp.int32, similar.shape, 0)
            column = lax.broadcasted_iota(jnp.int32, similar.shape, 1)
            kept = kept & (row != column)
        found = jnp.max(jnp.where(kept, similar, NONE), axis=0, keepdims=True)
        best = found if best is None else jnp.maximum(best, found)
    return best


def early_kernel(refs, ids_ref, x_ids_ref, c_ids_ref, e_ids_ref, best_ref, own_ref, c_ref):
    mine, x, e, c = [unit_of(ref[...]) for ref in refs]
    own = jnp.concatenate([mine, x, e], axis=0)
    own_ids = jnp.concatenate([ids_ref[...], x_ids_ref[...], e_ids_ref[:1, :]], axis=1)
    best = best_of(own, own_ids, [mine, c], [ids_ref[...], c_ids_ref[...]], True)
    best_ref[...] = jnp.broadcast_to(best, best_ref.shape)
    own_ref[...] = own
    c_ref[...] = c


def early(blocks, ids):
    rows, width = blocks[0].shape
    return pl.pallas_call(
        early_kernel,
        out_shape=[
            jax.ShapeDtypeStruct((8, 3 * rows), jnp.float32),
            jax.ShapeDtypeStruct((3 * rows, width), jnp.bfloat16),
            jax.ShapeDtypeStruct((rows, width), jnp.bfloat16),
        ],
        in_specs=([VMEM] * len(blocks), *[VMEM] * len(ids)),
        out_specs=[VMEM] * 3,
        compiler_params=LIMIT,
        name="early",
    )(blocks, *ids)


def late_kernel(best_ref, own_ref, c_ref, refs, ids_ref, x_ids_ref, c_ids_ref, e_ids_ref, h_ids_ref, *out_refs):
    xe, h, ch = [unit_of(ref[...]) for ref in refs]
    own, c = own_ref[...], c_ref[...]
    mine = own[: c.shape[0]]
    own_ids = jnp.concatenate([ids_ref[...], x_ids_ref[...], e_ids_ref[:1, :]], axis=1)
    h_ids, ch_ids = h_ids_ref[:1, :], h_ids_ref[1:, :]
    best = best_of(own, own_ids, [h, ch], [h_ids, ch_ids])
    best = jnp.maximum(best, best_ref[:1, :])
    others, other_ids = [mine, c, h, ch], [ids_ref[...], c_ids_ref[...], h_ids, ch_ids]
    last = best_of(xe, e_ids_ref[1:, :], others, other_ids)
    best = jnp.concatenate([best, last], axis=1)
    for place, out_ref in enumerate(out_refs):
        rows = out_ref.shape[1]
        out_ref[...] = jnp.broadcast_to(best[:, place * rows : (place + 1) * rows], out_ref.shape)


def late(best, own, c, blocks, ids):
    rows = c.shape[0]
    return pl.pallas_call(
        late_kernel,
        out_shape=[jax.ShapeDtypeStruct((8, rows), jnp.float32)] * 4,
        in_specs=(VMEM, VMEM, VMEM, [VMEM] * len(blocks), *[VMEM] * len(ids)),
        out_specs=[VMEM] * 4,
        compiler_params=LIMIT,
        name="late",
    )(best, own, c, blocks, *ids)


def square(embeddings, assignment):
    def swap(flip, array):
        return lax.ppermute(array, AXES, [(i, i ^ flip) for i in range(16)])

    rows = embeddings.shape[0]
    mine, ids = embeddings, assignment.reshape(1, rows)
    e = swap(LOW, mine)
    h = swap(HIGH, mine)
    x = swap(SHARD, mine)
    c = swap(SUB, mine)
    x_ids, c_ids = swap(SHARD, ids), swap(SUB, ids)
    e_ids = swap(LOW, jnp.concatenate([ids, x_ids]))
    h_ids = swap(HIGH, jnp.concatenate([ids, c_ids]))
    xe = swap(SHARD, e)
    ch = swap(SUB, h)
    early_ids = [ids, x_ids, c_ids, e_ids]
    best, own, c = early([mine, x, e, c], early_ids)
    found, *others = late(best, own, c, [xe, h, ch], [*early_ids, h_ids])
    for flip, other in zip((SHARD, LOW, LOW | SHARD), others):
        found = jnp.maximum(found, swap(flip, other))
    return found[0]


def shared_owner(embeddings, assignment):
    route, gather = AXES[:1], AXES[1:]
    owners = lax.axis_size(route)
    flip = jnp.zeros((1, 1), jnp.int32)
    (sent,) = pack(flip, embeddings, assignment, 1)
    got = lax.all_to_all(sent, route, split_axis=0, concat_axis=0, tiled=True)
    others = lax.all_gather(got, gather, axis=0, tiled=True)
    first = (lax.axis_index(gather) * SLOTS).astype(jnp.int32).reshape(1, 1)
    best = shared_best_of(got, others, first, owners)
    returned = lax.all_to_all(best, route, split_axis=0, concat_axis=0, tiled=True)
    return unpack(flip, [returned[i] for i in range(owners)], assignment)


def solution(mesh):
    placed = (
        P(("groups", "blk", "shard", "sub"), None),
        P(("groups", "blk", "shard", "sub"), None),
    )
    four_bits = [mesh.shape[axis] for axis in AXES] == [4, 2, 2]
    program = square if four_bits else shared_owner
    return jax.shard_map(
        program,
        mesh=mesh,
        in_specs=placed,
        out_specs=P(("groups", "blk", "shard", "sub")),
        check_vma=False,
    )
```

```python
import functools
import math

import jax
import jax.numpy as jnp
from jax import lax
from jax.experimental import pallas as pl
from jax.experimental.pallas import tpu as pltpu
from jax.sharding import PartitionSpec as P

CLUSTERS = 16
CAP = 16
SLOTS = CLUSTERS * CAP
LANES = 128
EMPTY = 4.0
NONE = -2.0
HIGH, LOW, SHARD, SUB = 8, 4, 2, 1
LIMIT = pltpu.CompilerParams(vmem_limit_bytes=12 << 20)
AXES = ("blk", "shard", "sub")

VMEM = pl.BlockSpec(memory_space=pltpu.VMEM)
SMEM = pl.BlockSpec(memory_space=pltpu.SMEM)


def placement(cluster, flip):
    rows = cluster.shape[1]
    label = lax.broadcasted_iota(jnp.int32, (CLUSTERS, rows), 0)
    member = (cluster == label).astype(jnp.float32)
    before = lax.broadcasted_iota(jnp.int32, (rows, rows), 0) < lax.broadcasted_iota(
        jnp.int32, (rows, rows), 1
    )
    earlier = jnp.dot(
        member.astype(jnp.bfloat16),
        before.astype(jnp.float32).astype(jnp.bfloat16),
        preferred_element_type=jnp.float32,
    )
    within = jnp.sum(earlier * member, axis=0, keepdims=True).astype(jnp.int32)
    target = (cluster ^ flip) * CAP + within
    return lax.broadcasted_iota(jnp.int32, (SLOTS, rows), 0) == target


def pack_kernel(flip_ref, rows_ref, cluster_ref, *out_refs):
    values = rows_ref[...].astype(jnp.float32)
    width = values.shape[1]
    scaled = values * lax.rsqrt(jnp.mean(values * values, axis=1, keepdims=True) + 1e-06)
    unit = (scaled * (1.0 / math.sqrt(width))).astype(jnp.bfloat16)
    placed = placement(cluster_ref[...], flip_ref[0, 0]).astype(jnp.float32)
    slots = jnp.dot(placed.astype(jnp.bfloat16), unit, preferred_element_type=jnp.float32)
    used = jnp.sum(placed, axis=1, keepdims=True)
    first = lax.broadcasted_iota(jnp.int32, slots.shape, 1) == 0
    slots = jnp.where(first & (used < 0.5), EMPTY, slots).astype(jnp.bfloat16)
    count = SLOTS // len(out_refs)
    for block, out_ref in enumerate(out_refs):
        out_ref[...] = slots[block * count : (block + 1) * count]


def pack(flip, embeddings, assignment, blocks):
    rows, width = embeddings.shape
    return pl.pallas_call(
        pack_kernel,
        out_shape=[jax.ShapeDtypeStruct((SLOTS // blocks, width), jnp.bfloat16)] * blocks,
        in_specs=[SMEM, VMEM, VMEM],
        out_specs=[VMEM] * blocks,
        name="pack",
    )(flip, embeddings, assignment.reshape(1, rows))


def shared_best_kernel(count, first_ref, slots_ref, others_ref, out_ref, best_ref):
    step = pl.program_id(0)
    slots, others = slots_ref[...], others_ref[...]
    similar = lax.dot_general(
        others, slots, (((1,), (1,)), ((), ())), preferred_element_type=jnp.float32
    )
    used = others[:, :1].astype(jnp.float32) < 2.0
    row = lax.broadcasted_iota(jnp.int32, similar.shape, 0)
    column = lax.broadcasted_iota(jnp.int32, similar.shape, 1)
    kept = used & (row + step * slots.shape[0] != column + first_ref[0, 0])
    kept = kept & (row % count // CAP == column % count // CAP)
    best = jnp.max(jnp.where(kept, similar, NONE), axis=0, keepdims=True)

    @pl.when(step == 0)
    def _():
        best_ref[...] = best

    @pl.when(step > 0)
    def _():
        best_ref[...] = jnp.maximum(best_ref[...], best)

    @pl.when(step == pl.num_programs(0) - 1)
    def _():
        for source in range(out_ref.shape[0]):
            piece = best_ref[:, source * count : (source + 1) * count]
            out_ref[source, :, :count] = jnp.broadcast_to(piece, (8, count))
            if count < LANES:
                out_ref[source, :, count:] = jnp.full((8, LANES - count), NONE)


def shared_best_of(slots, others, first, owners):
    size, width = slots.shape
    return pl.pallas_call(
        functools.partial(shared_best_kernel, size // owners),
        grid=(others.shape[0] // size,),
        out_shape=jax.ShapeDtypeStruct((owners, 8, LANES), jnp.float32),
        in_specs=[
            pl.BlockSpec((1, 1), lambda i: (0, 0), memory_space=pltpu.SMEM),
            pl.BlockSpec((size, width), lambda i: (0, 0)),
            pl.BlockSpec((size, width), lambda i: (i, 0)),
        ],
        out_specs=pl.BlockSpec((owners, 8, LANES), lambda i: (0, 0, 0)),
        scratch_shapes=[pltpu.VMEM((1, size), jnp.float32)],
        name="shared_best",
    )(first, slots, others)


def unpack_kernel(flip_ref, cluster_ref, *refs):
    returned_refs, out_ref = refs[:-1], refs[-1]
    count = SLOTS // len(returned_refs)
    placed = placement(cluster_ref[...], flip_ref[0, 0])
    returned = jnp.concatenate(
        [jnp.broadcast_to(ref[:1, :], (count, LANES)) for ref in returned_refs], axis=0
    )
    slot = lax.broadcasted_iota(jnp.int32, (SLOTS, LANES), 0) % count
    lane = lax.broadcasted_iota(jnp.int32, (SLOTS, LANES), 1)
    by_slot = jnp.max(jnp.where(slot == lane, returned, NONE), axis=1, keepdims=True)
    out_ref[...] = jnp.max(jnp.where(placed, by_slot, NONE), axis=0, keepdims=True)


def unpack(flip, returned, assignment):
    rows = assignment.shape[0]
    return pl.pallas_call(
        unpack_kernel,
        out_shape=jax.ShapeDtypeStruct((1, rows), jnp.float32),
        in_specs=[SMEM, VMEM] + [VMEM] * len(returned),
        out_specs=VMEM,
        name="unpack",
    )(flip, assignment.reshape(1, rows), *returned).reshape(-1)


def unit_of(values):
    values = values.astype(jnp.float32)
    scaled = values * lax.rsqrt(jnp.mean(values * values, axis=1, keepdims=True) + 1e-06)
    return (scaled * (1.0 / math.sqrt(values.shape[1]))).astype(jnp.bfloat16)


def best_of(own, own_clusters, others, other_clusters, same_rows=False):
    best = None
    for place, (rows, clusters) in enumerate(zip(others, other_clusters)):
        count = rows.shape[0]
        similar = lax.dot_general(
            rows, own, (((1,), (1,)), ((), ())), preferred_element_type=jnp.float32
        )
        down = jnp.broadcast_to(clusters, (count, count)).T[:, :1]
        kept = down == own_clusters
        if same_rows and place == 0:
            row = lax.broadcasted_iota(jnp.int32, similar.shape, 0)
            column = lax.broadcasted_iota(jnp.int32, similar.shape, 1)
            kept = kept & (row != column)
        found = jnp.max(jnp.where(kept, similar, NONE), axis=0, keepdims=True)
        best = found if best is None else jnp.maximum(best, found)
    return best


def early_kernel(refs, ids_ref, x_ids_ref, c_ids_ref, e_ids_ref, best_ref, own_ref, c_ref):
    mine, x, e, c = [unit_of(ref[...]) for ref in refs]
    own = jnp.concatenate([mine, x, e], axis=0)
    own_ids = jnp.concatenate([ids_ref[...], x_ids_ref[...], e_ids_ref[:1, :]], axis=1)
    best = best_of(own, own_ids, [mine, c], [ids_ref[...], c_ids_ref[...]], True)
    best_ref[...] = jnp.broadcast_to(best, best_ref.shape)
    own_ref[...] = own
    c_ref[...] = c


def early(blocks, ids):
    rows, width = blocks[0].shape
    return pl.pallas_call(
        early_kernel,
        out_shape=[
            jax.ShapeDtypeStruct((8, 3 * rows), jnp.float32),
            jax.ShapeDtypeStruct((3 * rows, width), jnp.bfloat16),
            jax.ShapeDtypeStruct((rows, width), jnp.bfloat16),
        ],
        in_specs=([VMEM] * len(blocks), *[VMEM] * len(ids)),
        out_specs=[VMEM] * 3,
        compiler_params=LIMIT,
        name="early",
    )(blocks, *ids)


def late_kernel(best_ref, own_ref, c_ref, refs, ids_ref, x_ids_ref, c_ids_ref, e_ids_ref, h_ids_ref, *out_refs):
    xe, h, ch = [unit_of(ref[...]) for ref in refs]
    own, c = own_ref[...], c_ref[...]
    mine = own[: c.shape[0]]
    own_ids = jnp.concatenate([ids_ref[...], x_ids_ref[...], e_ids_ref[:1, :]], axis=1)
    h_ids, ch_ids = h_ids_ref[:1, :], h_ids_ref[1:, :]
    best = best_of(own, own_ids, [h, ch], [h_ids, ch_ids])
    best = jnp.maximum(best, best_ref[:1, :])
    others, other_ids = [mine, c, h, ch], [ids_ref[...], c_ids_ref[...], h_ids, ch_ids]
    last = best_of(xe, e_ids_ref[1:, :], others, other_ids)
    best = jnp.concatenate([best, last], axis=1)
    for place, out_ref in enumerate(out_refs):
        rows = out_ref.shape[1]
        out_ref[...] = jnp.broadcast_to(best[:, place * rows : (place + 1) * rows], out_ref.shape)


def late(best, own, c, blocks, ids):
    rows = c.shape[0]
    return pl.pallas_call(
        late_kernel,
        out_shape=[jax.ShapeDtypeStruct((8, rows), jnp.float32)] * 4,
        in_specs=(VMEM, VMEM, VMEM, [VMEM] * len(blocks), *[VMEM] * len(ids)),
        out_specs=[VMEM] * 4,
        compiler_params=LIMIT,
        name="late",
    )(best, own, c, blocks, *ids)


def square(embeddings, assignment):
    def swap(flip, array):
        return lax.ppermute(array, AXES, [(i, i ^ flip) for i in range(16)])

    rows = embeddings.shape[0]
    mine, ids = embeddings, assignment.reshape(1, rows)
    e = swap(LOW, mine)
    x = swap(SHARD, mine)
    c = swap(SUB, mine)
    h = swap(HIGH, mine)
    x_ids, c_ids = swap(SHARD, ids), swap(SUB, ids)
    e_ids = swap(LOW, jnp.concatenate([ids, x_ids]))
    h_ids = swap(HIGH, jnp.concatenate([ids, c_ids]))
    e_then, _ = lax.optimization_barrier((e, e_ids))
    h_then = h
    h_then, _ = lax.optimization_barrier((h, h_ids))
    xe = swap(SHARD, e_then)
    ch = swap(SUB, h_then)
    early_ids = [ids, x_ids, c_ids, e_ids]
    best, own, c = early([mine, x, e, c], early_ids)
    found, *others = late(best, own, c, [xe, h, ch], [*early_ids, h_ids])
    for flip, other in zip((SHARD, LOW, LOW | SHARD), others):
        found = jnp.maximum(found, swap(flip, other))
    return found[0]


def shared_owner(embeddings, assignment):
    route, gather = AXES[:1], AXES[1:]
    owners = lax.axis_size(route)
    flip = jnp.zeros((1, 1), jnp.int32)
    (sent,) = pack(flip, embeddings, assignment, 1)
    got = lax.all_to_all(sent, route, split_axis=0, concat_axis=0, tiled=True)
    others = lax.all_gather(got, gather, axis=0, tiled=True)
    first = (lax.axis_index(gather) * SLOTS).astype(jnp.int32).reshape(1, 1)
    best = shared_best_of(got, others, first, owners)
    returned = lax.all_to_all(best, route, split_axis=0, concat_axis=0, tiled=True)
    return unpack(flip, [returned[i] for i in range(owners)], assignment)


def solution(mesh):
    placed = (
        P(("groups", "blk", "shard", "sub"), None),
        P(("groups", "blk", "shard", "sub"), None),
    )
    four_bits = [mesh.shape[axis] for axis in AXES] == [4, 2, 2]
    program = square if four_bits else shared_owner
    return jax.shard_map(
        program,
        mesh=mesh,
        in_specs=placed,
        out_specs=P(("groups", "blk", "shard", "sub")),
        check_vma=False,
    )
```

```python
import functools
import math

import jax
import jax.numpy as jnp
from jax import lax
from jax.experimental import pallas as pl
from jax.experimental.pallas import tpu as pltpu
from jax.sharding import PartitionSpec as P

CLUSTERS = 16
CAP = 16
SLOTS = CLUSTERS * CAP
LANES = 128
EMPTY = 4.0
NONE = -2.0
HIGH, LOW, SHARD, SUB = 8, 4, 2, 1
LIMIT = pltpu.CompilerParams(vmem_limit_bytes=12 << 20)
AXES = ("blk", "shard", "sub")

VMEM = pl.BlockSpec(memory_space=pltpu.VMEM)
SMEM = pl.BlockSpec(memory_space=pltpu.SMEM)


def placement(cluster, flip):
    rows = cluster.shape[1]
    label = lax.broadcasted_iota(jnp.int32, (CLUSTERS, rows), 0)
    member = (cluster == label).astype(jnp.float32)
    before = lax.broadcasted_iota(jnp.int32, (rows, rows), 0) < lax.broadcasted_iota(
        jnp.int32, (rows, rows), 1
    )
    earlier = jnp.dot(
        member.astype(jnp.bfloat16),
        before.astype(jnp.float32).astype(jnp.bfloat16),
        preferred_element_type=jnp.float32,
    )
    within = jnp.sum(earlier * member, axis=0, keepdims=True).astype(jnp.int32)
    target = (cluster ^ flip) * CAP + within
    return lax.broadcasted_iota(jnp.int32, (SLOTS, rows), 0) == target


def pack_kernel(flip_ref, rows_ref, cluster_ref, *out_refs):
    values = rows_ref[...].astype(jnp.float32)
    width = values.shape[1]
    scaled = values * lax.rsqrt(jnp.mean(values * values, axis=1, keepdims=True) + 1e-06)
    unit = (scaled * (1.0 / math.sqrt(width))).astype(jnp.bfloat16)
    placed = placement(cluster_ref[...], flip_ref[0, 0]).astype(jnp.float32)
    slots = jnp.dot(placed.astype(jnp.bfloat16), unit, preferred_element_type=jnp.float32)
    used = jnp.sum(placed, axis=1, keepdims=True)
    first = lax.broadcasted_iota(jnp.int32, slots.shape, 1) == 0
    slots = jnp.where(first & (used < 0.5), EMPTY, slots).astype(jnp.bfloat16)
    count = SLOTS // len(out_refs)
    for block, out_ref in enumerate(out_refs):
        out_ref[...] = slots[block * count : (block + 1) * count]


def pack(flip, embeddings, assignment, blocks):
    rows, width = embeddings.shape
    return pl.pallas_call(
        pack_kernel,
        out_shape=[jax.ShapeDtypeStruct((SLOTS // blocks, width), jnp.bfloat16)] * blocks,
        in_specs=[SMEM, VMEM, VMEM],
        out_specs=[VMEM] * blocks,
        name="pack",
    )(flip, embeddings, assignment.reshape(1, rows))


def shared_best_kernel(count, first_ref, slots_ref, others_ref, out_ref, best_ref):
    step = pl.program_id(0)
    slots, others = slots_ref[...], others_ref[...]
    similar = lax.dot_general(
        others, slots, (((1,), (1,)), ((), ())), preferred_element_type=jnp.float32
    )
    used = others[:, :1].astype(jnp.float32) < 2.0
    row = lax.broadcasted_iota(jnp.int32, similar.shape, 0)
    column = lax.broadcasted_iota(jnp.int32, similar.shape, 1)
    kept = used & (row + step * slots.shape[0] != column + first_ref[0, 0])
    kept = kept & (row % count // CAP == column % count // CAP)
    best = jnp.max(jnp.where(kept, similar, NONE), axis=0, keepdims=True)

    @pl.when(step == 0)
    def _():
        best_ref[...] = best

    @pl.when(step > 0)
    def _():
        best_ref[...] = jnp.maximum(best_ref[...], best)

    @pl.when(step == pl.num_programs(0) - 1)
    def _():
        for source in range(out_ref.shape[0]):
            piece = best_ref[:, source * count : (source + 1) * count]
            out_ref[source, :, :count] = jnp.broadcast_to(piece, (8, count))
            if count < LANES:
                out_ref[source, :, count:] = jnp.full((8, LANES - count), NONE)


def shared_best_of(slots, others, first, owners):
    size, width = slots.shape
    return pl.pallas_call(
        functools.partial(shared_best_kernel, size // owners),
        grid=(others.shape[0] // size,),
        out_shape=jax.ShapeDtypeStruct((owners, 8, LANES), jnp.float32),
        in_specs=[
            pl.BlockSpec((1, 1), lambda i: (0, 0), memory_space=pltpu.SMEM),
            pl.BlockSpec((size, width), lambda i: (0, 0)),
            pl.BlockSpec((size, width), lambda i: (i, 0)),
        ],
        out_specs=pl.BlockSpec((owners, 8, LANES), lambda i: (0, 0, 0)),
        scratch_shapes=[pltpu.VMEM((1, size), jnp.float32)],
        name="shared_best",
    )(first, slots, others)


def unpack_kernel(flip_ref, cluster_ref, *refs):
    returned_refs, out_ref = refs[:-1], refs[-1]
    count = SLOTS // len(returned_refs)
    placed = placement(cluster_ref[...], flip_ref[0, 0])
    returned = jnp.concatenate(
        [jnp.broadcast_to(ref[:1, :], (count, LANES)) for ref in returned_refs], axis=0
    )
    slot = lax.broadcasted_iota(jnp.int32, (SLOTS, LANES), 0) % count
    lane = lax.broadcasted_iota(jnp.int32, (SLOTS, LANES), 1)
    by_slot = jnp.max(jnp.where(slot == lane, returned, NONE), axis=1, keepdims=True)
    out_ref[...] = jnp.max(jnp.where(placed, by_slot, NONE), axis=0, keepdims=True)


def unpack(flip, returned, assignment):
    rows = assignment.shape[0]
    return pl.pallas_call(
        unpack_kernel,
        out_shape=jax.ShapeDtypeStruct((1, rows), jnp.float32),
        in_specs=[SMEM, VMEM] + [VMEM] * len(returned),
        out_specs=VMEM,
        name="unpack",
    )(flip, assignment.reshape(1, rows), *returned).reshape(-1)


def unit_of(values):
    values = values.astype(jnp.float32)
    scaled = values * lax.rsqrt(jnp.mean(values * values, axis=1, keepdims=True) + 1e-06)
    return (scaled * (1.0 / math.sqrt(values.shape[1]))).astype(jnp.bfloat16)


def best_of(own, own_clusters, others, other_clusters, same_rows=False):
    best = None
    for place, (rows, clusters) in enumerate(zip(others, other_clusters)):
        count = rows.shape[0]
        similar = lax.dot_general(
            rows, own, (((1,), (1,)), ((), ())), preferred_element_type=jnp.float32
        )
        down = jnp.broadcast_to(clusters, (count, count)).T[:, :1]
        kept = down == own_clusters
        if same_rows and place == 0:
            row = lax.broadcasted_iota(jnp.int32, similar.shape, 0)
            column = lax.broadcasted_iota(jnp.int32, similar.shape, 1)
            kept = kept & (row != column)
        found = jnp.max(jnp.where(kept, similar, NONE), axis=0, keepdims=True)
        best = found if best is None else jnp.maximum(best, found)
    return best


def early_kernel(refs, ids_ref, x_ids_ref, c_ids_ref, e_ids_ref, best_ref, own_ref, c_ref):
    mine, x, e, c = [unit_of(ref[...]) for ref in refs]
    own = jnp.concatenate([mine, x, e], axis=0)
    own_ids = jnp.concatenate([ids_ref[...], x_ids_ref[...], e_ids_ref[:1, :]], axis=1)
    best = best_of(own, own_ids, [mine, c], [ids_ref[...], c_ids_ref[...]], True)
    best_ref[...] = jnp.broadcast_to(best, best_ref.shape)
    own_ref[...] = own
    c_ref[...] = c


def early(blocks, ids):
    rows, width = blocks[0].shape
    return pl.pallas_call(
        early_kernel,
        out_shape=[
            jax.ShapeDtypeStruct((8, 3 * rows), jnp.float32),
            jax.ShapeDtypeStruct((3 * rows, width), jnp.bfloat16),
            jax.ShapeDtypeStruct((rows, width), jnp.bfloat16),
        ],
        in_specs=([VMEM] * len(blocks), *[VMEM] * len(ids)),
        out_specs=[VMEM] * 3,
        compiler_params=LIMIT,
        name="early",
    )(blocks, *ids)


def middle_kernel(
    best_ref, own_ref, c_ref, h_ref, ch_ref, ids_ref, x_ids_ref, c_ids_ref, e_ids_ref, h_ids_ref,
    mine_out_ref, x_out_ref, e_out_ref, far_ref,
):
    h, ch = unit_of(h_ref[...]), unit_of(ch_ref[...])
    own_ids = jnp.concatenate([ids_ref[...], x_ids_ref[...], e_ids_ref[:1, :]], axis=1)
    best = best_of(own_ref[...], own_ids, [h, ch], [h_ids_ref[:1, :], h_ids_ref[1:, :]])
    best = jnp.maximum(best, best_ref[:1, :])
    rows = c_ref.shape[0]
    for place, out_ref in enumerate((mine_out_ref, x_out_ref, e_out_ref)):
        out_ref[...] = jnp.broadcast_to(best[:, place * rows : (place + 1) * rows], out_ref.shape)
    far_ref[...] = jnp.concatenate([own_ref[:rows], c_ref[...], h, ch], axis=0)


def middle(best, own, c, h, ch, ids):
    rows, width = c.shape
    return pl.pallas_call(
        middle_kernel,
        out_shape=[jax.ShapeDtypeStruct((8, rows), jnp.float32)] * 3
        + [jax.ShapeDtypeStruct((4 * rows, width), jnp.bfloat16)],
        in_specs=[VMEM] * 10,
        out_specs=[VMEM] * 4,
        compiler_params=LIMIT,
        name="middle",
    )(best, own, c, h, ch, *ids)


def late_kernel(far_ref, xe_ref, ids_ref, c_ids_ref, e_ids_ref, h_ids_ref, out_ref):
    xe = unit_of(xe_ref[...])
    rows = xe.shape[0]
    others = [far_ref[place * rows : (place + 1) * rows] for place in range(4)]
    other_ids = [ids_ref[...], c_ids_ref[...], h_ids_ref[:1, :], h_ids_ref[1:, :]]
    out_ref[...] = jnp.broadcast_to(best_of(xe, e_ids_ref[1:, :], others, other_ids), out_ref.shape)


def late(far, xe, ids):
    rows = xe.shape[0]
    return pl.pallas_call(
        late_kernel,
        out_shape=jax.ShapeDtypeStruct((8, rows), jnp.float32),
        in_specs=[VMEM] * 6,
        out_specs=VMEM,
        compiler_params=LIMIT,
        name="late",
    )(far, xe, *ids)


def square(embeddings, assignment):
    def swap(flip, array):
        return lax.ppermute(array, AXES, [(i, i ^ flip) for i in range(16)])

    rows = embeddings.shape[0]
    mine, ids = embeddings, assignment.reshape(1, rows)
    x_ids, c_ids = swap(SHARD, ids), swap(SUB, ids)
    e = swap(LOW, mine)
    x = swap(SHARD, mine)
    far = mine
    h = swap(HIGH, far)
    e_ids = swap(LOW, jnp.concatenate([ids, x_ids]))
    h_ids = swap(HIGH, jnp.concatenate([ids, c_ids]))
    mine_c, _ = lax.optimization_barrier((mine, e))
    c = swap(SUB, mine_c)
    e_then, _ = lax.optimization_barrier((e, e_ids))
    h_then, _, _ = lax.optimization_barrier((h, h_ids, e_ids))
    xe = swap(SHARD, e_then)
    ch = swap(SUB, h_then)
    best, own, c = early([mine, x, e, c], [ids, x_ids, c_ids, e_ids])
    found, x_best, e_best, far = middle(best, own, c, h, ch, [ids, x_ids, c_ids, e_ids, h_ids])
    x_best, e_best = swap(SHARD, x_best), swap(LOW, e_best)
    xe_best = swap(LOW | SHARD, late(far, xe, [ids, c_ids, e_ids, h_ids]))
    return jnp.maximum(jnp.maximum(found, x_best), jnp.maximum(e_best, xe_best))[0]


def shared_owner(embeddings, assignment):
    route, gather = AXES[:1], AXES[1:]
    owners = lax.axis_size(route)
    flip = jnp.zeros((1, 1), jnp.int32)
    (sent,) = pack(flip, embeddings, assignment, 1)
    got = lax.all_to_all(sent, route, split_axis=0, concat_axis=0, tiled=True)
    others = lax.all_gather(got, gather, axis=0, tiled=True)
    first = (lax.axis_index(gather) * SLOTS).astype(jnp.int32).reshape(1, 1)
    best = shared_best_of(got, others, first, owners)
    returned = lax.all_to_all(best, route, split_axis=0, concat_axis=0, tiled=True)
    return unpack(flip, [returned[i] for i in range(owners)], assignment)


def solution(mesh):
    placed = (
        P(("groups", "blk", "shard", "sub"), None),
        P(("groups", "blk", "shard", "sub"), None),
    )
    four_bits = [mesh.shape[axis] for axis in AXES] == [4, 2, 2]
    program = square if four_bits else shared_owner
    return jax.shard_map(
        program,
        mesh=mesh,
        in_specs=placed,
        out_specs=P(("groups", "blk", "shard", "sub")),
        check_vma=False,
    )
```

```python
import functools
import math

import jax
import jax.numpy as jnp
from jax import lax
from jax.experimental import pallas as pl
from jax.experimental.pallas import tpu as pltpu
from jax.sharding import PartitionSpec as P

CLUSTERS = 16
CAP = 16
SLOTS = CLUSTERS * CAP
LANES = 128
EMPTY = 4.0
NONE = -2.0
HIGH, LOW, SHARD, SUB = 8, 4, 2, 1
LIMIT = pltpu.CompilerParams(vmem_limit_bytes=12 << 20)
AXES = ("blk", "shard", "sub")

VMEM = pl.BlockSpec(memory_space=pltpu.VMEM)
SMEM = pl.BlockSpec(memory_space=pltpu.SMEM)


def placement(cluster, flip):
    rows = cluster.shape[1]
    label = lax.broadcasted_iota(jnp.int32, (CLUSTERS, rows), 0)
    member = (cluster == label).astype(jnp.float32)
    before = lax.broadcasted_iota(jnp.int32, (rows, rows), 0) < lax.broadcasted_iota(
        jnp.int32, (rows, rows), 1
    )
    earlier = jnp.dot(
        member.astype(jnp.bfloat16),
        before.astype(jnp.float32).astype(jnp.bfloat16),
        preferred_element_type=jnp.float32,
    )
    within = jnp.sum(earlier * member, axis=0, keepdims=True).astype(jnp.int32)
    target = (cluster ^ flip) * CAP + within
    return lax.broadcasted_iota(jnp.int32, (SLOTS, rows), 0) == target


def pack_kernel(flip_ref, rows_ref, cluster_ref, *out_refs):
    values = rows_ref[...].astype(jnp.float32)
    width = values.shape[1]
    scaled = values * lax.rsqrt(jnp.mean(values * values, axis=1, keepdims=True) + 1e-06)
    unit = (scaled * (1.0 / math.sqrt(width))).astype(jnp.bfloat16)
    placed = placement(cluster_ref[...], flip_ref[0, 0]).astype(jnp.float32)
    slots = jnp.dot(placed.astype(jnp.bfloat16), unit, preferred_element_type=jnp.float32)
    used = jnp.sum(placed, axis=1, keepdims=True)
    first = lax.broadcasted_iota(jnp.int32, slots.shape, 1) == 0
    slots = jnp.where(first & (used < 0.5), EMPTY, slots).astype(jnp.bfloat16)
    count = SLOTS // len(out_refs)
    for block, out_ref in enumerate(out_refs):
        out_ref[...] = slots[block * count : (block + 1) * count]


def pack(flip, embeddings, assignment, blocks):
    rows, width = embeddings.shape
    return pl.pallas_call(
        pack_kernel,
        out_shape=[jax.ShapeDtypeStruct((SLOTS // blocks, width), jnp.bfloat16)] * blocks,
        in_specs=[SMEM, VMEM, VMEM],
        out_specs=[VMEM] * blocks,
        name="pack",
    )(flip, embeddings, assignment.reshape(1, rows))


def shared_best_kernel(count, first_ref, slots_ref, others_ref, out_ref, best_ref):
    step = pl.program_id(0)
    slots, others = slots_ref[...], others_ref[...]
    similar = lax.dot_general(
        others, slots, (((1,), (1,)), ((), ())), preferred_element_type=jnp.float32
    )
    used = others[:, :1].astype(jnp.float32) < 2.0
    row = lax.broadcasted_iota(jnp.int32, similar.shape, 0)
    column = lax.broadcasted_iota(jnp.int32, similar.shape, 1)
    kept = used & (row + step * slots.shape[0] != column + first_ref[0, 0])
    kept = kept & (row % count // CAP == column % count // CAP)
    best = jnp.max(jnp.where(kept, similar, NONE), axis=0, keepdims=True)

    @pl.when(step == 0)
    def _():
        best_ref[...] = best

    @pl.when(step > 0)
    def _():
        best_ref[...] = jnp.maximum(best_ref[...], best)

    @pl.when(step == pl.num_programs(0) - 1)
    def _():
        for source in range(out_ref.shape[0]):
            piece = best_ref[:, source * count : (source + 1) * count]
            out_ref[source, :, :count] = jnp.broadcast_to(piece, (8, count))
            if count < LANES:
                out_ref[source, :, count:] = jnp.full((8, LANES - count), NONE)


def shared_best_of(slots, others, first, owners):
    size, width = slots.shape
    return pl.pallas_call(
        functools.partial(shared_best_kernel, size // owners),
        grid=(others.shape[0] // size,),
        out_shape=jax.ShapeDtypeStruct((owners, 8, LANES), jnp.float32),
        in_specs=[
            pl.BlockSpec((1, 1), lambda i: (0, 0), memory_space=pltpu.SMEM),
            pl.BlockSpec((size, width), lambda i: (0, 0)),
            pl.BlockSpec((size, width), lambda i: (i, 0)),
        ],
        out_specs=pl.BlockSpec((owners, 8, LANES), lambda i: (0, 0, 0)),
        scratch_shapes=[pltpu.VMEM((1, size), jnp.float32)],
        name="shared_best",
    )(first, slots, others)


def unpack_kernel(flip_ref, cluster_ref, *refs):
    returned_refs, out_ref = refs[:-1], refs[-1]
    count = SLOTS // len(returned_refs)
    placed = placement(cluster_ref[...], flip_ref[0, 0])
    returned = jnp.concatenate(
        [jnp.broadcast_to(ref[:1, :], (count, LANES)) for ref in returned_refs], axis=0
    )
    slot = lax.broadcasted_iota(jnp.int32, (SLOTS, LANES), 0) % count
    lane = lax.broadcasted_iota(jnp.int32, (SLOTS, LANES), 1)
    by_slot = jnp.max(jnp.where(slot == lane, returned, NONE), axis=1, keepdims=True)
    out_ref[...] = jnp.max(jnp.where(placed, by_slot, NONE), axis=0, keepdims=True)


def unpack(flip, returned, assignment):
    rows = assignment.shape[0]
    return pl.pallas_call(
        unpack_kernel,
        out_shape=jax.ShapeDtypeStruct((1, rows), jnp.float32),
        in_specs=[SMEM, VMEM] + [VMEM] * len(returned),
        out_specs=VMEM,
        name="unpack",
    )(flip, assignment.reshape(1, rows), *returned).reshape(-1)


def unit_of(values):
    values = values.astype(jnp.float32)
    scaled = values * lax.rsqrt(jnp.mean(values * values, axis=1, keepdims=True) + 1e-06)
    return (scaled * (1.0 / math.sqrt(values.shape[1]))).astype(jnp.bfloat16)


def best_of(own, own_clusters, others, other_clusters, same_rows=False):
    best = None
    for place, (rows, clusters) in enumerate(zip(others, other_clusters)):
        count = rows.shape[0]
        similar = lax.dot_general(
            rows, own, (((1,), (1,)), ((), ())), preferred_element_type=jnp.float32
        )
        down = jnp.broadcast_to(clusters, (count, count)).T[:, :1]
        kept = down == own_clusters
        if same_rows and place == 0:
            row = lax.broadcasted_iota(jnp.int32, similar.shape, 0)
            column = lax.broadcasted_iota(jnp.int32, similar.shape, 1)
            kept = kept & (row != column)
        found = jnp.max(jnp.where(kept, similar, NONE), axis=0, keepdims=True)
        best = found if best is None else jnp.maximum(best, found)
    return best


def early_kernel(refs, ids_ref, x_ids_ref, c_ids_ref, e_ids_ref, best_ref, own_ref, c_ref):
    mine, x, e, c = [unit_of(ref[...]) for ref in refs]
    own = jnp.concatenate([mine, x, e], axis=0)
    own_ids = jnp.concatenate([ids_ref[...], x_ids_ref[...], e_ids_ref[:1, :]], axis=1)
    best = best_of(own, own_ids, [mine, c], [ids_ref[...], c_ids_ref[...]], True)
    best_ref[...] = jnp.broadcast_to(best, best_ref.shape)
    own_ref[...] = own
    c_ref[...] = c


def early(blocks, ids):
    rows, width = blocks[0].shape
    return pl.pallas_call(
        early_kernel,
        out_shape=[
            jax.ShapeDtypeStruct((8, 3 * rows), jnp.float32),
            jax.ShapeDtypeStruct((3 * rows, width), jnp.bfloat16),
            jax.ShapeDtypeStruct((rows, width), jnp.bfloat16),
        ],
        in_specs=([VMEM] * len(blocks), *[VMEM] * len(ids)),
        out_specs=[VMEM] * 3,
        compiler_params=LIMIT,
        name="early",
    )(blocks, *ids)


def middle_kernel(
    best_ref, own_ref, c_ref, h_ref, ch_front_ref, ch_back_ref, ids_ref, x_ids_ref, c_ids_ref, e_ids_ref, h_ids_ref,
    mine_out_ref, x_out_ref, e_out_ref, far_ref,
):
    h = unit_of(h_ref[...])
    ch = jnp.concatenate([unit_of(ch_front_ref[...]), unit_of(ch_back_ref[...])], axis=0)
    own_ids = jnp.concatenate([ids_ref[...], x_ids_ref[...], e_ids_ref[:1, :]], axis=1)
    best = best_of(own_ref[...], own_ids, [h, ch], [h_ids_ref[:1, :], h_ids_ref[1:, :]])
    best = jnp.maximum(best, best_ref[:1, :])
    rows = c_ref.shape[0]
    for place, out_ref in enumerate((mine_out_ref, x_out_ref, e_out_ref)):
        out_ref[...] = jnp.broadcast_to(best[:, place * rows : (place + 1) * rows], out_ref.shape)
    far_ref[...] = jnp.concatenate([own_ref[:rows], c_ref[...], h, ch], axis=0)


def middle(best, own, c, h, ch, ids):
    rows, width = c.shape
    return pl.pallas_call(
        middle_kernel,
        out_shape=[jax.ShapeDtypeStruct((8, rows), jnp.float32)] * 3
        + [jax.ShapeDtypeStruct((4 * rows, width), jnp.bfloat16)],
        in_specs=[VMEM] * 11,
        out_specs=[VMEM] * 4,
        compiler_params=LIMIT,
        name="middle",
    )(best, own, c, h, *ch, *ids)


def late_kernel(far_ref, xe_ref, ids_ref, c_ids_ref, e_ids_ref, h_ids_ref, out_ref):
    xe = unit_of(xe_ref[...])
    rows = xe.shape[0]
    others = [far_ref[place * rows : (place + 1) * rows] for place in range(4)]
    other_ids = [ids_ref[...], c_ids_ref[...], h_ids_ref[:1, :], h_ids_ref[1:, :]]
    out_ref[...] = jnp.broadcast_to(best_of(xe, e_ids_ref[1:, :], others, other_ids), out_ref.shape)


def late(far, xe, ids):
    rows = xe.shape[0]
    return pl.pallas_call(
        late_kernel,
        out_shape=jax.ShapeDtypeStruct((8, rows), jnp.float32),
        in_specs=[VMEM] * 6,
        out_specs=VMEM,
        compiler_params=LIMIT,
        name="late",
    )(far, xe, *ids)


def square(embeddings, assignment):
    def swap(flip, array):
        return lax.ppermute(array, AXES, [(i, i ^ flip) for i in range(16)])

    rows = embeddings.shape[0]
    mine, ids = embeddings, assignment.reshape(1, rows)
    x_ids, c_ids = swap(SHARD, ids), swap(SUB, ids)
    x_ids, c_ids = swap(SHARD, ids), swap(SUB, ids)
    e = swap(LOW, mine)
    x = swap(SHARD, mine)
    far, _ = lax.optimization_barrier((mine, c_ids))
    h = swap(HIGH, far)
    e_ids = swap(LOW, jnp.concatenate([ids, x_ids]))
    h_ids = swap(HIGH, jnp.concatenate([ids, c_ids]))
    mine_c, _ = lax.optimization_barrier((mine, e_ids))
    c = swap(SUB, mine_c)
    e_then, _ = lax.optimization_barrier((e, e_ids))
    h_then, _ = lax.optimization_barrier((h, h_ids))
    xe = swap(SHARD, e_then)
    ch = [swap(SUB, h_then[: rows // 2]), swap(SUB, h_then[rows // 2 :])]
    best, own, c = early([mine, x, e, c], [ids, x_ids, c_ids, e_ids])
    found, x_best, e_best, far = middle(best, own, c, h, ch, [ids, x_ids, c_ids, e_ids, h_ids])
    x_best, e_best = swap(SHARD, x_best), swap(LOW, e_best)
    xe_best = swap(LOW | SHARD, late(far, xe, [ids, c_ids, e_ids, h_ids]))
    return jnp.maximum(jnp.maximum(found, x_best), jnp.maximum(e_best, xe_best))[0]


def shared_owner(embeddings, assignment):
    route, gather = AXES[:1], AXES[1:]
    owners = lax.axis_size(route)
    flip = jnp.zeros((1, 1), jnp.int32)
    (sent,) = pack(flip, embeddings, assignment, 1)
    got = lax.all_to_all(sent, route, split_axis=0, concat_axis=0, tiled=True)
    others = lax.all_gather(got, gather, axis=0, tiled=True)
    first = (lax.axis_index(gather) * SLOTS).astype(jnp.int32).reshape(1, 1)
    best = shared_best_of(got, others, first, owners)
    returned = lax.all_to_all(best, route, split_axis=0, concat_axis=0, tiled=True)
    return unpack(flip, [returned[i] for i in range(owners)], assignment)


def solution(mesh):
    placed = (
        P(("groups", "blk", "shard", "sub"), None),
        P(("groups", "blk", "shard", "sub"), None),
    )
    four_bits = [mesh.shape[axis] for axis in AXES] == [4, 2, 2]
    program = square if four_bits else shared_owner
    return jax.shard_map(
        program,
        mesh=mesh,
        in_specs=placed,
        out_specs=P(("groups", "blk", "shard", "sub")),
        check_vma=False,
    )
```

```python
import functools
import math

import jax
import jax.numpy as jnp
from jax import lax
from jax.experimental import pallas as pl
from jax.experimental.pallas import tpu as pltpu
from jax.sharding import PartitionSpec as P

CLUSTERS = 16
CAP = 16
SLOTS = CLUSTERS * CAP
LANES = 128
EMPTY = 4.0
NONE = -2.0
HIGH, LOW, SHARD, SUB = 8, 4, 2, 1
LIMIT = pltpu.CompilerParams(vmem_limit_bytes=12 << 20)
AXES = ("blk", "shard", "sub")

VMEM = pl.BlockSpec(memory_space=pltpu.VMEM)
SMEM = pl.BlockSpec(memory_space=pltpu.SMEM)


def placement(cluster, flip):
    rows = cluster.shape[1]
    label = lax.broadcasted_iota(jnp.int32, (CLUSTERS, rows), 0)
    member = (cluster == label).astype(jnp.float32)
    before = lax.broadcasted_iota(jnp.int32, (rows, rows), 0) < lax.broadcasted_iota(
        jnp.int32, (rows, rows), 1
    )
    earlier = jnp.dot(
        member.astype(jnp.bfloat16),
        before.astype(jnp.float32).astype(jnp.bfloat16),
        preferred_element_type=jnp.float32,
    )
    within = jnp.sum(earlier * member, axis=0, keepdims=True).astype(jnp.int32)
    target = (cluster ^ flip) * CAP + within
    return lax.broadcasted_iota(jnp.int32, (SLOTS, rows), 0) == target


def pack_kernel(flip_ref, rows_ref, cluster_ref, *out_refs):
    values = rows_ref[...].astype(jnp.float32)
    width = values.shape[1]
    scaled = values * lax.rsqrt(jnp.mean(values * values, axis=1, keepdims=True) + 1e-06)
    unit = (scaled * (1.0 / math.sqrt(width))).astype(jnp.bfloat16)
    placed = placement(cluster_ref[...], flip_ref[0, 0]).astype(jnp.float32)
    slots = jnp.dot(placed.astype(jnp.bfloat16), unit, preferred_element_type=jnp.float32)
    used = jnp.sum(placed, axis=1, keepdims=True)
    first = lax.broadcasted_iota(jnp.int32, slots.shape, 1) == 0
    slots = jnp.where(first & (used < 0.5), EMPTY, slots).astype(jnp.bfloat16)
    count = SLOTS // len(out_refs)
    for block, out_ref in enumerate(out_refs):
        out_ref[...] = slots[block * count : (block + 1) * count]


def pack(flip, embeddings, assignment, blocks):
    rows, width = embeddings.shape
    return pl.pallas_call(
        pack_kernel,
        out_shape=[jax.ShapeDtypeStruct((SLOTS // blocks, width), jnp.bfloat16)] * blocks,
        in_specs=[SMEM, VMEM, VMEM],
        out_specs=[VMEM] * blocks,
        name="pack",
    )(flip, embeddings, assignment.reshape(1, rows))


def shared_best_kernel(count, first_ref, slots_ref, others_ref, out_ref, best_ref):
    step = pl.program_id(0)
    slots, others = slots_ref[...], others_ref[...]
    similar = lax.dot_general(
        others, slots, (((1,), (1,)), ((), ())), preferred_element_type=jnp.float32
    )
    used = others[:, :1].astype(jnp.float32) < 2.0
    row = lax.broadcasted_iota(jnp.int32, similar.shape, 0)
    column = lax.broadcasted_iota(jnp.int32, similar.shape, 1)
    kept = used & (row + step * slots.shape[0] != column + first_ref[0, 0])
    kept = kept & (row % count // CAP == column % count // CAP)
    best = jnp.max(jnp.where(kept, similar, NONE), axis=0, keepdims=True)

    @pl.when(step == 0)
    def _():
        best_ref[...] = best

    @pl.when(step > 0)
    def _():
        best_ref[...] = jnp.maximum(best_ref[...], best)

    @pl.when(step == pl.num_programs(0) - 1)
    def _():
        for source in range(out_ref.shape[0]):
            piece = best_ref[:, source * count : (source + 1) * count]
            out_ref[source, :, :count] = jnp.broadcast_to(piece, (8, count))
            if count < LANES:
                out_ref[source, :, count:] = jnp.full((8, LANES - count), NONE)


def shared_best_of(slots, others, first, owners):
    size, width = slots.shape
    return pl.pallas_call(
        functools.partial(shared_best_kernel, size // owners),
        grid=(others.shape[0] // size,),
        out_shape=jax.ShapeDtypeStruct((owners, 8, LANES), jnp.float32),
        in_specs=[
            pl.BlockSpec((1, 1), lambda i: (0, 0), memory_space=pltpu.SMEM),
            pl.BlockSpec((size, width), lambda i: (0, 0)),
            pl.BlockSpec((size, width), lambda i: (i, 0)),
        ],
        out_specs=pl.BlockSpec((owners, 8, LANES), lambda i: (0, 0, 0)),
        scratch_shapes=[pltpu.VMEM((1, size), jnp.float32)],
        name="shared_best",
    )(first, slots, others)


def unpack_kernel(flip_ref, cluster_ref, *refs):
    returned_refs, out_ref = refs[:-1], refs[-1]
    count = SLOTS // len(returned_refs)
    placed = placement(cluster_ref[...], flip_ref[0, 0])
    returned = jnp.concatenate(
        [jnp.broadcast_to(ref[:1, :], (count, LANES)) for ref in returned_refs], axis=0
    )
    slot = lax.broadcasted_iota(jnp.int32, (SLOTS, LANES), 0) % count
    lane = lax.broadcasted_iota(jnp.int32, (SLOTS, LANES), 1)
    by_slot = jnp.max(jnp.where(slot == lane, returned, NONE), axis=1, keepdims=True)
    out_ref[...] = jnp.max(jnp.where(placed, by_slot, NONE), axis=0, keepdims=True)


def unpack(flip, returned, assignment):
    rows = assignment.shape[0]
    return pl.pallas_call(
        unpack_kernel,
        out_shape=jax.ShapeDtypeStruct((1, rows), jnp.float32),
        in_specs=[SMEM, VMEM] + [VMEM] * len(returned),
        out_specs=VMEM,
        name="unpack",
    )(flip, assignment.reshape(1, rows), *returned).reshape(-1)


def unit_of(values):
    values = values.astype(jnp.float32)
    scaled = values * lax.rsqrt(jnp.mean(values * values, axis=1, keepdims=True) + 1e-06)
    return (scaled * (1.0 / math.sqrt(values.shape[1]))).astype(jnp.bfloat16)


def best_of(own, own_clusters, others, other_clusters, same_rows=False):
    best = None
    for place, (rows, clusters) in enumerate(zip(others, other_clusters)):
        count = rows.shape[0]
        similar = lax.dot_general(
            rows, own, (((1,), (1,)), ((), ())), preferred_element_type=jnp.float32
        )
        down = jnp.broadcast_to(clusters, (count, count)).T[:, :1]
        kept = down == own_clusters
        if same_rows and place == 0:
            row = lax.broadcasted_iota(jnp.int32, similar.shape, 0)
            column = lax.broadcasted_iota(jnp.int32, similar.shape, 1)
            kept = kept & (row != column)
        found = jnp.max(jnp.where(kept, similar, NONE), axis=0, keepdims=True)
        best = found if best is None else jnp.maximum(best, found)
    return best


def early_kernel(refs, ids_ref, x_ids_ref, c_ids_ref, e_ids_ref, best_ref, own_ref, c_ref):
    mine, x, e, c = [unit_of(ref[...]) for ref in refs]
    own = jnp.concatenate([mine, x, e], axis=0)
    own_ids = jnp.concatenate([ids_ref[...], x_ids_ref[...], e_ids_ref[:1, :]], axis=1)
    best = best_of(own, own_ids, [mine, c], [ids_ref[...], c_ids_ref[...]], True)
    best_ref[...] = jnp.broadcast_to(best, best_ref.shape)
    own_ref[...] = own
    c_ref[...] = c


def early(blocks, ids):
    rows, width = blocks[0].shape
    return pl.pallas_call(
        early_kernel,
        out_shape=[
            jax.ShapeDtypeStruct((8, 3 * rows), jnp.float32),
            jax.ShapeDtypeStruct((3 * rows, width), jnp.bfloat16),
            jax.ShapeDtypeStruct((rows, width), jnp.bfloat16),
        ],
        in_specs=([VMEM] * len(blocks), *[VMEM] * len(ids)),
        out_specs=[VMEM] * 3,
        compiler_params=LIMIT,
        name="early",
    )(blocks, *ids)


def middle_kernel(
    best_ref, own_ref, c_ref, h_ref, ch_front_ref, ch_back_ref, ids_ref, x_ids_ref, c_ids_ref, e_ids_ref, h_ids_ref,
    mine_out_ref, x_out_ref, e_out_ref, far_ref,
):
    h = unit_of(h_ref[...])
    ch = jnp.concatenate([unit_of(ch_front_ref[...]), unit_of(ch_back_ref[...])], axis=0)
    own_ids = jnp.concatenate([ids_ref[...], x_ids_ref[...], e_ids_ref[:1, :]], axis=1)
    best = best_of(own_ref[...], own_ids, [h, ch], [h_ids_ref[:1, :], h_ids_ref[1:, :]])
    best = jnp.maximum(best, best_ref[:1, :])
    rows = c_ref.shape[0]
    for place, out_ref in enumerate((mine_out_ref, x_out_ref, e_out_ref)):
        out_ref[...] = jnp.broadcast_to(best[:, place * rows : (place + 1) * rows], out_ref.shape)
    far_ref[...] = jnp.concatenate([own_ref[:rows], c_ref[...], h, ch], axis=0)


def middle(best, own, c, h, ch, ids):
    rows, width = c.shape
    return pl.pallas_call(
        middle_kernel,
        out_shape=[jax.ShapeDtypeStruct((8, rows), jnp.float32)] * 3
        + [jax.ShapeDtypeStruct((4 * rows, width), jnp.bfloat16)],
        in_specs=[VMEM] * 11,
        out_specs=[VMEM] * 4,
        compiler_params=LIMIT,
        name="middle",
    )(best, own, c, h, *ch, *ids)


def late_kernel(far_ref, xe_ref, ids_ref, c_ids_ref, e_ids_ref, h_ids_ref, out_ref):
    xe = unit_of(xe_ref[...])
    rows = xe.shape[0]
    others = [far_ref[place * rows : (place + 1) * rows] for place in range(4)]
    other_ids = [ids_ref[...], c_ids_ref[...], h_ids_ref[:1, :], h_ids_ref[1:, :]]
    out_ref[...] = jnp.broadcast_to(best_of(xe, e_ids_ref[1:, :], others, other_ids), out_ref.shape)


def late(far, xe, ids):
    rows = xe.shape[0]
    return pl.pallas_call(
        late_kernel,
        out_shape=jax.ShapeDtypeStruct((8, rows), jnp.float32),
        in_specs=[VMEM] * 6,
        out_specs=VMEM,
        compiler_params=LIMIT,
        name="late",
    )(far, xe, *ids)


def square(embeddings, assignment):
    def swap(flip, array):
        return lax.ppermute(array, AXES, [(i, i ^ flip) for i in range(16)])

    rows = embeddings.shape[0]
    mine, ids = embeddings, assignment.reshape(1, rows)
    x_ids, c_ids = swap(SHARD, ids), swap(SUB, ids)
    x_ids, c_ids = swap(SHARD, ids), swap(SUB, ids)
    e = swap(LOW, mine)
    x = swap(SHARD, mine)
    h = swap(HIGH, mine)
    e_ids = swap(LOW, jnp.concatenate([ids, x_ids]))
    h_ids = swap(HIGH, jnp.concatenate([ids, c_ids]))
    mine_c = mine
    c = swap(SUB, mine_c)
    e_then, _, _ = lax.optimization_barrier((e, e_ids, x))
    h_then, _ = lax.optimization_barrier((h, h_ids))
    xe = swap(SHARD, e_then)
    ch = [swap(SUB, h_then[: rows // 2]), swap(SUB, h_then[rows // 2 :])]
    best, own, c = early([mine, x, e, c], [ids, x_ids, c_ids, e_ids])
    found, x_best, e_best, far = middle(best, own, c, h, ch, [ids, x_ids, c_ids, e_ids, h_ids])
    x_best, e_best = swap(SHARD, x_best), swap(LOW, e_best)
    xe_best = swap(LOW | SHARD, late(far, xe, [ids, c_ids, e_ids, h_ids]))
    return jnp.maximum(jnp.maximum(found, x_best), jnp.maximum(e_best, xe_best))[0]


def shared_owner(embeddings, assignment):
    route, gather = AXES[:1], AXES[1:]
    owners = lax.axis_size(route)
    flip = jnp.zeros((1, 1), jnp.int32)
    (sent,) = pack(flip, embeddings, assignment, 1)
    got = lax.all_to_all(sent, route, split_axis=0, concat_axis=0, tiled=True)
    others = lax.all_gather(got, gather, axis=0, tiled=True)
    first = (lax.axis_index(gather) * SLOTS).astype(jnp.int32).reshape(1, 1)
    best = shared_best_of(got, others, first, owners)
    returned = lax.all_to_all(best, route, split_axis=0, concat_axis=0, tiled=True)
    return unpack(flip, [returned[i] for i in range(owners)], assignment)


def solution(mesh):
    placed = (
        P(("groups", "blk", "shard", "sub"), None),
        P(("groups", "blk", "shard", "sub"), None),
    )
    four_bits = [mesh.shape[axis] for axis in AXES] == [4, 2, 2]
    program = square if four_bits else shared_owner
    return jax.shard_map(
        program,
        mesh=mesh,
        in_specs=placed,
        out_specs=P(("groups", "blk", "shard", "sub")),
        check_vma=False,
    )
```

```python
import functools
import math

import jax
import jax.numpy as jnp
from jax import lax
from jax.experimental import pallas as pl
from jax.experimental.pallas import tpu as pltpu
from jax.sharding import PartitionSpec as P

CLUSTERS = 16
CAP = 16
SLOTS = CLUSTERS * CAP
LANES = 128
EMPTY = 4.0
NONE = -2.0
HIGH, LOW, SHARD, SUB = 8, 4, 2, 1
LIMIT = pltpu.CompilerParams(vmem_limit_bytes=12 << 20)
AXES = ("blk", "shard", "sub")

VMEM = pl.BlockSpec(memory_space=pltpu.VMEM)
SMEM = pl.BlockSpec(memory_space=pltpu.SMEM)


def placement(cluster, flip):
    rows = cluster.shape[1]
    label = lax.broadcasted_iota(jnp.int32, (CLUSTERS, rows), 0)
    member = (cluster == label).astype(jnp.float32)
    before = lax.broadcasted_iota(jnp.int32, (rows, rows), 0) < lax.broadcasted_iota(
        jnp.int32, (rows, rows), 1
    )
    earlier = jnp.dot(
        member.astype(jnp.bfloat16),
        before.astype(jnp.float32).astype(jnp.bfloat16),
        preferred_element_type=jnp.float32,
    )
    within = jnp.sum(earlier * member, axis=0, keepdims=True).astype(jnp.int32)
    target = (cluster ^ flip) * CAP + within
    return lax.broadcasted_iota(jnp.int32, (SLOTS, rows), 0) == target


def pack_kernel(flip_ref, rows_ref, cluster_ref, *out_refs):
    values = rows_ref[...].astype(jnp.float32)
    width = values.shape[1]
    scaled = values * lax.rsqrt(jnp.mean(values * values, axis=1, keepdims=True) + 1e-06)
    unit = (scaled * (1.0 / math.sqrt(width))).astype(jnp.bfloat16)
    placed = placement(cluster_ref[...], flip_ref[0, 0]).astype(jnp.float32)
    slots = jnp.dot(placed.astype(jnp.bfloat16), unit, preferred_element_type=jnp.float32)
    used = jnp.sum(placed, axis=1, keepdims=True)
    first = lax.broadcasted_iota(jnp.int32, slots.shape, 1) == 0
    slots = jnp.where(first & (used < 0.5), EMPTY, slots).astype(jnp.bfloat16)
    count = SLOTS // len(out_refs)
    for block, out_ref in enumerate(out_refs):
        out_ref[...] = slots[block * count : (block + 1) * count]


def pack(flip, embeddings, assignment, blocks):
    rows, width = embeddings.shape
    return pl.pallas_call(
        pack_kernel,
        out_shape=[jax.ShapeDtypeStruct((SLOTS // blocks, width), jnp.bfloat16)] * blocks,
        in_specs=[SMEM, VMEM, VMEM],
        out_specs=[VMEM] * blocks,
        name="pack",
    )(flip, embeddings, assignment.reshape(1, rows))


def shared_best_kernel(count, first_ref, slots_ref, others_ref, out_ref, best_ref):
    step = pl.program_id(0)
    slots, others = slots_ref[...], others_ref[...]
    similar = lax.dot_general(
        others, slots, (((1,), (1,)), ((), ())), preferred_element_type=jnp.float32
    )
    used = others[:, :1].astype(jnp.float32) < 2.0
    row = lax.broadcasted_iota(jnp.int32, similar.shape, 0)
    column = lax.broadcasted_iota(jnp.int32, similar.shape, 1)
    kept = used & (row + step * slots.shape[0] != column + first_ref[0, 0])
    kept = kept & (row % count // CAP == column % count // CAP)
    best = jnp.max(jnp.where(kept, similar, NONE), axis=0, keepdims=True)

    @pl.when(step == 0)
    def _():
        best_ref[...] = best

    @pl.when(step > 0)
    def _():
        best_ref[...] = jnp.maximum(best_ref[...], best)

    @pl.when(step == pl.num_programs(0) - 1)
    def _():
        for source in range(out_ref.shape[0]):
            piece = best_ref[:, source * count : (source + 1) * count]
            out_ref[source, :, :count] = jnp.broadcast_to(piece, (8, count))
            if count < LANES:
                out_ref[source, :, count:] = jnp.full((8, LANES - count), NONE)


def shared_best_of(slots, others, first, owners):
    size, width = slots.shape
    return pl.pallas_call(
        functools.partial(shared_best_kernel, size // owners),
        grid=(others.shape[0] // size,),
        out_shape=jax.ShapeDtypeStruct((owners, 8, LANES), jnp.float32),
        in_specs=[
            pl.BlockSpec((1, 1), lambda i: (0, 0), memory_space=pltpu.SMEM),
            pl.BlockSpec((size, width), lambda i: (0, 0)),
            pl.BlockSpec((size, width), lambda i: (i, 0)),
        ],
        out_specs=pl.BlockSpec((owners, 8, LANES), lambda i: (0, 0, 0)),
        scratch_shapes=[pltpu.VMEM((1, size), jnp.float32)],
        name="shared_best",
    )(first, slots, others)


def unpack_kernel(flip_ref, cluster_ref, *refs):
    returned_refs, out_ref = refs[:-1], refs[-1]
    count = SLOTS // len(returned_refs)
    placed = placement(cluster_ref[...], flip_ref[0, 0])
    returned = jnp.concatenate(
        [jnp.broadcast_to(ref[:1, :], (count, LANES)) for ref in returned_refs], axis=0
    )
    slot = lax.broadcasted_iota(jnp.int32, (SLOTS, LANES), 0) % count
    lane = lax.broadcasted_iota(jnp.int32, (SLOTS, LANES), 1)
    by_slot = jnp.max(jnp.where(slot == lane, returned, NONE), axis=1, keepdims=True)
    out_ref[...] = jnp.max(jnp.where(placed, by_slot, NONE), axis=0, keepdims=True)


def unpack(flip, returned, assignment):
    rows = assignment.shape[0]
    return pl.pallas_call(
        unpack_kernel,
        out_shape=jax.ShapeDtypeStruct((1, rows), jnp.float32),
        in_specs=[SMEM, VMEM] + [VMEM] * len(returned),
        out_specs=VMEM,
        name="unpack",
    )(flip, assignment.reshape(1, rows), *returned).reshape(-1)


def unit_of(values):
    values = values.astype(jnp.float32)
    scaled = values * lax.rsqrt(jnp.mean(values * values, axis=1, keepdims=True) + 1e-06)
    return (scaled * (1.0 / math.sqrt(values.shape[1]))).astype(jnp.bfloat16)


def best_of(own, own_clusters, others, other_clusters, same_rows=False):
    best = None
    for place, (rows, clusters) in enumerate(zip(others, other_clusters)):
        count = rows.shape[0]
        similar = lax.dot_general(
            rows, own, (((1,), (1,)), ((), ())), preferred_element_type=jnp.float32
        )
        down = jnp.broadcast_to(clusters, (count, count)).T[:, :1]
        kept = down == own_clusters
        if same_rows and place == 0:
            row = lax.broadcasted_iota(jnp.int32, similar.shape, 0)
            column = lax.broadcasted_iota(jnp.int32, similar.shape, 1)
            kept = kept & (row != column)
        found = jnp.max(jnp.where(kept, similar, NONE), axis=0, keepdims=True)
        best = found if best is None else jnp.maximum(best, found)
    return best


def block(refs):
    return jnp.concatenate([unit_of(ref[...]) for ref in refs], axis=0)


def early_kernel(mine_ref, x_refs, e_refs, c_refs, ids_ref, x_ids_ref, c_ids_ref, e_ids_ref, best_ref, own_ref, c_ref):
    mine, c = unit_of(mine_ref[...]), block(c_refs)
    own = jnp.concatenate([mine, block(x_refs), block(e_refs)], axis=0)
    own_ids = jnp.concatenate([ids_ref[...], x_ids_ref[...], e_ids_ref[:1, :]], axis=1)
    best = best_of(own, own_ids, [mine, c], [ids_ref[...], c_ids_ref[...]], True)
    best_ref[...] = jnp.broadcast_to(best, best_ref.shape)
    own_ref[...] = own
    c_ref[...] = c


def early(mine, x, e, c, ids):
    rows, width = mine.shape
    return pl.pallas_call(
        early_kernel,
        out_shape=[
            jax.ShapeDtypeStruct((8, 3 * rows), jnp.float32),
            jax.ShapeDtypeStruct((3 * rows, width), jnp.bfloat16),
            jax.ShapeDtypeStruct((rows, width), jnp.bfloat16),
        ],
        in_specs=(VMEM, [VMEM] * len(x), [VMEM] * len(e), [VMEM] * len(c), *[VMEM] * len(ids)),
        out_specs=[VMEM] * 3,
        compiler_params=LIMIT,
        name="early",
    )(mine, x, e, c, *ids)


def middle_kernel(
    best_ref, own_ref, c_ref, h_refs, ch_refs, ids_ref, x_ids_ref, c_ids_ref, e_ids_ref, h_ids_ref,
    mine_out_ref, x_out_ref, e_out_ref, far_ref,
):
    h, ch = block(h_refs), block(ch_refs)
    own_ids = jnp.concatenate([ids_ref[...], x_ids_ref[...], e_ids_ref[:1, :]], axis=1)
    best = best_of(own_ref[...], own_ids, [h, ch], [h_ids_ref[:1, :], h_ids_ref[1:, :]])
    best = jnp.maximum(best, best_ref[:1, :])
    rows = c_ref.shape[0]
    for place, out_ref in enumerate((mine_out_ref, x_out_ref, e_out_ref)):
        out_ref[...] = jnp.broadcast_to(best[:, place * rows : (place + 1) * rows], out_ref.shape)
    far_ref[...] = jnp.concatenate([own_ref[:rows], c_ref[...], h, ch], axis=0)


def middle(best, own, c, h, ch, ids):
    rows, width = c.shape
    return pl.pallas_call(
        middle_kernel,
        out_shape=[jax.ShapeDtypeStruct((8, rows), jnp.float32)] * 3
        + [jax.ShapeDtypeStruct((4 * rows, width), jnp.bfloat16)],
        in_specs=(VMEM, VMEM, VMEM, [VMEM] * len(h), [VMEM] * len(ch), *[VMEM] * len(ids)),
        out_specs=[VMEM] * 4,
        compiler_params=LIMIT,
        name="middle",
    )(best, own, c, h, ch, *ids)


def late_kernel(far_ref, xe_refs, ids_ref, c_ids_ref, e_ids_ref, h_ids_ref, out_ref):
    xe = block(xe_refs)
    rows = xe.shape[0]
    others = [far_ref[place * rows : (place + 1) * rows] for place in range(4)]
    other_ids = [ids_ref[...], c_ids_ref[...], h_ids_ref[:1, :], h_ids_ref[1:, :]]
    out_ref[...] = jnp.broadcast_to(best_of(xe, e_ids_ref[1:, :], others, other_ids), out_ref.shape)


def late(far, xe, ids):
    return pl.pallas_call(
        late_kernel,
        out_shape=jax.ShapeDtypeStruct((8, far.shape[0] // 4), jnp.float32),
        in_specs=(VMEM, [VMEM] * len(xe), *[VMEM] * len(ids)),
        out_specs=VMEM,
        compiler_params=LIMIT,
        name="late",
    )(far, xe, *ids)


def square(embeddings, assignment):
    def swap(flip, array):
        return lax.ppermute(array, AXES, [(i, i ^ flip) for i in range(16)])

    rows = embeddings.shape[0]
    mine, ids = embeddings, assignment.reshape(1, rows)
    c = swap(SUB, mine)
    e = swap(LOW, mine)
    x = swap(SHARD, mine)
    far, _ = lax.optimization_barrier((mine, c))
    h = swap(HIGH, far)
    x_ids, c_ids = swap(SHARD, ids), swap(SUB, ids)
    e_ids = swap(LOW, jnp.concatenate([ids, x_ids]))
    h_ids = swap(HIGH, jnp.concatenate([ids, c_ids]))
    e_then, _, _ = lax.optimization_barrier((e, x, e_ids))
    xe = [swap(SHARD, e_then[:rows * 3 // 4]), swap(LOW, x[rows * 3 // 4:])]
    h_then, _ = lax.optimization_barrier((h, h_ids))
    ch = [swap(SUB, h_then[: rows // 2]), swap(SUB, h_then[rows // 2 :])]
    x, e, h, c = [x], [e], [h], [c]
    best, own, c = early(mine, x, e, c, [ids, x_ids, c_ids, e_ids])
    found, x_best, e_best, far = middle(best, own, c, h, ch, [ids, x_ids, c_ids, e_ids, h_ids])
    xe_best = late(far, xe, [ids, c_ids, e_ids, h_ids])
    x_best, e_best, xe_best = lax.optimization_barrier((x_best, e_best, xe_best))
    xe_best, e_best, x_best = swap(LOW | SHARD, xe_best), swap(LOW, e_best), swap(SHARD, x_best)
    return jnp.maximum(jnp.maximum(jnp.maximum(xe_best, e_best), x_best), found)[0]


def shared_owner(embeddings, assignment):
    route, gather = AXES[:1], AXES[1:]
    owners = lax.axis_size(route)
    flip = jnp.zeros((1, 1), jnp.int32)
    (sent,) = pack(flip, embeddings, assignment, 1)
    got = lax.all_to_all(sent, route, split_axis=0, concat_axis=0, tiled=True)
    others = lax.all_gather(got, gather, axis=0, tiled=True)
    first = (lax.axis_index(gather) * SLOTS).astype(jnp.int32).reshape(1, 1)
    best = shared_best_of(got, others, first, owners)
    returned = lax.all_to_all(best, route, split_axis=0, concat_axis=0, tiled=True)
    return unpack(flip, [returned[i] for i in range(owners)], assignment)


def solution(mesh):
    placed = (
        P(("groups", "blk", "shard", "sub"), None),
        P(("groups", "blk", "shard", "sub"), None),
    )
    four_bits = [mesh.shape[axis] for axis in AXES] == [4, 2, 2]
    program = square if four_bits else shared_owner
    return jax.shard_map(
        program,
        mesh=mesh,
        in_specs=placed,
        out_specs=P(("groups", "blk", "shard", "sub")),
        check_vma=False,
    )
```

```python
import functools
import math

import jax
import jax.numpy as jnp
from jax import lax
from jax.experimental import pallas as pl
from jax.experimental.pallas import tpu as pltpu
from jax.sharding import PartitionSpec as P

CLUSTERS = 16
CAP = 16
SLOTS = CLUSTERS * CAP
LANES = 128
EMPTY = 4.0
NONE = -2.0
TAIL = 8
HIGH, LOW, SHARD, SUB = 8, 4, 2, 1
LIMIT = pltpu.CompilerParams(vmem_limit_bytes=12 << 20)
AXES = ("blk", "shard", "sub")

VMEM = pl.BlockSpec(memory_space=pltpu.VMEM)
SMEM = pl.BlockSpec(memory_space=pltpu.SMEM)


def placement(cluster, flip):
    rows = cluster.shape[1]
    label = lax.broadcasted_iota(jnp.int32, (CLUSTERS, rows), 0)
    member = (cluster == label).astype(jnp.float32)
    before = lax.broadcasted_iota(jnp.int32, (rows, rows), 0) < lax.broadcasted_iota(
        jnp.int32, (rows, rows), 1
    )
    earlier = jnp.dot(
        member.astype(jnp.bfloat16),
        before.astype(jnp.float32).astype(jnp.bfloat16),
        preferred_element_type=jnp.float32,
    )
    within = jnp.sum(earlier * member, axis=0, keepdims=True).astype(jnp.int32)
    target = (cluster ^ flip) * CAP + within
    return lax.broadcasted_iota(jnp.int32, (SLOTS, rows), 0) == target


def pack_kernel(flip_ref, rows_ref, cluster_ref, *out_refs):
    values = rows_ref[...].astype(jnp.float32)
    width = values.shape[1]
    scaled = values * lax.rsqrt(jnp.mean(values * values, axis=1, keepdims=True) + 1e-06)
    unit = (scaled * (1.0 / math.sqrt(width))).astype(jnp.bfloat16)
    placed = placement(cluster_ref[...], flip_ref[0, 0]).astype(jnp.float32)
    slots = jnp.dot(placed.astype(jnp.bfloat16), unit, preferred_element_type=jnp.float32)
    used = jnp.sum(placed, axis=1, keepdims=True)
    first = lax.broadcasted_iota(jnp.int32, slots.shape, 1) == 0
    slots = jnp.where(first & (used < 0.5), EMPTY, slots).astype(jnp.bfloat16)
    count = SLOTS // len(out_refs)
    for block, out_ref in enumerate(out_refs):
        out_ref[...] = slots[block * count : (block + 1) * count]


def pack(flip, embeddings, assignment, blocks):
    rows, width = embeddings.shape
    return pl.pallas_call(
        pack_kernel,
        out_shape=[jax.ShapeDtypeStruct((SLOTS // blocks, width), jnp.bfloat16)] * blocks,
        in_specs=[SMEM, VMEM, VMEM],
        out_specs=[VMEM] * blocks,
        name="pack",
    )(flip, embeddings, assignment.reshape(1, rows))


def shared_best_kernel(count, first_ref, slots_ref, others_ref, out_ref, best_ref):
    step = pl.program_id(0)
    slots, others = slots_ref[...], others_ref[...]
    similar = lax.dot_general(
        others, slots, (((1,), (1,)), ((), ())), preferred_element_type=jnp.float32
    )
    used = others[:, :1].astype(jnp.float32) < 2.0
    row = lax.broadcasted_iota(jnp.int32, similar.shape, 0)
    column = lax.broadcasted_iota(jnp.int32, similar.shape, 1)
    kept = used & (row + step * slots.shape[0] != column + first_ref[0, 0])
    kept = kept & (row % count // CAP == column % count // CAP)
    best = jnp.max(jnp.where(kept, similar, NONE), axis=0, keepdims=True)

    @pl.when(step == 0)
    def _():
        best_ref[...] = best

    @pl.when(step > 0)
    def _():
        best_ref[...] = jnp.maximum(best_ref[...], best)

    @pl.when(step == pl.num_programs(0) - 1)
    def _():
        for source in range(out_ref.shape[0]):
            piece = best_ref[:, source * count : (source + 1) * count]
            out_ref[source, :, :count] = jnp.broadcast_to(piece, (8, count))
            if count < LANES:
                out_ref[source, :, count:] = jnp.full((8, LANES - count), NONE)


def shared_best_of(slots, others, first, owners):
    size, width = slots.shape
    return pl.pallas_call(
        functools.partial(shared_best_kernel, size // owners),
        grid=(others.shape[0] // size,),
        out_shape=jax.ShapeDtypeStruct((owners, 8, LANES), jnp.float32),
        in_specs=[
            pl.BlockSpec((1, 1), lambda i: (0, 0), memory_space=pltpu.SMEM),
            pl.BlockSpec((size, width), lambda i: (0, 0)),
            pl.BlockSpec((size, width), lambda i: (i, 0)),
        ],
        out_specs=pl.BlockSpec((owners, 8, LANES), lambda i: (0, 0, 0)),
        scratch_shapes=[pltpu.VMEM((1, size), jnp.float32)],
        name="shared_best",
    )(first, slots, others)


def unpack_kernel(flip_ref, cluster_ref, *refs):
    returned_refs, out_ref = refs[:-1], refs[-1]
    count = SLOTS // len(returned_refs)
    placed = placement(cluster_ref[...], flip_ref[0, 0])
    returned = jnp.concatenate(
        [jnp.broadcast_to(ref[:1, :], (count, LANES)) for ref in returned_refs], axis=0
    )
    slot = lax.broadcasted_iota(jnp.int32, (SLOTS, LANES), 0) % count
    lane = lax.broadcasted_iota(jnp.int32, (SLOTS, LANES), 1)
    by_slot = jnp.max(jnp.where(slot == lane, returned, NONE), axis=1, keepdims=True)
    out_ref[...] = jnp.max(jnp.where(placed, by_slot, NONE), axis=0, keepdims=True)


def unpack(flip, returned, assignment):
    rows = assignment.shape[0]
    return pl.pallas_call(
        unpack_kernel,
        out_shape=jax.ShapeDtypeStruct((1, rows), jnp.float32),
        in_specs=[SMEM, VMEM] + [VMEM] * len(returned),
        out_specs=VMEM,
        name="unpack",
    )(flip, assignment.reshape(1, rows), *returned).reshape(-1)


def unit_of(values):
    values = values.astype(jnp.float32)
    scaled = values * lax.rsqrt(jnp.mean(values * values, axis=1, keepdims=True) + 1e-06)
    return (scaled * (1.0 / math.sqrt(values.shape[1]))).astype(jnp.bfloat16)


def normalize_kernel(rows_ref, tail_ref, whole_ref, front_ref, back_ref):
    rows, width = rows_ref.shape
    half = rows // 2
    unit = unit_of(rows_ref[...])
    tail = jnp.concatenate([tail_ref[...], jnp.zeros((TAIL, width - rows), jnp.bfloat16)], axis=1)
    whole_ref[:rows] = unit
    whole_ref[rows:] = tail
    front_ref[...] = unit[:half]
    back_ref[:half] = unit[half:]
    back_ref[half:] = tail


def normalize(embeddings, assignment):
    rows, width = embeddings.shape
    tail = jnp.broadcast_to(assignment.reshape(1, rows).astype(jnp.bfloat16), (TAIL, rows))
    return pl.pallas_call(
        normalize_kernel,
        out_shape=[
            jax.ShapeDtypeStruct((size, width), jnp.bfloat16)
            for size in (rows + TAIL, rows // 2, rows // 2 + TAIL)
        ],
        in_specs=[VMEM, VMEM],
        out_specs=[VMEM] * 3,
        compiler_params=LIMIT,
        name="normalize",
    )(embeddings, tail)


def block(refs):
    pieces = [ref[...] for ref in refs[:-1]] + [refs[-1][: refs[-1].shape[0] - TAIL]]
    rows = pieces[0] if len(pieces) == 1 else jnp.concatenate(pieces, axis=0)
    return rows, refs[-1][pieces[-1].shape[0] :, : rows.shape[0]][:1].astype(jnp.float32)


def best_of(own, others, same_rows=False):
    rows, clusters = zip(*own)
    rows, clusters = jnp.concatenate(rows, axis=0), jnp.concatenate(clusters, axis=1)
    best = None
    for place, (other_rows, other_clusters) in enumerate(others):
        count = other_rows.shape[0]
        similar = lax.dot_general(
            other_rows, rows, (((1,), (1,)), ((), ())), preferred_element_type=jnp.float32
        )
        down = jnp.broadcast_to(other_clusters, (count, count)).T[:, :1]
        kept = down == clusters
        if same_rows and place == 0:
            row = lax.broadcasted_iota(jnp.int32, similar.shape, 0)
            column = lax.broadcasted_iota(jnp.int32, similar.shape, 1)
            kept = kept & (row != column)
        found = jnp.max(jnp.where(kept, similar, NONE), axis=0, keepdims=True)
        best = found if best is None else jnp.maximum(best, found)
    return best


def early_kernel(mine_refs, x_refs, e_refs, c_refs, out_ref):
    mine = block(mine_refs)
    best = best_of([mine, block(x_refs), block(e_refs)], [mine, block(c_refs)], True)
    out_ref[...] = jnp.broadcast_to(best, out_ref.shape)


def middle_kernel(best_ref, mine_refs, x_refs, e_refs, h_refs, ch_refs, *out_refs):
    best = best_of([block(mine_refs), block(x_refs), block(e_refs)], [block(h_refs), block(ch_refs)])
    best = jnp.maximum(best, best_ref[:1, :])
    for place, out_ref in enumerate(out_refs):
        rows = out_ref.shape[1]
        out_ref[...] = jnp.broadcast_to(best[:, place * rows : (place + 1) * rows], out_ref.shape)


def late_kernel(xe_refs, mine_refs, c_refs, h_refs, ch_refs, out_ref):
    others = [block(refs) for refs in (mine_refs, c_refs, h_refs, ch_refs)]
    out_ref[...] = jnp.broadcast_to(best_of([block(xe_refs)], others), out_ref.shape)


def call(kernel, name, out_shape, arrays):
    return pl.pallas_call(
        kernel,
        out_shape=out_shape,
        in_specs=jax.tree.map(lambda _: VMEM, tuple(arrays)),
        out_specs=jax.tree.map(lambda _: VMEM, out_shape),
        compiler_params=LIMIT,
        name=name,
    )(*arrays)


def square(embeddings, assignment):
    def swap(flip, array):
        return lax.ppermute(array, AXES, [(i, i ^ flip) for i in range(16)])

    rows = embeddings.shape[0]
    bests = jax.ShapeDtypeStruct((8, rows), jnp.float32)
    mine, front, back = normalize(embeddings, assignment)
    x = swap(SHARD, mine)
    h = swap(HIGH, mine)
    e_front, e_back = swap(LOW, front), swap(LOW, back)
    mine_then, _ = lax.optimization_barrier((mine, x))
    c = swap(SUB, mine_then)
    xe_front, xe_back = swap(SHARD, e_front), swap(SHARD, e_back)
    h_then, _ = lax.optimization_barrier((h, xe_front))
    cuts = [rows * k // 4 for k in range(4)] + [rows + TAIL]
    ch = [swap(SUB, h_then[begin:end]) for begin, end in zip(cuts, cuts[1:])]
    x, h, c, e, xe = [x], [h], [c], [e_front, e_back], [xe_front, xe_back]
    mine = [mine]
    best = call(early_kernel, "early", jax.ShapeDtypeStruct((8, 3 * rows), jnp.float32), (mine, x, e, c))
    found, x_best, e_best = call(middle_kernel, "middle", [bests] * 3, (best, mine, x, e, h, ch))
    x_best, e_best = swap(SHARD, x_best), swap(LOW, e_best)
    xe_best = swap(LOW | SHARD, call(late_kernel, "late", bests, (xe, mine, c, h, ch)))
    return jnp.maximum(jnp.maximum(found, x_best), jnp.maximum(e_best, xe_best))[0]


def shared_owner(embeddings, assignment):
    route, gather = AXES[:1], AXES[1:]
    owners = lax.axis_size(route)
    flip = jnp.zeros((1, 1), jnp.int32)
    (sent,) = pack(flip, embeddings, assignment, 1)
    got = lax.all_to_all(sent, route, split_axis=0, concat_axis=0, tiled=True)
    others = lax.all_gather(got, gather, axis=0, tiled=True)
    first = (lax.axis_index(gather) * SLOTS).astype(jnp.int32).reshape(1, 1)
    best = shared_best_of(got, others, first, owners)
    returned = lax.all_to_all(best, route, split_axis=0, concat_axis=0, tiled=True)
    return unpack(flip, [returned[i] for i in range(owners)], assignment)


def solution(mesh):
    placed = (
        P(("groups", "blk", "shard", "sub"), None),
        P(("groups", "blk", "shard", "sub"), None),
    )
    four_bits = [mesh.shape[axis] for axis in AXES] == [4, 2, 2]
    program = square if four_bits else shared_owner
    return jax.shard_map(
        program,
        mesh=mesh,
        in_specs=placed,
        out_specs=P(("groups", "blk", "shard", "sub")),
        check_vma=False,
    )
```

```python
import functools
import math

import jax
import jax.numpy as jnp
from jax import lax
from jax.experimental import pallas as pl
from jax.experimental.pallas import tpu as pltpu
from jax.sharding import PartitionSpec as P

CLUSTERS = 16
CAP = 16
SLOTS = CLUSTERS * CAP
LANES = 128
EMPTY = 4.0
NONE = -2.0
HIGH, LOW, SHARD, SUB = 8, 4, 2, 1
LIMIT = pltpu.CompilerParams(vmem_limit_bytes=12 << 20)
AXES = ("blk", "shard", "sub")

VMEM = pl.BlockSpec(memory_space=pltpu.VMEM)
SMEM = pl.BlockSpec(memory_space=pltpu.SMEM)


def placement(cluster, flip):
    rows = cluster.shape[1]
    label = lax.broadcasted_iota(jnp.int32, (CLUSTERS, rows), 0)
    member = (cluster == label).astype(jnp.float32)
    before = lax.broadcasted_iota(jnp.int32, (rows, rows), 0) < lax.broadcasted_iota(
        jnp.int32, (rows, rows), 1
    )
    earlier = jnp.dot(
        member.astype(jnp.bfloat16),
        before.astype(jnp.float32).astype(jnp.bfloat16),
        preferred_element_type=jnp.float32,
    )
    within = jnp.sum(earlier * member, axis=0, keepdims=True).astype(jnp.int32)
    target = (cluster ^ flip) * CAP + within
    return lax.broadcasted_iota(jnp.int32, (SLOTS, rows), 0) == target


def pack_kernel(flip_ref, rows_ref, cluster_ref, *out_refs):
    values = rows_ref[...].astype(jnp.float32)
    width = values.shape[1]
    scaled = values * lax.rsqrt(jnp.mean(values * values, axis=1, keepdims=True) + 1e-06)
    unit = (scaled * (1.0 / math.sqrt(width))).astype(jnp.bfloat16)
    placed = placement(cluster_ref[...], flip_ref[0, 0]).astype(jnp.float32)
    slots = jnp.dot(placed.astype(jnp.bfloat16), unit, preferred_element_type=jnp.float32)
    used = jnp.sum(placed, axis=1, keepdims=True)
    first = lax.broadcasted_iota(jnp.int32, slots.shape, 1) == 0
    slots = jnp.where(first & (used < 0.5), EMPTY, slots).astype(jnp.bfloat16)
    count = SLOTS // len(out_refs)
    for block, out_ref in enumerate(out_refs):
        out_ref[...] = slots[block * count : (block + 1) * count]


def pack(flip, embeddings, assignment, blocks):
    rows, width = embeddings.shape
    return pl.pallas_call(
        pack_kernel,
        out_shape=[jax.ShapeDtypeStruct((SLOTS // blocks, width), jnp.bfloat16)] * blocks,
        in_specs=[SMEM, VMEM, VMEM],
        out_specs=[VMEM] * blocks,
        name="pack",
    )(flip, embeddings, assignment.reshape(1, rows))


def shared_best_kernel(count, first_ref, slots_ref, others_ref, out_ref, best_ref):
    step = pl.program_id(0)
    slots, others = slots_ref[...], others_ref[...]
    similar = lax.dot_general(
        others, slots, (((1,), (1,)), ((), ())), preferred_element_type=jnp.float32
    )
    used = others[:, :1].astype(jnp.float32) < 2.0
    row = lax.broadcasted_iota(jnp.int32, similar.shape, 0)
    column = lax.broadcasted_iota(jnp.int32, similar.shape, 1)
    kept = used & (row + step * slots.shape[0] != column + first_ref[0, 0])
    kept = kept & (row % count // CAP == column % count // CAP)
    best = jnp.max(jnp.where(kept, similar, NONE), axis=0, keepdims=True)

    @pl.when(step == 0)
    def _():
        best_ref[...] = best

    @pl.when(step > 0)
    def _():
        best_ref[...] = jnp.maximum(best_ref[...], best)

    @pl.when(step == pl.num_programs(0) - 1)
    def _():
        for source in range(out_ref.shape[0]):
            piece = best_ref[:, source * count : (source + 1) * count]
            out_ref[source, :, :count] = jnp.broadcast_to(piece, (8, count))
            if count < LANES:
                out_ref[source, :, count:] = jnp.full((8, LANES - count), NONE)


def shared_best_of(slots, others, first, owners):
    size, width = slots.shape
    return pl.pallas_call(
        functools.partial(shared_best_kernel, size // owners),
        grid=(others.shape[0] // size,),
        out_shape=jax.ShapeDtypeStruct((owners, 8, LANES), jnp.float32),
        in_specs=[
            pl.BlockSpec((1, 1), lambda i: (0, 0), memory_space=pltpu.SMEM),
            pl.BlockSpec((size, width), lambda i: (0, 0)),
            pl.BlockSpec((size, width), lambda i: (i, 0)),
        ],
        out_specs=pl.BlockSpec((owners, 8, LANES), lambda i: (0, 0, 0)),
        scratch_shapes=[pltpu.VMEM((1, size), jnp.float32)],
        name="shared_best",
    )(first, slots, others)


def unpack_kernel(flip_ref, cluster_ref, *refs):
    returned_refs, out_ref = refs[:-1], refs[-1]
    count = SLOTS // len(returned_refs)
    placed = placement(cluster_ref[...], flip_ref[0, 0])
    returned = jnp.concatenate(
        [jnp.broadcast_to(ref[:1, :], (count, LANES)) for ref in returned_refs], axis=0
    )
    slot = lax.broadcasted_iota(jnp.int32, (SLOTS, LANES), 0) % count
    lane = lax.broadcasted_iota(jnp.int32, (SLOTS, LANES), 1)
    by_slot = jnp.max(jnp.where(slot == lane, returned, NONE), axis=1, keepdims=True)
    out_ref[...] = jnp.max(jnp.where(placed, by_slot, NONE), axis=0, keepdims=True)


def unpack(flip, returned, assignment):
    rows = assignment.shape[0]
    return pl.pallas_call(
        unpack_kernel,
        out_shape=jax.ShapeDtypeStruct((1, rows), jnp.float32),
        in_specs=[SMEM, VMEM] + [VMEM] * len(returned),
        out_specs=VMEM,
        name="unpack",
    )(flip, assignment.reshape(1, rows), *returned).reshape(-1)


def unit_of(values):
    values = values.astype(jnp.float32)
    scaled = values * lax.rsqrt(jnp.mean(values * values, axis=1, keepdims=True) + 1e-06)
    return (scaled * (1.0 / math.sqrt(values.shape[1]))).astype(jnp.bfloat16)


def best_of(own, own_clusters, others, other_clusters, same_rows=False):
    best = None
    for place, (rows, clusters) in enumerate(zip(others, other_clusters)):
        count = rows.shape[0]
        similar = lax.dot_general(
            rows, own, (((1,), (1,)), ((), ())), preferred_element_type=jnp.float32
        )
        down = jnp.broadcast_to(clusters, (count, count)).T[:, :1]
        kept = down == own_clusters
        if same_rows and place == 0:
            row = lax.broadcasted_iota(jnp.int32, similar.shape, 0)
            column = lax.broadcasted_iota(jnp.int32, similar.shape, 1)
            kept = kept & (row != column)
        found = jnp.max(jnp.where(kept, similar, NONE), axis=0, keepdims=True)
        best = found if best is None else jnp.maximum(best, found)
    return best


def block(refs):
    return jnp.concatenate([unit_of(ref[...]) for ref in refs], axis=0)


def early_kernel(mine_ref, x_refs, e_refs, c_refs, ids_ref, x_ids_ref, c_ids_ref, e_ids_ref, best_ref, own_ref, c_ref):
    mine, c = unit_of(mine_ref[...]), block(c_refs)
    own = jnp.concatenate([mine, block(x_refs), block(e_refs)], axis=0)
    own_ids = jnp.concatenate([ids_ref[...], x_ids_ref[...], e_ids_ref[:1, :]], axis=1)
    best = best_of(own, own_ids, [mine, c], [ids_ref[...], c_ids_ref[...]], True)
    best_ref[...] = jnp.broadcast_to(best, best_ref.shape)
    own_ref[...] = own
    c_ref[...] = c


def early(mine, x, e, c, ids):
    rows, width = mine.shape
    return pl.pallas_call(
        early_kernel,
        out_shape=[
            jax.ShapeDtypeStruct((8, 3 * rows), jnp.float32),
            jax.ShapeDtypeStruct((3 * rows, width), jnp.bfloat16),
            jax.ShapeDtypeStruct((rows, width), jnp.bfloat16),
        ],
        in_specs=(VMEM, [VMEM] * len(x), [VMEM] * len(e), [VMEM] * len(c), *[VMEM] * len(ids)),
        out_specs=[VMEM] * 3,
        compiler_params=LIMIT,
        name="early",
    )(mine, x, e, c, *ids)


def middle_kernel(
    best_ref, own_ref, c_ref, h_refs, ch_refs, ids_ref, x_ids_ref, c_ids_ref, e_ids_ref, h_ids_ref,
    mine_out_ref, x_out_ref, e_out_ref, far_ref,
):
    h, ch = block(h_refs), block(ch_refs)
    own_ids = jnp.concatenate([ids_ref[...], x_ids_ref[...], e_ids_ref[:1, :]], axis=1)
    best = best_of(own_ref[...], own_ids, [h, ch], [h_ids_ref[:1, :], h_ids_ref[1:, :]])
    best = jnp.maximum(best, best_ref[:1, :])
    rows = c_ref.shape[0]
    for place, out_ref in enumerate((mine_out_ref, x_out_ref, e_out_ref)):
        out_ref[...] = jnp.broadcast_to(best[:, place * rows : (place + 1) * rows], out_ref.shape)
    far_ref[...] = jnp.concatenate([own_ref[:rows], c_ref[...], h, ch], axis=0)


def middle(best, own, c, h, ch, ids):
    rows, width = c.shape
    return pl.pallas_call(
        middle_kernel,
        out_shape=[jax.ShapeDtypeStruct((8, rows), jnp.float32)] * 3
        + [jax.ShapeDtypeStruct((4 * rows, width), jnp.bfloat16)],
        in_specs=(VMEM, VMEM, VMEM, [VMEM] * len(h), [VMEM] * len(ch), *[VMEM] * len(ids)),
        out_specs=[VMEM] * 4,
        compiler_params=LIMIT,
        name="middle",
    )(best, own, c, h, ch, *ids)


def late_kernel(far_ref, xe_refs, ids_ref, c_ids_ref, e_ids_ref, h_ids_ref, out_ref):
    xe = block(xe_refs)
    rows = xe.shape[0]
    others = [far_ref[place * rows : (place + 1) * rows] for place in range(4)]
    other_ids = [ids_ref[...], c_ids_ref[...], h_ids_ref[:1, :], h_ids_ref[1:, :]]
    out_ref[...] = jnp.broadcast_to(best_of(xe, e_ids_ref[1:, :], others, other_ids), out_ref.shape)


def late(far, xe, ids):
    return pl.pallas_call(
        late_kernel,
        out_shape=jax.ShapeDtypeStruct((8, far.shape[0] // 4), jnp.float32),
        in_specs=(VMEM, [VMEM] * len(xe), *[VMEM] * len(ids)),
        out_specs=VMEM,
        compiler_params=LIMIT,
        name="late",
    )(far, xe, *ids)


def square(embeddings, assignment):
    def swap(flip, array):
        return lax.ppermute(array, AXES, [(i, i ^ flip) for i in range(16)])

    rows = embeddings.shape[0]
    mine, ids = embeddings, assignment.reshape(1, rows)
    c = swap(SUB, mine)
    e = swap(LOW, mine)
    x = swap(SHARD, mine)
    far, _ = lax.optimization_barrier((mine, c))
    h = swap(HIGH, far)
    x_ids, c_ids = swap(SHARD, ids), swap(SUB, ids)
    e_ids = swap(LOW, jnp.concatenate([ids, x_ids]))
    h_ids = swap(HIGH, jnp.concatenate([ids, c_ids]))
    xe = swap(SHARD, e)
    h_then, _, _, _ = lax.optimization_barrier((h, h_ids, e_ids, x))
    ch = [swap(SUB, h_then[: rows // 2]), swap(SUB, h_then[rows // 2 :])]
    x, e, h, c, xe = [x], [e], [h], [c], [xe]
    best, own, c = early(mine, x, e, c, [ids, x_ids, c_ids, e_ids])
    found, x_best, e_best, far = middle(best, own, c, h, ch, [ids, x_ids, c_ids, e_ids, h_ids])
    x_best, e_best = swap(SHARD, x_best), swap(LOW, e_best)
    xe_best = swap(LOW | SHARD, late(far, xe, [ids, c_ids, e_ids, h_ids]))
    return jnp.maximum(jnp.maximum(found, x_best), jnp.maximum(e_best, xe_best))[0]


def shared_owner(embeddings, assignment):
    route, gather = AXES[:1], AXES[1:]
    owners = lax.axis_size(route)
    flip = jnp.zeros((1, 1), jnp.int32)
    (sent,) = pack(flip, embeddings, assignment, 1)
    got = lax.all_to_all(sent, route, split_axis=0, concat_axis=0, tiled=True)
    others = lax.all_gather(got, gather, axis=0, tiled=True)
    first = (lax.axis_index(gather) * SLOTS).astype(jnp.int32).reshape(1, 1)
    best = shared_best_of(got, others, first, owners)
    returned = lax.all_to_all(best, route, split_axis=0, concat_axis=0, tiled=True)
    return unpack(flip, [returned[i] for i in range(owners)], assignment)


def solution(mesh):
    placed = (
        P(("groups", "blk", "shard", "sub"), None),
        P(("groups", "blk", "shard", "sub"), None),
    )
    four_bits = [mesh.shape[axis] for axis in AXES] == [4, 2, 2]
    program = square if four_bits else shared_owner
    return jax.shard_map(
        program,
        mesh=mesh,
        in_specs=placed,
        out_specs=P(("groups", "blk", "shard", "sub")),
        check_vma=False,
    )
```

```python
import functools
import math

import jax
import jax.numpy as jnp
from jax import lax
from jax.experimental import pallas as pl
from jax.experimental.pallas import tpu as pltpu
from jax.sharding import PartitionSpec as P

CLUSTERS = 16
CAP = 16
SLOTS = CLUSTERS * CAP
LANES = 128
EMPTY = 4.0
NONE = -2.0
TAIL = 8
HIGH, LOW, SHARD, SUB = 8, 4, 2, 1
LIMIT = pltpu.CompilerParams(vmem_limit_bytes=12 << 20)
AXES = ("blk", "shard", "sub")

VMEM = pl.BlockSpec(memory_space=pltpu.VMEM)
SMEM = pl.BlockSpec(memory_space=pltpu.SMEM)


def placement(cluster, flip):
    rows = cluster.shape[1]
    label = lax.broadcasted_iota(jnp.int32, (CLUSTERS, rows), 0)
    member = (cluster == label).astype(jnp.float32)
    before = lax.broadcasted_iota(jnp.int32, (rows, rows), 0) < lax.broadcasted_iota(
        jnp.int32, (rows, rows), 1
    )
    earlier = jnp.dot(
        member.astype(jnp.bfloat16),
        before.astype(jnp.float32).astype(jnp.bfloat16),
        preferred_element_type=jnp.float32,
    )
    within = jnp.sum(earlier * member, axis=0, keepdims=True).astype(jnp.int32)
    target = (cluster ^ flip) * CAP + within
    return lax.broadcasted_iota(jnp.int32, (SLOTS, rows), 0) == target


def pack_kernel(flip_ref, rows_ref, cluster_ref, *out_refs):
    values = rows_ref[...].astype(jnp.float32)
    width = values.shape[1]
    scaled = values * lax.rsqrt(jnp.mean(values * values, axis=1, keepdims=True) + 1e-06)
    unit = (scaled * (1.0 / math.sqrt(width))).astype(jnp.bfloat16)
    placed = placement(cluster_ref[...], flip_ref[0, 0]).astype(jnp.float32)
    slots = jnp.dot(placed.astype(jnp.bfloat16), unit, preferred_element_type=jnp.float32)
    used = jnp.sum(placed, axis=1, keepdims=True)
    first = lax.broadcasted_iota(jnp.int32, slots.shape, 1) == 0
    slots = jnp.where(first & (used < 0.5), EMPTY, slots).astype(jnp.bfloat16)
    count = SLOTS // len(out_refs)
    for block, out_ref in enumerate(out_refs):
        out_ref[...] = slots[block * count : (block + 1) * count]


def pack(flip, embeddings, assignment, blocks):
    rows, width = embeddings.shape
    return pl.pallas_call(
        pack_kernel,
        out_shape=[jax.ShapeDtypeStruct((SLOTS // blocks, width), jnp.bfloat16)] * blocks,
        in_specs=[SMEM, VMEM, VMEM],
        out_specs=[VMEM] * blocks,
        name="pack",
    )(flip, embeddings, assignment.reshape(1, rows))


def shared_best_kernel(count, first_ref, slots_ref, others_ref, out_ref, best_ref):
    step = pl.program_id(0)
    slots, others = slots_ref[...], others_ref[...]
    similar = lax.dot_general(
        others, slots, (((1,), (1,)), ((), ())), preferred_element_type=jnp.float32
    )
    used = others[:, :1].astype(jnp.float32) < 2.0
    row = lax.broadcasted_iota(jnp.int32, similar.shape, 0)
    column = lax.broadcasted_iota(jnp.int32, similar.shape, 1)
    kept = used & (row + step * slots.shape[0] != column + first_ref[0, 0])
    kept = kept & (row % count // CAP == column % count // CAP)
    best = jnp.max(jnp.where(kept, similar, NONE), axis=0, keepdims=True)

    @pl.when(step == 0)
    def _():
        best_ref[...] = best

    @pl.when(step > 0)
    def _():
        best_ref[...] = jnp.maximum(best_ref[...], best)

    @pl.when(step == pl.num_programs(0) - 1)
    def _():
        for source in range(out_ref.shape[0]):
            piece = best_ref[:, source * count : (source + 1) * count]
            out_ref[source, :, :count] = jnp.broadcast_to(piece, (8, count))
            if count < LANES:
                out_ref[source, :, count:] = jnp.full((8, LANES - count), NONE)


def shared_best_of(slots, others, first, owners):
    size, width = slots.shape
    return pl.pallas_call(
        functools.partial(shared_best_kernel, size // owners),
        grid=(others.shape[0] // size,),
        out_shape=jax.ShapeDtypeStruct((owners, 8, LANES), jnp.float32),
        in_specs=[
            pl.BlockSpec((1, 1), lambda i: (0, 0), memory_space=pltpu.SMEM),
            pl.BlockSpec((size, width), lambda i: (0, 0)),
            pl.BlockSpec((size, width), lambda i: (i, 0)),
        ],
        out_specs=pl.BlockSpec((owners, 8, LANES), lambda i: (0, 0, 0)),
        scratch_shapes=[pltpu.VMEM((1, size), jnp.float32)],
        name="shared_best",
    )(first, slots, others)


def unpack_kernel(flip_ref, cluster_ref, *refs):
    returned_refs, out_ref = refs[:-1], refs[-1]
    count = SLOTS // len(returned_refs)
    placed = placement(cluster_ref[...], flip_ref[0, 0])
    returned = jnp.concatenate(
        [jnp.broadcast_to(ref[:1, :], (count, LANES)) for ref in returned_refs], axis=0
    )
    slot = lax.broadcasted_iota(jnp.int32, (SLOTS, LANES), 0) % count
    lane = lax.broadcasted_iota(jnp.int32, (SLOTS, LANES), 1)
    by_slot = jnp.max(jnp.where(slot == lane, returned, NONE), axis=1, keepdims=True)
    out_ref[...] = jnp.max(jnp.where(placed, by_slot, NONE), axis=0, keepdims=True)


def unpack(flip, returned, assignment):
    rows = assignment.shape[0]
    return pl.pallas_call(
        unpack_kernel,
        out_shape=jax.ShapeDtypeStruct((1, rows), jnp.float32),
        in_specs=[SMEM, VMEM] + [VMEM] * len(returned),
        out_specs=VMEM,
        name="unpack",
    )(flip, assignment.reshape(1, rows), *returned).reshape(-1)


def unit_of(values):
    values = values.astype(jnp.float32)
    scaled = values * lax.rsqrt(jnp.mean(values * values, axis=1, keepdims=True) + 1e-06)
    return (scaled * (1.0 / math.sqrt(values.shape[1]))).astype(jnp.bfloat16)


def best_of(own, own_clusters, others, other_clusters, same_rows=False):
    best = None
    for place, (rows, clusters) in enumerate(zip(others, other_clusters)):
        count = rows.shape[0]
        similar = lax.dot_general(
            rows, own, (((1,), (1,)), ((), ())), preferred_element_type=jnp.float32
        )
        down = jnp.broadcast_to(clusters, (count, count)).T[:, :1]
        kept = down == own_clusters
        if same_rows and place == 0:
            row = lax.broadcasted_iota(jnp.int32, similar.shape, 0)
            column = lax.broadcasted_iota(jnp.int32, similar.shape, 1)
            kept = kept & (row != column)
        found = jnp.max(jnp.where(kept, similar, NONE), axis=0, keepdims=True)
        best = found if best is None else jnp.maximum(best, found)
    return best


def block(refs):
    return jnp.concatenate([unit_of(ref[...]) for ref in refs], axis=0)


def labelled(refs):
    last = refs[-1][...]
    pieces = [ref[...] for ref in refs[:-1]] + [last[: last.shape[0] - TAIL]]
    rows = jnp.concatenate([unit_of(piece) for piece in pieces], axis=0)
    return rows, last[last.shape[0] - TAIL :, : rows.shape[0]].astype(jnp.float32)[:1].astype(jnp.int32)


def early_kernel(mine_ref, x_refs, e_refs, c_refs, ids_ref, x_ids_ref, c_ids_ref, e_ids_ref, best_ref, own_ref, c_ref):
    mine, c = unit_of(mine_ref[...]), block(c_refs)
    own = jnp.concatenate([mine, block(x_refs), block(e_refs)], axis=0)
    own_ids = jnp.concatenate([ids_ref[...], x_ids_ref[...], e_ids_ref[:1, :]], axis=1)
    best = best_of(own, own_ids, [mine, c], [ids_ref[...], c_ids_ref[...]], True)
    best_ref[...] = jnp.broadcast_to(best, best_ref.shape)
    own_ref[...] = own
    c_ref[...] = c


def early(mine, x, e, c, ids):
    rows, width = mine.shape
    return pl.pallas_call(
        early_kernel,
        out_shape=[
            jax.ShapeDtypeStruct((8, 3 * rows), jnp.float32),
            jax.ShapeDtypeStruct((3 * rows, width), jnp.bfloat16),
            jax.ShapeDtypeStruct((rows, width), jnp.bfloat16),
        ],
        in_specs=(VMEM, [VMEM] * len(x), [VMEM] * len(e), [VMEM] * len(c), *[VMEM] * len(ids)),
        out_specs=[VMEM] * 3,
        compiler_params=LIMIT,
        name="early",
    )(mine, x, e, c, *ids)


def label_kernel(rows_ref, ids_ref, out_ref):
    rows, width = rows_ref.shape
    out_ref[:rows] = rows_ref[...]
    ids = jnp.broadcast_to(ids_ref[...].astype(jnp.float32), (TAIL, rows))
    tail = jnp.concatenate([ids, jnp.zeros((TAIL, width - rows), jnp.float32)], axis=1)
    out_ref[rows:] = tail.astype(jnp.bfloat16)


def label(rows, ids):
    return pl.pallas_call(
        label_kernel,
        out_shape=jax.ShapeDtypeStruct((rows.shape[0] + TAIL, rows.shape[1]), rows.dtype),
        in_specs=[VMEM, VMEM],
        out_specs=VMEM,
        compiler_params=LIMIT,
        name="label",
    )(rows, ids)


def middle_kernel(
    best_ref, own_ref, c_ref, h_refs, ch_refs, ids_ref, x_ids_ref, e_ids_ref,
    mine_out_ref, x_out_ref, e_out_ref, far_ref, far_ids_ref,
):
    (h, h_ids), (ch, ch_ids) = labelled(h_refs), labelled(ch_refs)
    own_ids = jnp.concatenate([ids_ref[...], x_ids_ref[...], e_ids_ref[:1, :]], axis=1)
    best = best_of(own_ref[...], own_ids, [h, ch], [h_ids, ch_ids])
    best = jnp.maximum(best, best_ref[:1, :])
    rows = c_ref.shape[0]
    for place, out_ref in enumerate((mine_out_ref, x_out_ref, e_out_ref)):
        out_ref[...] = jnp.broadcast_to(best[:, place * rows : (place + 1) * rows], out_ref.shape)
    far_ref[...] = jnp.concatenate([own_ref[:rows], c_ref[...], h, ch], axis=0)
    far_ids_ref[...] = jnp.concatenate([h_ids, ch_ids], axis=0)


def middle(best, own, c, h, ch, ids):
    rows, width = c.shape
    return pl.pallas_call(
        middle_kernel,
        out_shape=[jax.ShapeDtypeStruct((8, rows), jnp.float32)] * 3
        + [jax.ShapeDtypeStruct((4 * rows, width), jnp.bfloat16), jax.ShapeDtypeStruct((2, rows), jnp.int32)],
        in_specs=(VMEM, VMEM, VMEM, [VMEM] * len(h), [VMEM] * len(ch), *[VMEM] * len(ids)),
        out_specs=[VMEM] * 5,
        compiler_params=LIMIT,
        name="middle",
    )(best, own, c, h, ch, *ids)


def late_kernel(far_ref, xe_refs, ids_ref, c_ids_ref, e_ids_ref, h_ids_ref, out_ref):
    xe = block(xe_refs)
    rows = xe.shape[0]
    others = [far_ref[place * rows : (place + 1) * rows] for place in range(4)]
    other_ids = [ids_ref[...], c_ids_ref[...], h_ids_ref[:1, :], h_ids_ref[1:, :]]
    out_ref[...] = jnp.broadcast_to(best_of(xe, e_ids_ref[1:, :], others, other_ids), out_ref.shape)


def late(far, xe, ids):
    return pl.pallas_call(
        late_kernel,
        out_shape=jax.ShapeDtypeStruct((8, far.shape[0] // 4), jnp.float32),
        in_specs=(VMEM, [VMEM] * len(xe), *[VMEM] * len(ids)),
        out_specs=VMEM,
        compiler_params=LIMIT,
        name="late",
    )(far, xe, *ids)


def square(embeddings, assignment):
    def swap(flip, array):
        return lax.ppermute(array, AXES, [(i, i ^ flip) for i in range(16)])

    rows = embeddings.shape[0]
    mine, ids = embeddings, assignment.reshape(1, rows)
    e = swap(LOW, mine)
    x = swap(SHARD, mine)
    c = swap(SUB, mine)
    h = swap(HIGH, label(mine, ids))
    x_ids, c_ids = swap(SHARD, ids), swap(SUB, ids)
    e_ids = swap(LOW, jnp.concatenate([ids, x_ids]))
    e_then, _, _ = lax.optimization_barrier((e, x, x_ids))
    xe = swap(SHARD, e_then)
    h_then, *_ = lax.optimization_barrier((h, e_ids, x, c_ids, c))
    ch = [swap(SUB, h_then[: rows // 2]), swap(SUB, h_then[rows // 2 :])]
    x, e, h, c, xe = [x], [e], [h], [c], [xe]
    best, own, c = early(mine, x, e, c, [ids, x_ids, c_ids, e_ids])
    found, x_best, e_best, far, h_ids = middle(best, own, c, h, ch, [ids, x_ids, e_ids])
    x_best, e_best = swap(SHARD, x_best), swap(LOW, e_best)
    xe_best = swap(LOW | SHARD, late(far, xe, [ids, c_ids, e_ids, h_ids]))
    return jnp.maximum(jnp.maximum(found, x_best), jnp.maximum(e_best, xe_best))[0]


def shared_owner(embeddings, assignment):
    route, gather = AXES[:1], AXES[1:]
    owners = lax.axis_size(route)
    flip = jnp.zeros((1, 1), jnp.int32)
    (sent,) = pack(flip, embeddings, assignment, 1)
    got = lax.all_to_all(sent, route, split_axis=0, concat_axis=0, tiled=True)
    others = lax.all_gather(got, gather, axis=0, tiled=True)
    first = (lax.axis_index(gather) * SLOTS).astype(jnp.int32).reshape(1, 1)
    best = shared_best_of(got, others, first, owners)
    returned = lax.all_to_all(best, route, split_axis=0, concat_axis=0, tiled=True)
    return unpack(flip, [returned[i] for i in range(owners)], assignment)


def solution(mesh):
    placed = (
        P(("groups", "blk", "shard", "sub"), None),
        P(("groups", "blk", "shard", "sub"), None),
    )
    four_bits = [mesh.shape[axis] for axis in AXES] == [4, 2, 2]
    program = square if four_bits else shared_owner
    return jax.shard_map(
        program,
        mesh=mesh,
        in_specs=placed,
        out_specs=P(("groups", "blk", "shard", "sub")),
        check_vma=False,
    )
```

```python
import functools
import math

import jax
import jax.numpy as jnp
from jax import lax
from jax.experimental import pallas as pl
from jax.experimental.pallas import tpu as pltpu
from jax.sharding import PartitionSpec as P

CLUSTERS = 16
CAP = 16
SLOTS = CLUSTERS * CAP
LANES = 128
EMPTY = 4.0
NONE = -2.0
TAIL = 8
HIGH, LOW, SHARD, SUB = 8, 4, 2, 1
LIMIT = pltpu.CompilerParams(vmem_limit_bytes=12 << 20)
AXES = ("blk", "shard", "sub")

VMEM = pl.BlockSpec(memory_space=pltpu.VMEM)
SMEM = pl.BlockSpec(memory_space=pltpu.SMEM)


def placement(cluster, flip):
    rows = cluster.shape[1]
    label = lax.broadcasted_iota(jnp.int32, (CLUSTERS, rows), 0)
    member = (cluster == label).astype(jnp.float32)
    before = lax.broadcasted_iota(jnp.int32, (rows, rows), 0) < lax.broadcasted_iota(
        jnp.int32, (rows, rows), 1
    )
    earlier = jnp.dot(
        member.astype(jnp.bfloat16),
        before.astype(jnp.float32).astype(jnp.bfloat16),
        preferred_element_type=jnp.float32,
    )
    within = jnp.sum(earlier * member, axis=0, keepdims=True).astype(jnp.int32)
    target = (cluster ^ flip) * CAP + within
    return lax.broadcasted_iota(jnp.int32, (SLOTS, rows), 0) == target


def pack_kernel(flip_ref, rows_ref, cluster_ref, *out_refs):
    values = rows_ref[...].astype(jnp.float32)
    width = values.shape[1]
    scaled = values * lax.rsqrt(jnp.mean(values * values, axis=1, keepdims=True) + 1e-06)
    unit = (scaled * (1.0 / math.sqrt(width))).astype(jnp.bfloat16)
    placed = placement(cluster_ref[...], flip_ref[0, 0]).astype(jnp.float32)
    slots = jnp.dot(placed.astype(jnp.bfloat16), unit, preferred_element_type=jnp.float32)
    used = jnp.sum(placed, axis=1, keepdims=True)
    first = lax.broadcasted_iota(jnp.int32, slots.shape, 1) == 0
    slots = jnp.where(first & (used < 0.5), EMPTY, slots).astype(jnp.bfloat16)
    count = SLOTS // len(out_refs)
    for block, out_ref in enumerate(out_refs):
        out_ref[...] = slots[block * count : (block + 1) * count]


def pack(flip, embeddings, assignment, blocks):
    rows, width = embeddings.shape
    return pl.pallas_call(
        pack_kernel,
        out_shape=[jax.ShapeDtypeStruct((SLOTS // blocks, width), jnp.bfloat16)] * blocks,
        in_specs=[SMEM, VMEM, VMEM],
        out_specs=[VMEM] * blocks,
        name="pack",
    )(flip, embeddings, assignment.reshape(1, rows))


def shared_best_kernel(count, first_ref, slots_ref, others_ref, out_ref, best_ref):
    step = pl.program_id(0)
    slots, others = slots_ref[...], others_ref[...]
    similar = lax.dot_general(
        others, slots, (((1,), (1,)), ((), ())), preferred_element_type=jnp.float32
    )
    used = others[:, :1].astype(jnp.float32) < 2.0
    row = lax.broadcasted_iota(jnp.int32, similar.shape, 0)
    column = lax.broadcasted_iota(jnp.int32, similar.shape, 1)
    kept = used & (row + step * slots.shape[0] != column + first_ref[0, 0])
    kept = kept & (row % count // CAP == column % count // CAP)
    best = jnp.max(jnp.where(kept, similar, NONE), axis=0, keepdims=True)

    @pl.when(step == 0)
    def _():
        best_ref[...] = best

    @pl.when(step > 0)
    def _():
        best_ref[...] = jnp.maximum(best_ref[...], best)

    @pl.when(step == pl.num_programs(0) - 1)
    def _():
        for source in range(out_ref.shape[0]):
            piece = best_ref[:, source * count : (source + 1) * count]
            out_ref[source, :, :count] = jnp.broadcast_to(piece, (8, count))
            if count < LANES:
                out_ref[source, :, count:] = jnp.full((8, LANES - count), NONE)


def shared_best_of(slots, others, first, owners):
    size, width = slots.shape
    return pl.pallas_call(
        functools.partial(shared_best_kernel, size // owners),
        grid=(others.shape[0] // size,),
        out_shape=jax.ShapeDtypeStruct((owners, 8, LANES), jnp.float32),
        in_specs=[
            pl.BlockSpec((1, 1), lambda i: (0, 0), memory_space=pltpu.SMEM),
            pl.BlockSpec((size, width), lambda i: (0, 0)),
            pl.BlockSpec((size, width), lambda i: (i, 0)),
        ],
        out_specs=pl.BlockSpec((owners, 8, LANES), lambda i: (0, 0, 0)),
        scratch_shapes=[pltpu.VMEM((1, size), jnp.float32)],
        name="shared_best",
    )(first, slots, others)


def unpack_kernel(flip_ref, cluster_ref, *refs):
    returned_refs, out_ref = refs[:-1], refs[-1]
    count = SLOTS // len(returned_refs)
    placed = placement(cluster_ref[...], flip_ref[0, 0])
    returned = jnp.concatenate(
        [jnp.broadcast_to(ref[:1, :], (count, LANES)) for ref in returned_refs], axis=0
    )
    slot = lax.broadcasted_iota(jnp.int32, (SLOTS, LANES), 0) % count
    lane = lax.broadcasted_iota(jnp.int32, (SLOTS, LANES), 1)
    by_slot = jnp.max(jnp.where(slot == lane, returned, NONE), axis=1, keepdims=True)
    out_ref[...] = jnp.max(jnp.where(placed, by_slot, NONE), axis=0, keepdims=True)


def unpack(flip, returned, assignment):
    rows = assignment.shape[0]
    return pl.pallas_call(
        unpack_kernel,
        out_shape=jax.ShapeDtypeStruct((1, rows), jnp.float32),
        in_specs=[SMEM, VMEM] + [VMEM] * len(returned),
        out_specs=VMEM,
        name="unpack",
    )(flip, assignment.reshape(1, rows), *returned).reshape(-1)


def unit_of(values):
    values = values.astype(jnp.float32)
    scaled = values * lax.rsqrt(jnp.mean(values * values, axis=1, keepdims=True) + 1e-06)
    return (scaled * (1.0 / math.sqrt(values.shape[1]))).astype(jnp.bfloat16)


def best_of(own, own_clusters, others, other_clusters, same_rows=False):
    best = None
    for place, (rows, clusters) in enumerate(zip(others, other_clusters)):
        count = rows.shape[0]
        similar = lax.dot_general(
            rows, own, (((1,), (1,)), ((), ())), preferred_element_type=jnp.float32
        )
        down = jnp.broadcast_to(clusters, (count, count)).T[:, :1]
        kept = down == own_clusters
        if same_rows and place == 0:
            row = lax.broadcasted_iota(jnp.int32, similar.shape, 0)
            column = lax.broadcasted_iota(jnp.int32, similar.shape, 1)
            kept = kept & (row != column)
        found = jnp.max(jnp.where(kept, similar, NONE), axis=0, keepdims=True)
        best = found if best is None else jnp.maximum(best, found)
    return best


def block(refs):
    return jnp.concatenate([unit_of(ref[...]) for ref in refs], axis=0)


def labelled(refs):
    last = refs[-1][...]
    pieces = [ref[...] for ref in refs[:-1]] + [last[: last.shape[0] - TAIL]]
    rows = jnp.concatenate([unit_of(piece) for piece in pieces], axis=0)
    return rows, last[last.shape[0] - TAIL :, : rows.shape[0]].astype(jnp.float32)[:1].astype(jnp.int32)


def early_kernel(mine_ref, x_refs, e_refs, c_refs, ids_ref, x_ids_ref, c_ids_ref, e_ids_ref, best_ref, own_ref, c_ref):
    mine, c = unit_of(mine_ref[...]), block(c_refs)
    own = jnp.concatenate([mine, block(x_refs), block(e_refs)], axis=0)
    own_ids = jnp.concatenate([ids_ref[...], x_ids_ref[...], e_ids_ref[:1, :]], axis=1)
    best = best_of(own, own_ids, [mine, c], [ids_ref[...], c_ids_ref[...]], True)
    best_ref[...] = jnp.broadcast_to(best, best_ref.shape)
    own_ref[...] = own
    c_ref[...] = c


def early(mine, x, e, c, ids):
    rows, width = mine.shape
    return pl.pallas_call(
        early_kernel,
        out_shape=[
            jax.ShapeDtypeStruct((8, 3 * rows), jnp.float32),
            jax.ShapeDtypeStruct((3 * rows, width), jnp.bfloat16),
            jax.ShapeDtypeStruct((rows, width), jnp.bfloat16),
        ],
        in_specs=(VMEM, [VMEM] * len(x), [VMEM] * len(e), [VMEM] * len(c), *[VMEM] * len(ids)),
        out_specs=[VMEM] * 3,
        compiler_params=LIMIT,
        name="early",
    )(mine, x, e, c, *ids)


def label_kernel(rows_ref, ids_ref, out_ref):
    rows, width = rows_ref.shape
    out_ref[:rows] = rows_ref[...]
    ids = jnp.broadcast_to(ids_ref[...].astype(jnp.float32), (TAIL, rows))
    tail = jnp.concatenate([ids, jnp.zeros((TAIL, width - rows), jnp.float32)], axis=1)
    out_ref[rows:] = tail.astype(jnp.bfloat16)


def label(rows, ids):
    return pl.pallas_call(
        label_kernel,
        out_shape=jax.ShapeDtypeStruct((rows.shape[0] + TAIL, rows.shape[1]), rows.dtype),
        in_specs=[VMEM, VMEM],
        out_specs=VMEM,
        compiler_params=LIMIT,
        name="label",
    )(rows, ids)


def middle_kernel(
    best_ref, own_ref, c_ref, h_refs, ch_refs, ids_ref, x_ids_ref, e_ids_ref,
    mine_out_ref, x_out_ref, e_out_ref, far_ref, far_ids_ref,
):
    (h, h_ids), (ch, ch_ids) = labelled(h_refs), labelled(ch_refs)
    own_ids = jnp.concatenate([ids_ref[...], x_ids_ref[...], e_ids_ref[:1, :]], axis=1)
    best = best_of(own_ref[...], own_ids, [h, ch], [h_ids, ch_ids])
    best = jnp.maximum(best, best_ref[:1, :])
    rows = c_ref.shape[0]
    for place, out_ref in enumerate((mine_out_ref, x_out_ref, e_out_ref)):
        out_ref[...] = jnp.broadcast_to(best[:, place * rows : (place + 1) * rows], out_ref.shape)
    far_ref[...] = jnp.concatenate([own_ref[:rows], c_ref[...], h, ch], axis=0)
    far_ids_ref[...] = jnp.concatenate([h_ids, ch_ids], axis=0)


def middle(best, own, c, h, ch, ids):
    rows, width = c.shape
    return pl.pallas_call(
        middle_kernel,
        out_shape=[jax.ShapeDtypeStruct((8, rows), jnp.float32)] * 3
        + [jax.ShapeDtypeStruct((4 * rows, width), jnp.bfloat16), jax.ShapeDtypeStruct((2, rows), jnp.int32)],
        in_specs=(VMEM, VMEM, VMEM, [VMEM] * len(h), [VMEM] * len(ch), *[VMEM] * len(ids)),
        out_specs=[VMEM] * 5,
        compiler_params=LIMIT,
        name="middle",
    )(best, own, c, h, ch, *ids)


def late_kernel(far_ref, xe_refs, ids_ref, c_ids_ref, e_ids_ref, h_ids_ref, out_ref):
    xe = block(xe_refs)
    rows = xe.shape[0]
    others = [far_ref[place * rows : (place + 1) * rows] for place in range(4)]
    other_ids = [ids_ref[...], c_ids_ref[...], h_ids_ref[:1, :], h_ids_ref[1:, :]]
    out_ref[...] = jnp.broadcast_to(best_of(xe, e_ids_ref[1:, :], others, other_ids), out_ref.shape)


def late(far, xe, ids):
    return pl.pallas_call(
        late_kernel,
        out_shape=jax.ShapeDtypeStruct((8, far.shape[0] // 4), jnp.float32),
        in_specs=(VMEM, [VMEM] * len(xe), *[VMEM] * len(ids)),
        out_specs=VMEM,
        compiler_params=LIMIT,
        name="late",
    )(far, xe, *ids)


def square(embeddings, assignment):
    def swap(flip, array):
        return lax.ppermute(array, AXES, [(i, i ^ flip) for i in range(16)])

    rows = embeddings.shape[0]
    mine, ids = embeddings, assignment.reshape(1, rows)
    e = swap(LOW, mine)
    x = swap(SHARD, mine)
    c = swap(SUB, mine)
    h = swap(HIGH, label(mine, ids))
    x_ids, c_ids = swap(SHARD, ids), swap(SUB, ids)
    e_ids = swap(LOW, jnp.concatenate([ids, x_ids]))
    e_then, _, _ = lax.optimization_barrier((e, x, x_ids))
    xe = swap(SHARD, e_then)
    h_then, *_ = lax.optimization_barrier((h, e_ids, x, c_ids, c))
    ch = [swap(SUB, h_then[: rows // 2]), swap(SUB, h_then[rows // 2 :])]
    x, e, h, c, xe = [x], [e], [h], [c], [xe]
    best, own, c = early(mine, x, e, c, [ids, x_ids, c_ids, e_ids])
    found, x_best, e_best, far, h_ids = middle(best, own, c, h, ch, [ids, x_ids, e_ids])
    xe_best = late(far, xe, [ids, c_ids, e_ids, h_ids])
    x_best, e_best, xe_best = lax.optimization_barrier((x_best, e_best, xe_best))
    xe_best, e_best, x_best = swap(LOW | SHARD, xe_best), swap(LOW, e_best), swap(SHARD, x_best)
    return jnp.maximum(jnp.maximum(jnp.maximum(xe_best, e_best), x_best), found)[0]


def shared_owner(embeddings, assignment):
    route, gather = AXES[:1], AXES[1:]
    owners = lax.axis_size(route)
    flip = jnp.zeros((1, 1), jnp.int32)
    (sent,) = pack(flip, embeddings, assignment, 1)
    got = lax.all_to_all(sent, route, split_axis=0, concat_axis=0, tiled=True)
    others = lax.all_gather(got, gather, axis=0, tiled=True)
    first = (lax.axis_index(gather) * SLOTS).astype(jnp.int32).reshape(1, 1)
    best = shared_best_of(got, others, first, owners)
    returned = lax.all_to_all(best, route, split_axis=0, concat_axis=0, tiled=True)
    return unpack(flip, [returned[i] for i in range(owners)], assignment)


def solution(mesh):
    placed = (
        P(("groups", "blk", "shard", "sub"), None),
        P(("groups", "blk", "shard", "sub"), None),
    )
    four_bits = [mesh.shape[axis] for axis in AXES] == [4, 2, 2]
    program = square if four_bits else shared_owner
    return jax.shard_map(
        program,
        mesh=mesh,
        in_specs=placed,
        out_specs=P(("groups", "blk", "shard", "sub")),
        check_vma=False,
    )
```

```python
import functools
import math

import jax
import jax.numpy as jnp
from jax import lax
from jax.experimental import pallas as pl
from jax.experimental.pallas import tpu as pltpu
from jax.sharding import PartitionSpec as P

CLUSTERS = 16
CAP = 16
SLOTS = CLUSTERS * CAP
LANES = 128
EMPTY = 4.0
NONE = -2.0
TAIL = 8
HIGH, LOW, SHARD, SUB = 8, 4, 2, 1
LIMIT = pltpu.CompilerParams(vmem_limit_bytes=12 << 20)
AXES = ("blk", "shard", "sub")

VMEM = pl.BlockSpec(memory_space=pltpu.VMEM)
SMEM = pl.BlockSpec(memory_space=pltpu.SMEM)


def placement(cluster, flip):
    rows = cluster.shape[1]
    label = lax.broadcasted_iota(jnp.int32, (CLUSTERS, rows), 0)
    member = (cluster == label).astype(jnp.float32)
    before = lax.broadcasted_iota(jnp.int32, (rows, rows), 0) < lax.broadcasted_iota(
        jnp.int32, (rows, rows), 1
    )
    earlier = jnp.dot(
        member.astype(jnp.bfloat16),
        before.astype(jnp.float32).astype(jnp.bfloat16),
        preferred_element_type=jnp.float32,
    )
    within = jnp.sum(earlier * member, axis=0, keepdims=True).astype(jnp.int32)
    target = (cluster ^ flip) * CAP + within
    return lax.broadcasted_iota(jnp.int32, (SLOTS, rows), 0) == target


def pack_kernel(flip_ref, rows_ref, cluster_ref, *out_refs):
    values = rows_ref[...].astype(jnp.float32)
    width = values.shape[1]
    scaled = values * lax.rsqrt(jnp.mean(values * values, axis=1, keepdims=True) + 1e-06)
    unit = (scaled * (1.0 / math.sqrt(width))).astype(jnp.bfloat16)
    placed = placement(cluster_ref[...], flip_ref[0, 0]).astype(jnp.float32)
    slots = jnp.dot(placed.astype(jnp.bfloat16), unit, preferred_element_type=jnp.float32)
    used = jnp.sum(placed, axis=1, keepdims=True)
    first = lax.broadcasted_iota(jnp.int32, slots.shape, 1) == 0
    slots = jnp.where(first & (used < 0.5), EMPTY, slots).astype(jnp.bfloat16)
    count = SLOTS // len(out_refs)
    for block, out_ref in enumerate(out_refs):
        out_ref[...] = slots[block * count : (block + 1) * count]


def pack(flip, embeddings, assignment, blocks):
    rows, width = embeddings.shape
    return pl.pallas_call(
        pack_kernel,
        out_shape=[jax.ShapeDtypeStruct((SLOTS // blocks, width), jnp.bfloat16)] * blocks,
        in_specs=[SMEM, VMEM, VMEM],
        out_specs=[VMEM] * blocks,
        name="pack",
    )(flip, embeddings, assignment.reshape(1, rows))


def shared_best_kernel(count, first_ref, slots_ref, others_ref, out_ref, best_ref):
    step = pl.program_id(0)
    slots, others = slots_ref[...], others_ref[...]
    similar = lax.dot_general(
        others, slots, (((1,), (1,)), ((), ())), preferred_element_type=jnp.float32
    )
    used = others[:, :1].astype(jnp.float32) < 2.0
    row = lax.broadcasted_iota(jnp.int32, similar.shape, 0)
    column = lax.broadcasted_iota(jnp.int32, similar.shape, 1)
    kept = used & (row + step * slots.shape[0] != column + first_ref[0, 0])
    kept = kept & (row % count // CAP == column % count // CAP)
    best = jnp.max(jnp.where(kept, similar, NONE), axis=0, keepdims=True)

    @pl.when(step == 0)
    def _():
        best_ref[...] = best

    @pl.when(step > 0)
    def _():
        best_ref[...] = jnp.maximum(best_ref[...], best)

    @pl.when(step == pl.num_programs(0) - 1)
    def _():
        for source in range(out_ref.shape[0]):
            piece = best_ref[:, source * count : (source + 1) * count]
            out_ref[source, :, :count] = jnp.broadcast_to(piece, (8, count))
            if count < LANES:
                out_ref[source, :, count:] = jnp.full((8, LANES - count), NONE)


def shared_best_of(slots, others, first, owners):
    size, width = slots.shape
    return pl.pallas_call(
        functools.partial(shared_best_kernel, size // owners),
        grid=(others.shape[0] // size,),
        out_shape=jax.ShapeDtypeStruct((owners, 8, LANES), jnp.float32),
        in_specs=[
            pl.BlockSpec((1, 1), lambda i: (0, 0), memory_space=pltpu.SMEM),
            pl.BlockSpec((size, width), lambda i: (0, 0)),
            pl.BlockSpec((size, width), lambda i: (i, 0)),
        ],
        out_specs=pl.BlockSpec((owners, 8, LANES), lambda i: (0, 0, 0)),
        scratch_shapes=[pltpu.VMEM((1, size), jnp.float32)],
        name="shared_best",
    )(first, slots, others)


def unpack_kernel(flip_ref, cluster_ref, *refs):
    returned_refs, out_ref = refs[:-1], refs[-1]
    count = SLOTS // len(returned_refs)
    placed = placement(cluster_ref[...], flip_ref[0, 0])
    returned = jnp.concatenate(
        [jnp.broadcast_to(ref[:1, :], (count, LANES)) for ref in returned_refs], axis=0
    )
    slot = lax.broadcasted_iota(jnp.int32, (SLOTS, LANES), 0) % count
    lane = lax.broadcasted_iota(jnp.int32, (SLOTS, LANES), 1)
    by_slot = jnp.max(jnp.where(slot == lane, returned, NONE), axis=1, keepdims=True)
    out_ref[...] = jnp.max(jnp.where(placed, by_slot, NONE), axis=0, keepdims=True)


def unpack(flip, returned, assignment):
    rows = assignment.shape[0]
    return pl.pallas_call(
        unpack_kernel,
        out_shape=jax.ShapeDtypeStruct((1, rows), jnp.float32),
        in_specs=[SMEM, VMEM] + [VMEM] * len(returned),
        out_specs=VMEM,
        name="unpack",
    )(flip, assignment.reshape(1, rows), *returned).reshape(-1)


def unit_of(values):
    values = values.astype(jnp.float32)
    scaled = values * lax.rsqrt(jnp.mean(values * values, axis=1, keepdims=True) + 1e-06)
    return (scaled * (1.0 / math.sqrt(values.shape[1]))).astype(jnp.bfloat16)


def best_of(own, own_clusters, others, other_clusters, same_rows=False):
    best = None
    for place, (rows, clusters) in enumerate(zip(others, other_clusters)):
        count = rows.shape[0]
        similar = lax.dot_general(
            rows, own, (((1,), (1,)), ((), ())), preferred_element_type=jnp.float32
        )
        down = jnp.broadcast_to(clusters, (count, count)).T[:, :1]
        kept = down == own_clusters
        if same_rows and place == 0:
            row = lax.broadcasted_iota(jnp.int32, similar.shape, 0)
            column = lax.broadcasted_iota(jnp.int32, similar.shape, 1)
            kept = kept & (row != column)
        found = jnp.max(jnp.where(kept, similar, NONE), axis=0, keepdims=True)
        best = found if best is None else jnp.maximum(best, found)
    return best


def block(refs):
    return jnp.concatenate([unit_of(ref[...]) for ref in refs], axis=0)


def labelled(refs):
    last = refs[-1][...]
    pieces = [ref[...] for ref in refs[:-1]] + [last[: last.shape[0] - TAIL]]
    rows = jnp.concatenate([unit_of(piece) for piece in pieces], axis=0)
    return rows, last[last.shape[0] - TAIL :, : rows.shape[0]].astype(jnp.float32)[:1].astype(jnp.int32)


def early_kernel(mine_ref, x_refs, e_refs, c_refs, ids_ref, x_ids_ref, c_ids_ref, e_ids_ref, best_ref, own_ref, c_ref):
    mine, c = unit_of(mine_ref[...]), block(c_refs)
    own = jnp.concatenate([mine, block(x_refs), block(e_refs)], axis=0)
    own_ids = jnp.concatenate([ids_ref[...], x_ids_ref[...], e_ids_ref[:1, :]], axis=1)
    best = best_of(own, own_ids, [mine, c], [ids_ref[...], c_ids_ref[...]], True)
    best_ref[...] = jnp.broadcast_to(best, best_ref.shape)
    own_ref[...] = own
    c_ref[...] = c


def early(mine, x, e, c, ids):
    rows, width = mine.shape
    return pl.pallas_call(
        early_kernel,
        out_shape=[
            jax.ShapeDtypeStruct((8, 3 * rows), jnp.float32),
            jax.ShapeDtypeStruct((3 * rows, width), jnp.bfloat16),
            jax.ShapeDtypeStruct((rows, width), jnp.bfloat16),
        ],
        in_specs=(VMEM, [VMEM] * len(x), [VMEM] * len(e), [VMEM] * len(c), *[VMEM] * len(ids)),
        out_specs=[VMEM] * 3,
        compiler_params=LIMIT,
        name="early",
    )(mine, x, e, c, *ids)


def label_kernel(rows_ref, ids_ref, out_ref):
    rows, width = rows_ref.shape
    out_ref[:rows] = rows_ref[...]
    ids = jnp.broadcast_to(ids_ref[...].astype(jnp.float32), (TAIL, rows))
    tail = jnp.concatenate([ids, jnp.zeros((TAIL, width - rows), jnp.float32)], axis=1)
    out_ref[rows:] = tail.astype(jnp.bfloat16)


def label(rows, ids):
    return pl.pallas_call(
        label_kernel,
        out_shape=jax.ShapeDtypeStruct((rows.shape[0] + TAIL, rows.shape[1]), rows.dtype),
        in_specs=[VMEM, VMEM],
        out_specs=VMEM,
        compiler_params=LIMIT,
        name="label",
    )(rows, ids)


def middle_kernel(
    best_ref, own_ref, c_ref, h_refs, ch_refs, ids_ref, x_ids_ref, e_ids_ref,
    mine_out_ref, x_out_ref, e_out_ref, far_ref, far_ids_ref,
):
    (h, h_ids), (ch, ch_ids) = labelled(h_refs), labelled(ch_refs)
    own_ids = jnp.concatenate([ids_ref[...], x_ids_ref[...], e_ids_ref[:1, :]], axis=1)
    best = best_of(own_ref[...], own_ids, [h, ch], [h_ids, ch_ids])
    best = jnp.maximum(best, best_ref[:1, :])
    rows = c_ref.shape[0]
    for place, out_ref in enumerate((mine_out_ref, x_out_ref, e_out_ref)):
        out_ref[...] = jnp.broadcast_to(best[:, place * rows : (place + 1) * rows], out_ref.shape)
    far_ref[...] = jnp.concatenate([own_ref[:rows], c_ref[...], h, ch], axis=0)
    far_ids_ref[...] = jnp.concatenate([h_ids, ch_ids], axis=0)


def middle(best, own, c, h, ch, ids):
    rows, width = c.shape
    return pl.pallas_call(
        middle_kernel,
        out_shape=[jax.ShapeDtypeStruct((8, rows), jnp.float32)] * 3
        + [jax.ShapeDtypeStruct((4 * rows, width), jnp.bfloat16), jax.ShapeDtypeStruct((2, rows), jnp.int32)],
        in_specs=(VMEM, VMEM, VMEM, [VMEM] * len(h), [VMEM] * len(ch), *[VMEM] * len(ids)),
        out_specs=[VMEM] * 5,
        compiler_params=LIMIT,
        name="middle",
    )(best, own, c, h, ch, *ids)


def late_kernel(far_ref, xe_refs, ids_ref, c_ids_ref, e_ids_ref, h_ids_ref, out_ref):
    xe = block(xe_refs)
    rows = xe.shape[0]
    others = [far_ref[place * rows : (place + 1) * rows] for place in range(4)]
    other_ids = [ids_ref[...], c_ids_ref[...], h_ids_ref[:1, :], h_ids_ref[1:, :]]
    out_ref[...] = jnp.broadcast_to(best_of(xe, e_ids_ref[1:, :], others, other_ids), out_ref.shape)


def late(far, xe, ids):
    return pl.pallas_call(
        late_kernel,
        out_shape=jax.ShapeDtypeStruct((8, far.shape[0] // 4), jnp.float32),
        in_specs=(VMEM, [VMEM] * len(xe), *[VMEM] * len(ids)),
        out_specs=VMEM,
        compiler_params=LIMIT,
        name="late",
    )(far, xe, *ids)


def square(embeddings, assignment):
    def swap(flip, array):
        return lax.ppermute(array, AXES, [(i, i ^ flip) for i in range(16)])

    rows = embeddings.shape[0]
    mine, ids = embeddings, assignment.reshape(1, rows)
    e = swap(LOW, mine)
    x = swap(SHARD, mine)
    c = swap(SUB, mine)
    h = swap(HIGH, label(mine, ids))
    x_ids, c_ids = swap(SHARD, ids), swap(SUB, ids)
    e_ids = swap(LOW, jnp.concatenate([ids, x_ids]))
    e_then, _, _ = lax.optimization_barrier((e, x, x_ids))
    xe = swap(SHARD, e_then)
    h_then, *_ = lax.optimization_barrier((h, e_ids, x, c_ids, c))
    ch = [swap(SUB, h_then[: rows // 2]), swap(SUB, h_then[rows // 2 :])]
    x, e, h, c, xe = [x], [e], [h], [c], [xe]
    best, own, c = early(mine, x, e, c, [ids, x_ids, c_ids, e_ids])
    found, x_best, e_best, far, h_ids = middle(best, own, c, h, ch, [ids, x_ids, e_ids])
    x_best = swap(SHARD, x_best)
    xe_best = late(far, xe, [ids, c_ids, e_ids, h_ids])
    e_best, xe_best = lax.optimization_barrier((e_best, xe_best))
    xe_best, e_best = swap(LOW | SHARD, xe_best), swap(LOW, e_best)
    return jnp.maximum(jnp.maximum(jnp.maximum(xe_best, e_best), x_best), found)[0]


def shared_owner(embeddings, assignment):
    route, gather = AXES[:1], AXES[1:]
    owners = lax.axis_size(route)
    flip = jnp.zeros((1, 1), jnp.int32)
    (sent,) = pack(flip, embeddings, assignment, 1)
    got = lax.all_to_all(sent, route, split_axis=0, concat_axis=0, tiled=True)
    others = lax.all_gather(got, gather, axis=0, tiled=True)
    first = (lax.axis_index(gather) * SLOTS).astype(jnp.int32).reshape(1, 1)
    best = shared_best_of(got, others, first, owners)
    returned = lax.all_to_all(best, route, split_axis=0, concat_axis=0, tiled=True)
    return unpack(flip, [returned[i] for i in range(owners)], assignment)


def solution(mesh):
    placed = (
        P(("groups", "blk", "shard", "sub"), None),
        P(("groups", "blk", "shard", "sub"), None),
    )
    four_bits = [mesh.shape[axis] for axis in AXES] == [4, 2, 2]
    program = square if four_bits else shared_owner
    return jax.shard_map(
        program,
        mesh=mesh,
        in_specs=placed,
        out_specs=P(("groups", "blk", "shard", "sub")),
        check_vma=False,
    )
```

```python
import functools
import math

import jax
import jax.numpy as jnp
from jax import lax
from jax.experimental import pallas as pl
from jax.experimental.pallas import tpu as pltpu
from jax.sharding import PartitionSpec as P

CLUSTERS = 16
CAP = 16
SLOTS = CLUSTERS * CAP
LANES = 128
EMPTY = 4.0
NONE = -2.0
TAIL = 8
HIGH, LOW, SHARD, SUB = 8, 4, 2, 1
LIMIT = pltpu.CompilerParams(vmem_limit_bytes=12 << 20)
AXES = ("blk", "shard", "sub")

VMEM = pl.BlockSpec(memory_space=pltpu.VMEM)
SMEM = pl.BlockSpec(memory_space=pltpu.SMEM)


def placement(cluster, flip):
    rows = cluster.shape[1]
    label = lax.broadcasted_iota(jnp.int32, (CLUSTERS, rows), 0)
    member = (cluster == label).astype(jnp.float32)
    before = lax.broadcasted_iota(jnp.int32, (rows, rows), 0) < lax.broadcasted_iota(
        jnp.int32, (rows, rows), 1
    )
    earlier = jnp.dot(
        member.astype(jnp.bfloat16),
        before.astype(jnp.float32).astype(jnp.bfloat16),
        preferred_element_type=jnp.float32,
    )
    within = jnp.sum(earlier * member, axis=0, keepdims=True).astype(jnp.int32)
    target = (cluster ^ flip) * CAP + within
    return lax.broadcasted_iota(jnp.int32, (SLOTS, rows), 0) == target


def pack_kernel(flip_ref, rows_ref, cluster_ref, *out_refs):
    values = rows_ref[...].astype(jnp.float32)
    width = values.shape[1]
    scaled = values * lax.rsqrt(jnp.mean(values * values, axis=1, keepdims=True) + 1e-06)
    unit = (scaled * (1.0 / math.sqrt(width))).astype(jnp.bfloat16)
    placed = placement(cluster_ref[...], flip_ref[0, 0]).astype(jnp.float32)
    slots = jnp.dot(placed.astype(jnp.bfloat16), unit, preferred_element_type=jnp.float32)
    used = jnp.sum(placed, axis=1, keepdims=True)
    first = lax.broadcasted_iota(jnp.int32, slots.shape, 1) == 0
    slots = jnp.where(first & (used < 0.5), EMPTY, slots).astype(jnp.bfloat16)
    count = SLOTS // len(out_refs)
    for block, out_ref in enumerate(out_refs):
        out_ref[...] = slots[block * count : (block + 1) * count]


def pack(flip, embeddings, assignment, blocks):
    rows, width = embeddings.shape
    return pl.pallas_call(
        pack_kernel,
        out_shape=[jax.ShapeDtypeStruct((SLOTS // blocks, width), jnp.bfloat16)] * blocks,
        in_specs=[SMEM, VMEM, VMEM],
        out_specs=[VMEM] * blocks,
        name="pack",
    )(flip, embeddings, assignment.reshape(1, rows))


def shared_best_kernel(count, first_ref, slots_ref, others_ref, out_ref, best_ref):
    step = pl.program_id(0)
    slots, others = slots_ref[...], others_ref[...]
    similar = lax.dot_general(
        others, slots, (((1,), (1,)), ((), ())), preferred_element_type=jnp.float32
    )
    used = others[:, :1].astype(jnp.float32) < 2.0
    row = lax.broadcasted_iota(jnp.int32, similar.shape, 0)
    column = lax.broadcasted_iota(jnp.int32, similar.shape, 1)
    kept = used & (row + step * slots.shape[0] != column + first_ref[0, 0])
    kept = kept & (row % count // CAP == column % count // CAP)
    best = jnp.max(jnp.where(kept, similar, NONE), axis=0, keepdims=True)

    @pl.when(step == 0)
    def _():
        best_ref[...] = best

    @pl.when(step > 0)
    def _():
        best_ref[...] = jnp.maximum(best_ref[...], best)

    @pl.when(step == pl.num_programs(0) - 1)
    def _():
        for source in range(out_ref.shape[0]):
            piece = best_ref[:, source * count : (source + 1) * count]
            out_ref[source, :, :count] = jnp.broadcast_to(piece, (8, count))
            if count < LANES:
                out_ref[source, :, count:] = jnp.full((8, LANES - count), NONE)


def shared_best_of(slots, others, first, owners):
    size, width = slots.shape
    return pl.pallas_call(
        functools.partial(shared_best_kernel, size // owners),
        grid=(others.shape[0] // size,),
        out_shape=jax.ShapeDtypeStruct((owners, 8, LANES), jnp.float32),
        in_specs=[
            pl.BlockSpec((1, 1), lambda i: (0, 0), memory_space=pltpu.SMEM),
            pl.BlockSpec((size, width), lambda i: (0, 0)),
            pl.BlockSpec((size, width), lambda i: (i, 0)),
        ],
        out_specs=pl.BlockSpec((owners, 8, LANES), lambda i: (0, 0, 0)),
        scratch_shapes=[pltpu.VMEM((1, size), jnp.float32)],
        name="shared_best",
    )(first, slots, others)


def unpack_kernel(flip_ref, cluster_ref, *refs):
    returned_refs, out_ref = refs[:-1], refs[-1]
    count = SLOTS // len(returned_refs)
    placed = placement(cluster_ref[...], flip_ref[0, 0])
    returned = jnp.concatenate(
        [jnp.broadcast_to(ref[:1, :], (count, LANES)) for ref in returned_refs], axis=0
    )
    slot = lax.broadcasted_iota(jnp.int32, (SLOTS, LANES), 0) % count
    lane = lax.broadcasted_iota(jnp.int32, (SLOTS, LANES), 1)
    by_slot = jnp.max(jnp.where(slot == lane, returned, NONE), axis=1, keepdims=True)
    out_ref[...] = jnp.max(jnp.where(placed, by_slot, NONE), axis=0, keepdims=True)


def unpack(flip, returned, assignment):
    rows = assignment.shape[0]
    return pl.pallas_call(
        unpack_kernel,
        out_shape=jax.ShapeDtypeStruct((1, rows), jnp.float32),
        in_specs=[SMEM, VMEM] + [VMEM] * len(returned),
        out_specs=VMEM,
        name="unpack",
    )(flip, assignment.reshape(1, rows), *returned).reshape(-1)


def unit_of(values):
    values = values.astype(jnp.float32)
    scaled = values * lax.rsqrt(jnp.mean(values * values, axis=1, keepdims=True) + 1e-06)
    return (scaled * (1.0 / math.sqrt(values.shape[1]))).astype(jnp.bfloat16)


def best_of(own, own_clusters, others, other_clusters, same_rows=False):
    best = None
    for place, (rows, clusters) in enumerate(zip(others, other_clusters)):
        count = rows.shape[0]
        similar = lax.dot_general(
            rows, own, (((1,), (1,)), ((), ())), preferred_element_type=jnp.float32
        )
        down = jnp.broadcast_to(clusters, (count, count)).T[:, :1]
        kept = down == own_clusters
        if same_rows and place == 0:
            row = lax.broadcasted_iota(jnp.int32, similar.shape, 0)
            column = lax.broadcasted_iota(jnp.int32, similar.shape, 1)
            kept = kept & (row != column)
        found = jnp.max(jnp.where(kept, similar, NONE), axis=0, keepdims=True)
        best = found if best is None else jnp.maximum(best, found)
    return best


def block(refs):
    return jnp.concatenate([unit_of(ref[...]) for ref in refs], axis=0)


def labelled(refs):
    last = refs[-1][...]
    pieces = [ref[...] for ref in refs[:-1]] + [last[: last.shape[0] - TAIL]]
    rows = jnp.concatenate([unit_of(piece) for piece in pieces], axis=0)
    return rows, last[last.shape[0] - TAIL :, : rows.shape[0]].astype(jnp.float32)[:1].astype(jnp.int32)


def early_kernel(mine_ref, x_refs, e_refs, c_refs, ids_ref, x_ids_ref, c_ids_ref, e_ids_ref, best_ref, own_ref, c_ref):
    mine, c = unit_of(mine_ref[...]), block(c_refs)
    own = jnp.concatenate([mine, block(x_refs), block(e_refs)], axis=0)
    own_ids = jnp.concatenate([ids_ref[...], x_ids_ref[...], e_ids_ref[:1, :]], axis=1)
    best = best_of(own, own_ids, [mine, c], [ids_ref[...], c_ids_ref[...]], True)
    best_ref[...] = jnp.broadcast_to(best, best_ref.shape)
    own_ref[...] = own
    c_ref[...] = c


def early(mine, x, e, c, ids):
    rows, width = mine.shape
    return pl.pallas_call(
        early_kernel,
        out_shape=[
            jax.ShapeDtypeStruct((8, 3 * rows), jnp.float32),
            jax.ShapeDtypeStruct((3 * rows, width), jnp.bfloat16),
            jax.ShapeDtypeStruct((rows, width), jnp.bfloat16),
        ],
        in_specs=(VMEM, [VMEM] * len(x), [VMEM] * len(e), [VMEM] * len(c), *[VMEM] * len(ids)),
        out_specs=[VMEM] * 3,
        compiler_params=LIMIT,
        name="early",
    )(mine, x, e, c, *ids)


def label_kernel(rows_ref, ids_ref, out_ref):
    rows, width = rows_ref.shape
    out_ref[:rows] = rows_ref[...]
    ids = jnp.broadcast_to(ids_ref[...].astype(jnp.float32), (TAIL, rows))
    tail = jnp.concatenate([ids, jnp.zeros((TAIL, width - rows), jnp.float32)], axis=1)
    out_ref[rows:] = tail.astype(jnp.bfloat16)


def label(rows, ids):
    return pl.pallas_call(
        label_kernel,
        out_shape=jax.ShapeDtypeStruct((rows.shape[0] + TAIL, rows.shape[1]), rows.dtype),
        in_specs=[VMEM, VMEM],
        out_specs=VMEM,
        compiler_params=LIMIT,
        name="label",
    )(rows, ids)


def middle_kernel(
    best_ref, own_ref, c_ref, h_refs, ch_refs, ids_ref, x_ids_ref, e_ids_ref,
    mine_out_ref, x_out_ref, e_out_ref, far_ref, far_ids_ref,
):
    (h, h_ids), (ch, ch_ids) = labelled(h_refs), labelled(ch_refs)
    own_ids = jnp.concatenate([ids_ref[...], x_ids_ref[...], e_ids_ref[:1, :]], axis=1)
    best = best_of(own_ref[...], own_ids, [h, ch], [h_ids, ch_ids])
    best = jnp.maximum(best, best_ref[:1, :])
    rows = c_ref.shape[0]
    for place, out_ref in enumerate((mine_out_ref, x_out_ref, e_out_ref)):
        out_ref[...] = jnp.broadcast_to(best[:, place * rows : (place + 1) * rows], out_ref.shape)
    far_ref[...] = jnp.concatenate([own_ref[:rows], c_ref[...], h, ch], axis=0)
    far_ids_ref[...] = jnp.concatenate([h_ids, ch_ids], axis=0)


def middle(best, own, c, h, ch, ids):
    rows, width = c.shape
    return pl.pallas_call(
        middle_kernel,
        out_shape=[jax.ShapeDtypeStruct((8, rows), jnp.float32)] * 3
        + [jax.ShapeDtypeStruct((4 * rows, width), jnp.bfloat16), jax.ShapeDtypeStruct((2, rows), jnp.int32)],
        in_specs=(VMEM, VMEM, VMEM, [VMEM] * len(h), [VMEM] * len(ch), *[VMEM] * len(ids)),
        out_specs=[VMEM] * 5,
        compiler_params=LIMIT,
        name="middle",
    )(best, own, c, h, ch, *ids)


def late_kernel(far_ref, xe_refs, ids_ref, c_ids_ref, e_ids_ref, h_ids_ref, out_ref):
    xe = block(xe_refs)
    rows = xe.shape[0]
    others = [far_ref[place * rows : (place + 1) * rows] for place in range(4)]
    other_ids = [ids_ref[...], c_ids_ref[...], h_ids_ref[:1, :], h_ids_ref[1:, :]]
    out_ref[...] = jnp.broadcast_to(best_of(xe, e_ids_ref[1:, :], others, other_ids), out_ref.shape)


def late(far, xe, ids):
    return pl.pallas_call(
        late_kernel,
        out_shape=jax.ShapeDtypeStruct((8, far.shape[0] // 4), jnp.float32),
        in_specs=(VMEM, [VMEM] * len(xe), *[VMEM] * len(ids)),
        out_specs=VMEM,
        compiler_params=LIMIT,
        name="late",
    )(far, xe, *ids)


def square(embeddings, assignment):
    def swap(flip, array):
        return lax.ppermute(array, AXES, [(i, i ^ flip) for i in range(16)])

    rows = embeddings.shape[0]
    mine, ids = embeddings, assignment.reshape(1, rows)
    e = swap(LOW, mine)
    x = swap(SHARD, mine)
    c = swap(SUB, mine)
    h = swap(HIGH, label(mine, ids))
    x_ids, c_ids = swap(SHARD, ids), swap(SUB, ids)
    e_ids = swap(LOW, jnp.concatenate([ids, x_ids]))
    e_then, _ = lax.optimization_barrier((e, x_ids))
    xe = swap(SHARD, e_then)
    h_then, *_ = lax.optimization_barrier((h, e_ids, c_ids, c))
    ch = [swap(SUB, h_then[: rows // 2]), swap(SUB, h_then[rows // 2 :])]
    x, e, h, c, xe = [x], [e], [h], [c], [xe]
    best, own, c = early(mine, x, e, c, [ids, x_ids, c_ids, e_ids])
    found, x_best, e_best, far, h_ids = middle(best, own, c, h, ch, [ids, x_ids, e_ids])
    x_best = swap(SHARD, x_best)
    xe_best = late(far, xe, [ids, c_ids, e_ids, h_ids])
    e_best, xe_best = lax.optimization_barrier((e_best, xe_best))
    xe_best, e_best = swap(LOW | SHARD, xe_best), swap(LOW, e_best)
    return jnp.maximum(jnp.maximum(jnp.maximum(xe_best, e_best), x_best), found)[0]


def shared_owner(embeddings, assignment):
    route, gather = AXES[:1], AXES[1:]
    owners = lax.axis_size(route)
    flip = jnp.zeros((1, 1), jnp.int32)
    (sent,) = pack(flip, embeddings, assignment, 1)
    got = lax.all_to_all(sent, route, split_axis=0, concat_axis=0, tiled=True)
    others = lax.all_gather(got, gather, axis=0, tiled=True)
    first = (lax.axis_index(gather) * SLOTS).astype(jnp.int32).reshape(1, 1)
    best = shared_best_of(got, others, first, owners)
    returned = lax.all_to_all(best, route, split_axis=0, concat_axis=0, tiled=True)
    return unpack(flip, [returned[i] for i in range(owners)], assignment)


def solution(mesh):
    placed = (
        P(("groups", "blk", "shard", "sub"), None),
        P(("groups", "blk", "shard", "sub"), None),
    )
    four_bits = [mesh.shape[axis] for axis in AXES] == [4, 2, 2]
    program = square if four_bits else shared_owner
    return jax.shard_map(
        program,
        mesh=mesh,
        in_specs=placed,
        out_specs=P(("groups", "blk", "shard", "sub")),
        check_vma=False,
    )
```

```python
import functools
import math

import jax
import jax.numpy as jnp
from jax import lax
from jax.experimental import pallas as pl
from jax.experimental.pallas import tpu as pltpu
from jax.sharding import PartitionSpec as P

CLUSTERS = 16
CAP = 16
SLOTS = CLUSTERS * CAP
LANES = 128
EMPTY = 4.0
NONE = -2.0
TAIL = 8
HIGH, LOW, SHARD, SUB = 8, 4, 2, 1
LIMIT = pltpu.CompilerParams(vmem_limit_bytes=12 << 20)
AXES = ("blk", "shard", "sub")

VMEM = pl.BlockSpec(memory_space=pltpu.VMEM)
SMEM = pl.BlockSpec(memory_space=pltpu.SMEM)


def placement(cluster, flip):
    rows = cluster.shape[1]
    label = lax.broadcasted_iota(jnp.int32, (CLUSTERS, rows), 0)
    member = (cluster == label).astype(jnp.float32)
    before = lax.broadcasted_iota(jnp.int32, (rows, rows), 0) < lax.broadcasted_iota(
        jnp.int32, (rows, rows), 1
    )
    earlier = jnp.dot(
        member.astype(jnp.bfloat16),
        before.astype(jnp.float32).astype(jnp.bfloat16),
        preferred_element_type=jnp.float32,
    )
    within = jnp.sum(earlier * member, axis=0, keepdims=True).astype(jnp.int32)
    target = (cluster ^ flip) * CAP + within
    return lax.broadcasted_iota(jnp.int32, (SLOTS, rows), 0) == target


def pack_kernel(flip_ref, rows_ref, cluster_ref, *out_refs):
    values = rows_ref[...].astype(jnp.float32)
    width = values.shape[1]
    scaled = values * lax.rsqrt(jnp.mean(values * values, axis=1, keepdims=True) + 1e-06)
    unit = (scaled * (1.0 / math.sqrt(width))).astype(jnp.bfloat16)
    placed = placement(cluster_ref[...], flip_ref[0, 0]).astype(jnp.float32)
    slots = jnp.dot(placed.astype(jnp.bfloat16), unit, preferred_element_type=jnp.float32)
    used = jnp.sum(placed, axis=1, keepdims=True)
    first = lax.broadcasted_iota(jnp.int32, slots.shape, 1) == 0
    slots = jnp.where(first & (used < 0.5), EMPTY, slots).astype(jnp.bfloat16)
    count = SLOTS // len(out_refs)
    for block, out_ref in enumerate(out_refs):
        out_ref[...] = slots[block * count : (block + 1) * count]


def pack(flip, embeddings, assignment, blocks):
    rows, width = embeddings.shape
    return pl.pallas_call(
        pack_kernel,
        out_shape=[jax.ShapeDtypeStruct((SLOTS // blocks, width), jnp.bfloat16)] * blocks,
        in_specs=[SMEM, VMEM, VMEM],
        out_specs=[VMEM] * blocks,
        name="pack",
    )(flip, embeddings, assignment.reshape(1, rows))


def shared_best_kernel(count, first_ref, slots_ref, others_ref, out_ref, best_ref):
    step = pl.program_id(0)
    slots, others = slots_ref[...], others_ref[...]
    similar = lax.dot_general(
        others, slots, (((1,), (1,)), ((), ())), preferred_element_type=jnp.float32
    )
    used = others[:, :1].astype(jnp.float32) < 2.0
    row = lax.broadcasted_iota(jnp.int32, similar.shape, 0)
    column = lax.broadcasted_iota(jnp.int32, similar.shape, 1)
    kept = used & (row + step * slots.shape[0] != column + first_ref[0, 0])
    kept = kept & (row % count // CAP == column % count // CAP)
    best = jnp.max(jnp.where(kept, similar, NONE), axis=0, keepdims=True)

    @pl.when(step == 0)
    def _():
        best_ref[...] = best

    @pl.when(step > 0)
    def _():
        best_ref[...] = jnp.maximum(best_ref[...], best)

    @pl.when(step == pl.num_programs(0) - 1)
    def _():
        for source in range(out_ref.shape[0]):
            piece = best_ref[:, source * count : (source + 1) * count]
            out_ref[source, :, :count] = jnp.broadcast_to(piece, (8, count))
            if count < LANES:
                out_ref[source, :, count:] = jnp.full((8, LANES - count), NONE)


def shared_best_of(slots, others, first, owners):
    size, width = slots.shape
    return pl.pallas_call(
        functools.partial(shared_best_kernel, size // owners),
        grid=(others.shape[0] // size,),
        out_shape=jax.ShapeDtypeStruct((owners, 8, LANES), jnp.float32),
        in_specs=[
            pl.BlockSpec((1, 1), lambda i: (0, 0), memory_space=pltpu.SMEM),
            pl.BlockSpec((size, width), lambda i: (0, 0)),
            pl.BlockSpec((size, width), lambda i: (i, 0)),
        ],
        out_specs=pl.BlockSpec((owners, 8, LANES), lambda i: (0, 0, 0)),
        scratch_shapes=[pltpu.VMEM((1, size), jnp.float32)],
        name="shared_best",
    )(first, slots, others)


def unpack_kernel(flip_ref, cluster_ref, *refs):
    returned_refs, out_ref = refs[:-1], refs[-1]
    count = SLOTS // len(returned_refs)
    placed = placement(cluster_ref[...], flip_ref[0, 0])
    returned = jnp.concatenate(
        [jnp.broadcast_to(ref[:1, :], (count, LANES)) for ref in returned_refs], axis=0
    )
    slot = lax.broadcasted_iota(jnp.int32, (SLOTS, LANES), 0) % count
    lane = lax.broadcasted_iota(jnp.int32, (SLOTS, LANES), 1)
    by_slot = jnp.max(jnp.where(slot == lane, returned, NONE), axis=1, keepdims=True)
    out_ref[...] = jnp.max(jnp.where(placed, by_slot, NONE), axis=0, keepdims=True)


def unpack(flip, returned, assignment):
    rows = assignment.shape[0]
    return pl.pallas_call(
        unpack_kernel,
        out_shape=jax.ShapeDtypeStruct((1, rows), jnp.float32),
        in_specs=[SMEM, VMEM] + [VMEM] * len(returned),
        out_specs=VMEM,
        name="unpack",
    )(flip, assignment.reshape(1, rows), *returned).reshape(-1)


def unit_of(values):
    values = values.astype(jnp.float32)
    scaled = values * lax.rsqrt(jnp.mean(values * values, axis=1, keepdims=True) + 1e-06)
    return (scaled * (1.0 / math.sqrt(values.shape[1]))).astype(jnp.bfloat16)


def best_of(own, own_clusters, others, other_clusters, same_rows=False):
    best = None
    for place, (rows, clusters) in enumerate(zip(others, other_clusters)):
        count = rows.shape[0]
        similar = lax.dot_general(
            rows, own, (((1,), (1,)), ((), ())), preferred_element_type=jnp.float32
        )
        down = jnp.broadcast_to(clusters, (count, count)).T[:, :1]
        kept = down == own_clusters
        if same_rows and place == 0:
            row = lax.broadcasted_iota(jnp.int32, similar.shape, 0)
            column = lax.broadcasted_iota(jnp.int32, similar.shape, 1)
            kept = kept & (row != column)
        found = jnp.max(jnp.where(kept, similar, NONE), axis=0, keepdims=True)
        best = found if best is None else jnp.maximum(best, found)
    return best


def block(refs):
    return jnp.concatenate([unit_of(ref[...]) for ref in refs], axis=0)


def labelled(refs):
    last = refs[-1][...]
    pieces = [ref[...] for ref in refs[:-1]] + [last[: last.shape[0] - TAIL]]
    rows = jnp.concatenate([unit_of(piece) for piece in pieces], axis=0)
    return rows, last[last.shape[0] - TAIL :, : rows.shape[0]].astype(jnp.float32)[:1].astype(jnp.int32)


def early_kernel(mine_ref, x_refs, e_refs, c_refs, ids_ref, x_ids_ref, c_ids_ref, e_ids_ref, best_ref, own_ref, c_ref):
    mine, c = unit_of(mine_ref[...]), block(c_refs)
    own = jnp.concatenate([mine, block(x_refs), block(e_refs)], axis=0)
    own_ids = jnp.concatenate([ids_ref[...], x_ids_ref[...], e_ids_ref[:1, :]], axis=1)
    best = best_of(own, own_ids, [mine, c], [ids_ref[...], c_ids_ref[...]], True)
    best_ref[...] = jnp.broadcast_to(best, best_ref.shape)
    own_ref[...] = own
    c_ref[...] = c


def early(mine, x, e, c, ids):
    rows, width = mine.shape
    return pl.pallas_call(
        early_kernel,
        out_shape=[
            jax.ShapeDtypeStruct((8, 3 * rows), jnp.float32),
            jax.ShapeDtypeStruct((3 * rows, width), jnp.bfloat16),
            jax.ShapeDtypeStruct((rows, width), jnp.bfloat16),
        ],
        in_specs=(VMEM, [VMEM] * len(x), [VMEM] * len(e), [VMEM] * len(c), *[VMEM] * len(ids)),
        out_specs=[VMEM] * 3,
        compiler_params=LIMIT,
        name="early",
    )(mine, x, e, c, *ids)


def label_kernel(rows_ref, ids_ref, out_ref):
    rows, width = rows_ref.shape
    out_ref[:rows] = rows_ref[...]
    ids = jnp.broadcast_to(ids_ref[...].astype(jnp.float32), (TAIL, rows))
    tail = jnp.concatenate([ids, jnp.zeros((TAIL, width - rows), jnp.float32)], axis=1)
    out_ref[rows:] = tail.astype(jnp.bfloat16)


def label(rows, ids):
    return pl.pallas_call(
        label_kernel,
        out_shape=jax.ShapeDtypeStruct((rows.shape[0] + TAIL, rows.shape[1]), rows.dtype),
        in_specs=[VMEM, VMEM],
        out_specs=VMEM,
        compiler_params=LIMIT,
        name="label",
    )(rows, ids)


def middle_kernel(
    best_ref, own_ref, c_ref, h_refs, ch_refs, ids_ref, x_ids_ref, e_ids_ref,
    mine_out_ref, x_out_ref, e_out_ref, far_ref, far_ids_ref,
):
    (h, h_ids), (ch, ch_ids) = labelled(h_refs), labelled(ch_refs)
    own_ids = jnp.concatenate([ids_ref[...], x_ids_ref[...], e_ids_ref[:1, :]], axis=1)
    best = best_of(own_ref[...], own_ids, [h, ch], [h_ids, ch_ids])
    best = jnp.maximum(best, best_ref[:1, :])
    rows = c_ref.shape[0]
    for place, out_ref in enumerate((mine_out_ref, x_out_ref, e_out_ref)):
        out_ref[...] = jnp.broadcast_to(best[:, place * rows : (place + 1) * rows], out_ref.shape)
    far_ref[...] = jnp.concatenate([own_ref[:rows], c_ref[...], h, ch], axis=0)
    far_ids_ref[...] = jnp.concatenate([h_ids, ch_ids], axis=0)


def middle(best, own, c, h, ch, ids):
    rows, width = c.shape
    return pl.pallas_call(
        middle_kernel,
        out_shape=[jax.ShapeDtypeStruct((8, rows), jnp.float32)] * 3
        + [jax.ShapeDtypeStruct((4 * rows, width), jnp.bfloat16), jax.ShapeDtypeStruct((2, rows), jnp.int32)],
        in_specs=(VMEM, VMEM, VMEM, [VMEM] * len(h), [VMEM] * len(ch), *[VMEM] * len(ids)),
        out_specs=[VMEM] * 5,
        compiler_params=LIMIT,
        name="middle",
    )(best, own, c, h, ch, *ids)


def late_kernel(far_ref, xe_refs, ids_ref, c_ids_ref, e_ids_ref, h_ids_ref, out_ref):
    xe = block(xe_refs)
    rows = xe.shape[0]
    others = [far_ref[place * rows : (place + 1) * rows] for place in range(4)]
    other_ids = [ids_ref[...], c_ids_ref[...], h_ids_ref[:1, :], h_ids_ref[1:, :]]
    out_ref[...] = jnp.broadcast_to(best_of(xe, e_ids_ref[1:, :], others, other_ids), out_ref.shape)


def late(far, xe, ids):
    return pl.pallas_call(
        late_kernel,
        out_shape=jax.ShapeDtypeStruct((8, far.shape[0] // 4), jnp.float32),
        in_specs=(VMEM, [VMEM] * len(xe), *[VMEM] * len(ids)),
        out_specs=VMEM,
        compiler_params=LIMIT,
        name="late",
    )(far, xe, *ids)


def square(embeddings, assignment):
    def swap(flip, array):
        return lax.ppermute(array, AXES, [(i, i ^ flip) for i in range(16)])

    rows = embeddings.shape[0]
    mine, ids = embeddings, assignment.reshape(1, rows)
    e = swap(LOW, mine)
    x = swap(SHARD, mine)
    h = swap(HIGH, label(mine, ids))
    x_ids, c_ids = swap(SHARD, ids), swap(SUB, ids)
    e_ids = swap(LOW, jnp.concatenate([ids, x_ids]))
    mine_then, _ = lax.optimization_barrier((mine, e_ids))
    c = swap(SUB, mine_then)
    e_then, _ = lax.optimization_barrier((e, x_ids))
    xe = swap(SHARD, e_then)
    h_then, _ = lax.optimization_barrier((h, c_ids))
    ch = [swap(SUB, h_then[: rows // 2]), swap(SUB, h_then[rows // 2 :])]
    x, e, h, c, xe = [x], [e], [h], [c], [xe]
    best, own, c = early(mine, x, e, c, [ids, x_ids, c_ids, e_ids])
    found, x_best, e_best, far, h_ids = middle(best, own, c, h, ch, [ids, x_ids, e_ids])
    x_best = swap(SHARD, x_best)
    xe_best = late(far, xe, [ids, c_ids, e_ids, h_ids])
    e_best, xe_best = lax.optimization_barrier((e_best, xe_best))
    xe_best, e_best = swap(LOW | SHARD, xe_best), swap(LOW, e_best)
    return jnp.maximum(jnp.maximum(jnp.maximum(xe_best, e_best), x_best), found)[0]


def shared_owner(embeddings, assignment):
    route, gather = AXES[:1], AXES[1:]
    owners = lax.axis_size(route)
    flip = jnp.zeros((1, 1), jnp.int32)
    (sent,) = pack(flip, embeddings, assignment, 1)
    got = lax.all_to_all(sent, route, split_axis=0, concat_axis=0, tiled=True)
    others = lax.all_gather(got, gather, axis=0, tiled=True)
    first = (lax.axis_index(gather) * SLOTS).astype(jnp.int32).reshape(1, 1)
    best = shared_best_of(got, others, first, owners)
    returned = lax.all_to_all(best, route, split_axis=0, concat_axis=0, tiled=True)
    return unpack(flip, [returned[i] for i in range(owners)], assignment)


def solution(mesh):
    placed = (
        P(("groups", "blk", "shard", "sub"), None),
        P(("groups", "blk", "shard", "sub"), None),
    )
    four_bits = [mesh.shape[axis] for axis in AXES] == [4, 2, 2]
    program = square if four_bits else shared_owner
    return jax.shard_map(
        program,
        mesh=mesh,
        in_specs=placed,
        out_specs=P(("groups", "blk", "shard", "sub")),
        check_vma=False,
    )
```

```python
import functools
import math

import jax
import jax.numpy as jnp
from jax import lax
from jax.experimental import pallas as pl
from jax.experimental.pallas import tpu as pltpu
from jax.sharding import PartitionSpec as P

CLUSTERS = 16
CAP = 16
SLOTS = CLUSTERS * CAP
LANES = 128
EMPTY = 4.0
NONE = -2.0
TAIL = 8
HIGH, LOW, SHARD, SUB = 8, 4, 2, 1
LIMIT = pltpu.CompilerParams(vmem_limit_bytes=12 << 20)
AXES = ("blk", "shard", "sub")

VMEM = pl.BlockSpec(memory_space=pltpu.VMEM)
SMEM = pl.BlockSpec(memory_space=pltpu.SMEM)


def placement(cluster, flip):
    rows = cluster.shape[1]
    label = lax.broadcasted_iota(jnp.int32, (CLUSTERS, rows), 0)
    member = (cluster == label).astype(jnp.float32)
    before = lax.broadcasted_iota(jnp.int32, (rows, rows), 0) < lax.broadcasted_iota(
        jnp.int32, (rows, rows), 1
    )
    earlier = jnp.dot(
        member.astype(jnp.bfloat16),
        before.astype(jnp.float32).astype(jnp.bfloat16),
        preferred_element_type=jnp.float32,
    )
    within = jnp.sum(earlier * member, axis=0, keepdims=True).astype(jnp.int32)
    target = (cluster ^ flip) * CAP + within
    return lax.broadcasted_iota(jnp.int32, (SLOTS, rows), 0) == target


def pack_kernel(flip_ref, rows_ref, cluster_ref, *out_refs):
    values = rows_ref[...].astype(jnp.float32)
    width = values.shape[1]
    scaled = values * lax.rsqrt(jnp.mean(values * values, axis=1, keepdims=True) + 1e-06)
    unit = (scaled * (1.0 / math.sqrt(width))).astype(jnp.bfloat16)
    placed = placement(cluster_ref[...], flip_ref[0, 0]).astype(jnp.float32)
    slots = jnp.dot(placed.astype(jnp.bfloat16), unit, preferred_element_type=jnp.float32)
    used = jnp.sum(placed, axis=1, keepdims=True)
    first = lax.broadcasted_iota(jnp.int32, slots.shape, 1) == 0
    slots = jnp.where(first & (used < 0.5), EMPTY, slots).astype(jnp.bfloat16)
    count = SLOTS // len(out_refs)
    for block, out_ref in enumerate(out_refs):
        out_ref[...] = slots[block * count : (block + 1) * count]


def pack(flip, embeddings, assignment, blocks):
    rows, width = embeddings.shape
    return pl.pallas_call(
        pack_kernel,
        out_shape=[jax.ShapeDtypeStruct((SLOTS // blocks, width), jnp.bfloat16)] * blocks,
        in_specs=[SMEM, VMEM, VMEM],
        out_specs=[VMEM] * blocks,
        name="pack",
    )(flip, embeddings, assignment.reshape(1, rows))


def shared_best_kernel(count, first_ref, slots_ref, others_ref, out_ref, best_ref):
    step = pl.program_id(0)
    slots, others = slots_ref[...], others_ref[...]
    similar = lax.dot_general(
        others, slots, (((1,), (1,)), ((), ())), preferred_element_type=jnp.float32
    )
    used = others[:, :1].astype(jnp.float32) < 2.0
    row = lax.broadcasted_iota(jnp.int32, similar.shape, 0)
    column = lax.broadcasted_iota(jnp.int32, similar.shape, 1)
    kept = used & (row + step * slots.shape[0] != column + first_ref[0, 0])
    kept = kept & (row % count // CAP == column % count // CAP)
    best = jnp.max(jnp.where(kept, similar, NONE), axis=0, keepdims=True)

    @pl.when(step == 0)
    def _():
        best_ref[...] = best

    @pl.when(step > 0)
    def _():
        best_ref[...] = jnp.maximum(best_ref[...], best)

    @pl.when(step == pl.num_programs(0) - 1)
    def _():
        for source in range(out_ref.shape[0]):
            piece = best_ref[:, source * count : (source + 1) * count]
            out_ref[source, :, :count] = jnp.broadcast_to(piece, (8, count))
            if count < LANES:
                out_ref[source, :, count:] = jnp.full((8, LANES - count), NONE)


def shared_best_of(slots, others, first, owners):
    size, width = slots.shape
    return pl.pallas_call(
        functools.partial(shared_best_kernel, size // owners),
        grid=(others.shape[0] // size,),
        out_shape=jax.ShapeDtypeStruct((owners, 8, LANES), jnp.float32),
        in_specs=[
            pl.BlockSpec((1, 1), lambda i: (0, 0), memory_space=pltpu.SMEM),
            pl.BlockSpec((size, width), lambda i: (0, 0)),
            pl.BlockSpec((size, width), lambda i: (i, 0)),
        ],
        out_specs=pl.BlockSpec((owners, 8, LANES), lambda i: (0, 0, 0)),
        scratch_shapes=[pltpu.VMEM((1, size), jnp.float32)],
        name="shared_best",
    )(first, slots, others)


def unpack_kernel(flip_ref, cluster_ref, *refs):
    returned_refs, out_ref = refs[:-1], refs[-1]
    count = SLOTS // len(returned_refs)
    placed = placement(cluster_ref[...], flip_ref[0, 0])
    returned = jnp.concatenate(
        [jnp.broadcast_to(ref[:1, :], (count, LANES)) for ref in returned_refs], axis=0
    )
    slot = lax.broadcasted_iota(jnp.int32, (SLOTS, LANES), 0) % count
    lane = lax.broadcasted_iota(jnp.int32, (SLOTS, LANES), 1)
    by_slot = jnp.max(jnp.where(slot == lane, returned, NONE), axis=1, keepdims=True)
    out_ref[...] = jnp.max(jnp.where(placed, by_slot, NONE), axis=0, keepdims=True)


def unpack(flip, returned, assignment):
    rows = assignment.shape[0]
    return pl.pallas_call(
        unpack_kernel,
        out_shape=jax.ShapeDtypeStruct((1, rows), jnp.float32),
        in_specs=[SMEM, VMEM] + [VMEM] * len(returned),
        out_specs=VMEM,
        name="unpack",
    )(flip, assignment.reshape(1, rows), *returned).reshape(-1)


def unit_of(values):
    values = values.astype(jnp.float32)
    scaled = values * lax.rsqrt(jnp.mean(values * values, axis=1, keepdims=True) + 1e-06)
    return (scaled * (1.0 / math.sqrt(values.shape[1]))).astype(jnp.bfloat16)


def best_of(own, own_clusters, others, other_clusters, same_rows=False):
    best = None
    for place, (rows, clusters) in enumerate(zip(others, other_clusters)):
        count = rows.shape[0]
        similar = lax.dot_general(
            rows, own, (((1,), (1,)), ((), ())), preferred_element_type=jnp.float32
        )
        down = jnp.broadcast_to(clusters, (count, count)).T[:, :1]
        kept = down == own_clusters
        if same_rows and place == 0:
            row = lax.broadcasted_iota(jnp.int32, similar.shape, 0)
            column = lax.broadcasted_iota(jnp.int32, similar.shape, 1)
            kept = kept & (row != column)
        found = jnp.max(jnp.where(kept, similar, NONE), axis=0, keepdims=True)
        best = found if best is None else jnp.maximum(best, found)
    return best


def block(refs):
    return jnp.concatenate([unit_of(ref[...]) for ref in refs], axis=0)


def labelled(refs):
    last = refs[-1][...]
    pieces = [ref[...] for ref in refs[:-1]] + [last[: last.shape[0] - TAIL]]
    rows = jnp.concatenate([unit_of(piece) for piece in pieces], axis=0)
    return rows, last[last.shape[0] - TAIL :, : rows.shape[0]].astype(jnp.float32)[:1].astype(jnp.int32)


def early_kernel(mine_ref, x_refs, e_refs, c_refs, ids_ref, x_ids_ref, c_ids_ref, e_ids_ref, best_ref, own_ref, c_ref):
    mine, c = unit_of(mine_ref[...]), block(c_refs)
    own = jnp.concatenate([mine, block(x_refs), block(e_refs)], axis=0)
    own_ids = jnp.concatenate([ids_ref[...], x_ids_ref[...], e_ids_ref[:1, :]], axis=1)
    best = best_of(own, own_ids, [mine, c], [ids_ref[...], c_ids_ref[...]], True)
    best_ref[...] = jnp.broadcast_to(best, best_ref.shape)
    own_ref[...] = own
    c_ref[...] = c


def early(mine, x, e, c, ids):
    rows, width = mine.shape
    return pl.pallas_call(
        early_kernel,
        out_shape=[
            jax.ShapeDtypeStruct((8, 3 * rows), jnp.float32),
            jax.ShapeDtypeStruct((3 * rows, width), jnp.bfloat16),
            jax.ShapeDtypeStruct((rows, width), jnp.bfloat16),
        ],
        in_specs=(VMEM, [VMEM] * len(x), [VMEM] * len(e), [VMEM] * len(c), *[VMEM] * len(ids)),
        out_specs=[VMEM] * 3,
        compiler_params=LIMIT,
        name="early",
    )(mine, x, e, c, *ids)


def label_kernel(rows_ref, ids_ref, out_ref):
    rows, width = rows_ref.shape
    out_ref[:rows] = rows_ref[...]
    ids = jnp.broadcast_to(ids_ref[...].astype(jnp.float32), (TAIL, rows))
    tail = jnp.concatenate([ids, jnp.zeros((TAIL, width - rows), jnp.float32)], axis=1)
    out_ref[rows:] = tail.astype(jnp.bfloat16)


def label(rows, ids):
    return pl.pallas_call(
        label_kernel,
        out_shape=jax.ShapeDtypeStruct((rows.shape[0] + TAIL, rows.shape[1]), rows.dtype),
        in_specs=[VMEM, VMEM],
        out_specs=VMEM,
        compiler_params=LIMIT,
        name="label",
    )(rows, ids)


def middle_kernel(
    best_ref, own_ref, c_ref, h_refs, ch_refs, ids_ref, x_ids_ref, e_ids_ref,
    mine_out_ref, x_out_ref, e_out_ref, far_ref, far_ids_ref,
):
    (h, h_ids), (ch, ch_ids) = labelled(h_refs), labelled(ch_refs)
    own_ids = jnp.concatenate([ids_ref[...], x_ids_ref[...], e_ids_ref[:1, :]], axis=1)
    best = best_of(own_ref[...], own_ids, [h, ch], [h_ids, ch_ids])
    best = jnp.maximum(best, best_ref[:1, :])
    rows = c_ref.shape[0]
    for place, out_ref in enumerate((mine_out_ref, x_out_ref, e_out_ref)):
        out_ref[...] = jnp.broadcast_to(best[:, place * rows : (place + 1) * rows], out_ref.shape)
    far_ref[...] = jnp.concatenate([own_ref[:rows], c_ref[...], h, ch], axis=0)
    far_ids_ref[...] = jnp.concatenate([h_ids, ch_ids], axis=0)


def middle(best, own, c, h, ch, ids):
    rows, width = c.shape
    return pl.pallas_call(
        middle_kernel,
        out_shape=[jax.ShapeDtypeStruct((8, rows), jnp.float32)] * 3
        + [jax.ShapeDtypeStruct((4 * rows, width), jnp.bfloat16), jax.ShapeDtypeStruct((2, rows), jnp.int32)],
        in_specs=(VMEM, VMEM, VMEM, [VMEM] * len(h), [VMEM] * len(ch), *[VMEM] * len(ids)),
        out_specs=[VMEM] * 5,
        compiler_params=LIMIT,
        name="middle",
    )(best, own, c, h, ch, *ids)


def late_kernel(far_ref, xe_refs, ids_ref, c_ids_ref, e_ids_ref, h_ids_ref, out_ref):
    xe = block(xe_refs)
    rows = xe.shape[0]
    others = [far_ref[place * rows : (place + 1) * rows] for place in range(4)]
    other_ids = [ids_ref[...], c_ids_ref[...], h_ids_ref[:1, :], h_ids_ref[1:, :]]
    out_ref[...] = jnp.broadcast_to(best_of(xe, e_ids_ref[1:, :], others, other_ids), out_ref.shape)


def late(far, xe, ids):
    return pl.pallas_call(
        late_kernel,
        out_shape=jax.ShapeDtypeStruct((8, far.shape[0] // 4), jnp.float32),
        in_specs=(VMEM, [VMEM] * len(xe), *[VMEM] * len(ids)),
        out_specs=VMEM,
        compiler_params=LIMIT,
        name="late",
    )(far, xe, *ids)


def square(embeddings, assignment):
    def swap(flip, array):
        return lax.ppermute(array, AXES, [(i, i ^ flip) for i in range(16)])

    rows = embeddings.shape[0]
    mine, ids = embeddings, assignment.reshape(1, rows)
    e = swap(LOW, mine)
    x = swap(SHARD, mine)
    c = swap(SUB, mine)
    h = swap(HIGH, label(mine, ids))
    x_ids, c_ids = swap(SHARD, ids), swap(SUB, ids)
    e_ids = swap(LOW, jnp.concatenate([ids, x_ids]))
    e_then, _, _ = lax.optimization_barrier((e, x_ids, c))
    xe = swap(SHARD, e_then)
    h_then, *_ = lax.optimization_barrier((h, e_ids, c_ids, c))
    ch = [swap(SUB, h_then[: rows // 2]), swap(SUB, h_then[rows // 2 :])]
    x, e, h, c, xe = [x], [e], [h], [c], [xe]
    best, own, c = early(mine, x, e, c, [ids, x_ids, c_ids, e_ids])
    found, x_best, e_best, far, h_ids = middle(best, own, c, h, ch, [ids, x_ids, e_ids])
    x_best = swap(SHARD, x_best)
    xe_best = late(far, xe, [ids, c_ids, e_ids, h_ids])
    e_best, xe_best = lax.optimization_barrier((e_best, xe_best))
    xe_best, e_best = swap(LOW | SHARD, xe_best), swap(LOW, e_best)
    return jnp.maximum(jnp.maximum(jnp.maximum(xe_best, e_best), x_best), found)[0]


def shared_owner(embeddings, assignment):
    route, gather = AXES[:1], AXES[1:]
    owners = lax.axis_size(route)
    flip = jnp.zeros((1, 1), jnp.int32)
    (sent,) = pack(flip, embeddings, assignment, 1)
    got = lax.all_to_all(sent, route, split_axis=0, concat_axis=0, tiled=True)
    others = lax.all_gather(got, gather, axis=0, tiled=True)
    first = (lax.axis_index(gather) * SLOTS).astype(jnp.int32).reshape(1, 1)
    best = shared_best_of(got, others, first, owners)
    returned = lax.all_to_all(best, route, split_axis=0, concat_axis=0, tiled=True)
    return unpack(flip, [returned[i] for i in range(owners)], assignment)


def solution(mesh):
    placed = (
        P(("groups", "blk", "shard", "sub"), None),
        P(("groups", "blk", "shard", "sub"), None),
    )
    four_bits = [mesh.shape[axis] for axis in AXES] == [4, 2, 2]
    program = square if four_bits else shared_owner
    return jax.shard_map(
        program,
        mesh=mesh,
        in_specs=placed,
        out_specs=P(("groups", "blk", "shard", "sub")),
        check_vma=False,
    )
```

```python
import functools
import math

import jax
import jax.numpy as jnp
from jax import lax
from jax.experimental import pallas as pl
from jax.experimental.pallas import tpu as pltpu
from jax.sharding import PartitionSpec as P

CLUSTERS = 16
CAP = 16
SLOTS = CLUSTERS * CAP
LANES = 128
EMPTY = 4.0
NONE = -2.0
HIGH, LOW, SHARD, SUB = 8, 4, 2, 1
LIMIT = pltpu.CompilerParams(vmem_limit_bytes=12 << 20)
AXES = ("blk", "shard", "sub")

VMEM = pl.BlockSpec(memory_space=pltpu.VMEM)
SMEM = pl.BlockSpec(memory_space=pltpu.SMEM)


def placement(cluster, flip):
    rows = cluster.shape[1]
    label = lax.broadcasted_iota(jnp.int32, (CLUSTERS, rows), 0)
    member = (cluster == label).astype(jnp.float32)
    before = lax.broadcasted_iota(jnp.int32, (rows, rows), 0) < lax.broadcasted_iota(
        jnp.int32, (rows, rows), 1
    )
    earlier = jnp.dot(
        member.astype(jnp.bfloat16),
        before.astype(jnp.float32).astype(jnp.bfloat16),
        preferred_element_type=jnp.float32,
    )
    within = jnp.sum(earlier * member, axis=0, keepdims=True).astype(jnp.int32)
    target = (cluster ^ flip) * CAP + within
    return lax.broadcasted_iota(jnp.int32, (SLOTS, rows), 0) == target


def pack_kernel(flip_ref, rows_ref, cluster_ref, *out_refs):
    values = rows_ref[...].astype(jnp.float32)
    width = values.shape[1]
    scaled = values * lax.rsqrt(jnp.mean(values * values, axis=1, keepdims=True) + 1e-06)
    unit = (scaled * (1.0 / math.sqrt(width))).astype(jnp.bfloat16)
    placed = placement(cluster_ref[...], flip_ref[0, 0]).astype(jnp.float32)
    slots = jnp.dot(placed.astype(jnp.bfloat16), unit, preferred_element_type=jnp.float32)
    used = jnp.sum(placed, axis=1, keepdims=True)
    first = lax.broadcasted_iota(jnp.int32, slots.shape, 1) == 0
    slots = jnp.where(first & (used < 0.5), EMPTY, slots).astype(jnp.bfloat16)
    count = SLOTS // len(out_refs)
    for block, out_ref in enumerate(out_refs):
        out_ref[...] = slots[block * count : (block + 1) * count]


def pack(flip, embeddings, assignment, blocks):
    rows, width = embeddings.shape
    return pl.pallas_call(
        pack_kernel,
        out_shape=[jax.ShapeDtypeStruct((SLOTS // blocks, width), jnp.bfloat16)] * blocks,
        in_specs=[SMEM, VMEM, VMEM],
        out_specs=[VMEM] * blocks,
        name="pack",
    )(flip, embeddings, assignment.reshape(1, rows))


def shared_best_kernel(count, first_ref, slots_ref, others_ref, out_ref, best_ref):
    step = pl.program_id(0)
    slots, others = slots_ref[...], others_ref[...]
    similar = lax.dot_general(
        others, slots, (((1,), (1,)), ((), ())), preferred_element_type=jnp.float32
    )
    used = others[:, :1].astype(jnp.float32) < 2.0
    row = lax.broadcasted_iota(jnp.int32, similar.shape, 0)
    column = lax.broadcasted_iota(jnp.int32, similar.shape, 1)
    kept = used & (row + step * slots.shape[0] != column + first_ref[0, 0])
    kept = kept & (row % count // CAP == column % count // CAP)
    best = jnp.max(jnp.where(kept, similar, NONE), axis=0, keepdims=True)

    @pl.when(step == 0)
    def _():
        best_ref[...] = best

    @pl.when(step > 0)
    def _():
        best_ref[...] = jnp.maximum(best_ref[...], best)

    @pl.when(step == pl.num_programs(0) - 1)
    def _():
        for source in range(out_ref.shape[0]):
            piece = best_ref[:, source * count : (source + 1) * count]
            out_ref[source, :, :count] = jnp.broadcast_to(piece, (8, count))
            if count < LANES:
                out_ref[source, :, count:] = jnp.full((8, LANES - count), NONE)


def shared_best_of(slots, others, first, owners):
    size, width = slots.shape
    return pl.pallas_call(
        functools.partial(shared_best_kernel, size // owners),
        grid=(others.shape[0] // size,),
        out_shape=jax.ShapeDtypeStruct((owners, 8, LANES), jnp.float32),
        in_specs=[
            pl.BlockSpec((1, 1), lambda i: (0, 0), memory_space=pltpu.SMEM),
            pl.BlockSpec((size, width), lambda i: (0, 0)),
            pl.BlockSpec((size, width), lambda i: (i, 0)),
        ],
        out_specs=pl.BlockSpec((owners, 8, LANES), lambda i: (0, 0, 0)),
        scratch_shapes=[pltpu.VMEM((1, size), jnp.float32)],
        name="shared_best",
    )(first, slots, others)


def unpack_kernel(flip_ref, cluster_ref, *refs):
    returned_refs, out_ref = refs[:-1], refs[-1]
    count = SLOTS // len(returned_refs)
    placed = placement(cluster_ref[...], flip_ref[0, 0])
    returned = jnp.concatenate(
        [jnp.broadcast_to(ref[:1, :], (count, LANES)) for ref in returned_refs], axis=0
    )
    slot = lax.broadcasted_iota(jnp.int32, (SLOTS, LANES), 0) % count
    lane = lax.broadcasted_iota(jnp.int32, (SLOTS, LANES), 1)
    by_slot = jnp.max(jnp.where(slot == lane, returned, NONE), axis=1, keepdims=True)
    out_ref[...] = jnp.max(jnp.where(placed, by_slot, NONE), axis=0, keepdims=True)


def unpack(flip, returned, assignment):
    rows = assignment.shape[0]
    return pl.pallas_call(
        unpack_kernel,
        out_shape=jax.ShapeDtypeStruct((1, rows), jnp.float32),
        in_specs=[SMEM, VMEM] + [VMEM] * len(returned),
        out_specs=VMEM,
        name="unpack",
    )(flip, assignment.reshape(1, rows), *returned).reshape(-1)


def unit_of(values):
    values = values.astype(jnp.float32)
    scaled = values * lax.rsqrt(jnp.mean(values * values, axis=1, keepdims=True) + 1e-06)
    return (scaled * (1.0 / math.sqrt(values.shape[1]))).astype(jnp.bfloat16)


def best_of(own, own_clusters, others, other_clusters, same_rows=False):
    best = None
    for place, (rows, clusters) in enumerate(zip(others, other_clusters)):
        count = rows.shape[0]
        similar = lax.dot_general(
            rows, own, (((1,), (1,)), ((), ())), preferred_element_type=jnp.float32
        )
        down = jnp.broadcast_to(clusters, (count, count)).T[:, :1]
        kept = down == own_clusters
        if same_rows and place == 0:
            row = lax.broadcasted_iota(jnp.int32, similar.shape, 0)
            column = lax.broadcasted_iota(jnp.int32, similar.shape, 1)
            kept = kept & (row != column)
        found = jnp.max(jnp.where(kept, similar, NONE), axis=0, keepdims=True)
        best = found if best is None else jnp.maximum(best, found)
    return best


def block(refs):
    return jnp.concatenate([unit_of(ref[...]) for ref in refs], axis=0)


def early_kernel(mine_ref, x_refs, e_refs, c_refs, ids_ref, x_ids_ref, c_ids_ref, e_ids_ref, best_ref, own_ref, c_ref):
    mine, c = unit_of(mine_ref[...]), block(c_refs)
    own = jnp.concatenate([mine, block(x_refs), block(e_refs)], axis=0)
    own_ids = jnp.concatenate([ids_ref[...], x_ids_ref[...], e_ids_ref[:1, :]], axis=1)
    best = best_of(own, own_ids, [mine, c], [ids_ref[...], c_ids_ref[...]], True)
    best_ref[...] = jnp.broadcast_to(best, best_ref.shape)
    own_ref[...] = own
    c_ref[...] = c


def early(mine, x, e, c, ids):
    rows, width = mine.shape
    return pl.pallas_call(
        early_kernel,
        out_shape=[
            jax.ShapeDtypeStruct((8, 3 * rows), jnp.float32),
            jax.ShapeDtypeStruct((3 * rows, width), jnp.bfloat16),
            jax.ShapeDtypeStruct((rows, width), jnp.bfloat16),
        ],
        in_specs=(VMEM, [VMEM] * len(x), [VMEM] * len(e), [VMEM] * len(c), *[VMEM] * len(ids)),
        out_specs=[VMEM] * 3,
        compiler_params=LIMIT,
        name="early",
    )(mine, x, e, c, *ids)


def middle_kernel(
    best_ref, own_ref, c_ref, h_refs, ch_refs, ids_ref, x_ids_ref, c_ids_ref, e_ids_ref, h_ids_ref,
    mine_out_ref, x_out_ref, e_out_ref, far_ref,
):
    h, ch = block(h_refs), block(ch_refs)
    own_ids = jnp.concatenate([ids_ref[...], x_ids_ref[...], e_ids_ref[:1, :]], axis=1)
    best = best_of(own_ref[...], own_ids, [h, ch], [h_ids_ref[:1, :], h_ids_ref[1:, :]])
    best = jnp.maximum(best, best_ref[:1, :])
    rows = c_ref.shape[0]
    for place, out_ref in enumerate((mine_out_ref, x_out_ref, e_out_ref)):
        out_ref[...] = jnp.broadcast_to(best[:, place * rows : (place + 1) * rows], out_ref.shape)
    far_ref[...] = jnp.concatenate([own_ref[:rows], c_ref[...], h, ch], axis=0)


def middle(best, own, c, h, ch, ids):
    rows, width = c.shape
    return pl.pallas_call(
        middle_kernel,
        out_shape=[jax.ShapeDtypeStruct((8, rows), jnp.float32)] * 3
        + [jax.ShapeDtypeStruct((4 * rows, width), jnp.bfloat16)],
        in_specs=(VMEM, VMEM, VMEM, [VMEM] * len(h), [VMEM] * len(ch), *[VMEM] * len(ids)),
        out_specs=[VMEM] * 4,
        compiler_params=LIMIT,
        name="middle",
    )(best, own, c, h, ch, *ids)


def late_kernel(far_ref, xe_refs, ids_ref, c_ids_ref, e_ids_ref, h_ids_ref, out_ref):
    xe = block(xe_refs)
    rows = xe.shape[0]
    others = [far_ref[place * rows : (place + 1) * rows] for place in range(4)]
    other_ids = [ids_ref[...], c_ids_ref[...], h_ids_ref[:1, :], h_ids_ref[1:, :]]
    out_ref[...] = jnp.broadcast_to(best_of(xe, e_ids_ref[1:, :], others, other_ids), out_ref.shape)


def late(far, xe, ids):
    return pl.pallas_call(
        late_kernel,
        out_shape=jax.ShapeDtypeStruct((8, far.shape[0] // 4), jnp.float32),
        in_specs=(VMEM, [VMEM] * len(xe), *[VMEM] * len(ids)),
        out_specs=VMEM,
        compiler_params=LIMIT,
        name="late",
    )(far, xe, *ids)


def square(embeddings, assignment):
    def swap(flip, array):
        return lax.ppermute(array, AXES, [(i, i ^ flip) for i in range(16)])

    rows = embeddings.shape[0]
    mine, ids = embeddings, assignment.reshape(1, rows)
    c = swap(SUB, mine)
    e = swap(LOW, mine)
    x = swap(SHARD, mine)
    far, _ = lax.optimization_barrier((mine, c))
    h = swap(HIGH, far)
    x_ids, c_ids = swap(SHARD, ids), swap(SUB, ids)
    e_ids = swap(LOW, jnp.concatenate([ids, x_ids]))
    h_ids = swap(HIGH, jnp.concatenate([ids, c_ids]))
    xe = swap(SHARD, e)
    h_then, _, _, _ = lax.optimization_barrier((h, h_ids, e_ids, x))
    ch = [swap(SUB, h_then[: rows // 2]), swap(SUB, h_then[rows // 2 :])]
    x, e, h, c, xe = [x], [e], [h], [c], [xe]
    best, own, c = early(mine, x, e, c, [ids, x_ids, c_ids, e_ids])
    found, x_best, e_best, far = middle(best, own, c, h, ch, [ids, x_ids, c_ids, e_ids, h_ids])
    x_best = swap(SHARD, x_best)
    xe_best = late(far, xe, [ids, c_ids, e_ids, h_ids])
    e_best, xe_best = lax.optimization_barrier((e_best, xe_best))
    xe_best, e_best = swap(LOW | SHARD, xe_best), swap(LOW, e_best)
    return jnp.maximum(jnp.maximum(jnp.maximum(xe_best, e_best), x_best), found)[0]


def shared_owner(embeddings, assignment):
    route, gather = AXES[:1], AXES[1:]
    owners = lax.axis_size(route)
    flip = jnp.zeros((1, 1), jnp.int32)
    (sent,) = pack(flip, embeddings, assignment, 1)
    got = lax.all_to_all(sent, route, split_axis=0, concat_axis=0, tiled=True)
    others = lax.all_gather(got, gather, axis=0, tiled=True)
    first = (lax.axis_index(gather) * SLOTS).astype(jnp.int32).reshape(1, 1)
    best = shared_best_of(got, others, first, owners)
    returned = lax.all_to_all(best, route, split_axis=0, concat_axis=0, tiled=True)
    return unpack(flip, [returned[i] for i in range(owners)], assignment)


def solution(mesh):
    placed = (
        P(("groups", "blk", "shard", "sub"), None),
        P(("groups", "blk", "shard", "sub"), None),
    )
    four_bits = [mesh.shape[axis] for axis in AXES] == [4, 2, 2]
    program = square if four_bits else shared_owner
    return jax.shard_map(
        program,
        mesh=mesh,
        in_specs=placed,
        out_specs=P(("groups", "blk", "shard", "sub")),
        check_vma=False,
    )
```

```python
import functools
import math

import jax
import jax.numpy as jnp
from jax import lax
from jax.experimental import pallas as pl
from jax.experimental.pallas import tpu as pltpu
from jax.sharding import PartitionSpec as P

CLUSTERS = 16
CAP = 16
SLOTS = CLUSTERS * CAP
LANES = 128
EMPTY = 4.0
NONE = -2.0
HIGH, LOW, SHARD, SUB = 8, 4, 2, 1
LIMIT = pltpu.CompilerParams(vmem_limit_bytes=12 << 20)
AXES = ("blk", "shard", "sub")

VMEM = pl.BlockSpec(memory_space=pltpu.VMEM)
SMEM = pl.BlockSpec(memory_space=pltpu.SMEM)


def placement(cluster, flip):
    rows = cluster.shape[1]
    label = lax.broadcasted_iota(jnp.int32, (CLUSTERS, rows), 0)
    member = (cluster == label).astype(jnp.float32)
    before = lax.broadcasted_iota(jnp.int32, (rows, rows), 0) < lax.broadcasted_iota(
        jnp.int32, (rows, rows), 1
    )
    earlier = jnp.dot(
        member.astype(jnp.bfloat16),
        before.astype(jnp.float32).astype(jnp.bfloat16),
        preferred_element_type=jnp.float32,
    )
    within = jnp.sum(earlier * member, axis=0, keepdims=True).astype(jnp.int32)
    target = (cluster ^ flip) * CAP + within
    return lax.broadcasted_iota(jnp.int32, (SLOTS, rows), 0) == target


def pack_kernel(flip_ref, rows_ref, cluster_ref, *out_refs):
    values = rows_ref[...].astype(jnp.float32)
    width = values.shape[1]
    scaled = values * lax.rsqrt(jnp.mean(values * values, axis=1, keepdims=True) + 1e-06)
    unit = (scaled * (1.0 / math.sqrt(width))).astype(jnp.bfloat16)
    placed = placement(cluster_ref[...], flip_ref[0, 0]).astype(jnp.float32)
    slots = jnp.dot(placed.astype(jnp.bfloat16), unit, preferred_element_type=jnp.float32)
    used = jnp.sum(placed, axis=1, keepdims=True)
    first = lax.broadcasted_iota(jnp.int32, slots.shape, 1) == 0
    slots = jnp.where(first & (used < 0.5), EMPTY, slots).astype(jnp.bfloat16)
    count = SLOTS // len(out_refs)
    for block, out_ref in enumerate(out_refs):
        out_ref[...] = slots[block * count : (block + 1) * count]


def pack(flip, embeddings, assignment, blocks):
    rows, width = embeddings.shape
    return pl.pallas_call(
        pack_kernel,
        out_shape=[jax.ShapeDtypeStruct((SLOTS // blocks, width), jnp.bfloat16)] * blocks,
        in_specs=[SMEM, VMEM, VMEM],
        out_specs=[VMEM] * blocks,
        name="pack",
    )(flip, embeddings, assignment.reshape(1, rows))


def shared_best_kernel(count, first_ref, slots_ref, others_ref, out_ref, best_ref):
    step = pl.program_id(0)
    slots, others = slots_ref[...], others_ref[...]
    similar = lax.dot_general(
        others, slots, (((1,), (1,)), ((), ())), preferred_element_type=jnp.float32
    )
    used = others[:, :1].astype(jnp.float32) < 2.0
    row = lax.broadcasted_iota(jnp.int32, similar.shape, 0)
    column = lax.broadcasted_iota(jnp.int32, similar.shape, 1)
    kept = used & (row + step * slots.shape[0] != column + first_ref[0, 0])
    kept = kept & (row % count // CAP == column % count // CAP)
    best = jnp.max(jnp.where(kept, similar, NONE), axis=0, keepdims=True)

    @pl.when(step == 0)
    def _():
        best_ref[...] = best

    @pl.when(step > 0)
    def _():
        best_ref[...] = jnp.maximum(best_ref[...], best)

    @pl.when(step == pl.num_programs(0) - 1)
    def _():
        for source in range(out_ref.shape[0]):
            piece = best_ref[:, source * count : (source + 1) * count]
            out_ref[source, :, :count] = jnp.broadcast_to(piece, (8, count))
            if count < LANES:
                out_ref[source, :, count:] = jnp.full((8, LANES - count), NONE)


def shared_best_of(slots, others, first, owners):
    size, width = slots.shape
    return pl.pallas_call(
        functools.partial(shared_best_kernel, size // owners),
        grid=(others.shape[0] // size,),
        out_shape=jax.ShapeDtypeStruct((owners, 8, LANES), jnp.float32),
        in_specs=[
            pl.BlockSpec((1, 1), lambda i: (0, 0), memory_space=pltpu.SMEM),
            pl.BlockSpec((size, width), lambda i: (0, 0)),
            pl.BlockSpec((size, width), lambda i: (i, 0)),
        ],
        out_specs=pl.BlockSpec((owners, 8, LANES), lambda i: (0, 0, 0)),
        scratch_shapes=[pltpu.VMEM((1, size), jnp.float32)],
        name="shared_best",
    )(first, slots, others)


def unpack_kernel(flip_ref, cluster_ref, *refs):
    returned_refs, out_ref = refs[:-1], refs[-1]
    count = SLOTS // len(returned_refs)
    placed = placement(cluster_ref[...], flip_ref[0, 0])
    returned = jnp.concatenate(
        [jnp.broadcast_to(ref[:1, :], (count, LANES)) for ref in returned_refs], axis=0
    )
    slot = lax.broadcasted_iota(jnp.int32, (SLOTS, LANES), 0) % count
    lane = lax.broadcasted_iota(jnp.int32, (SLOTS, LANES), 1)
    by_slot = jnp.max(jnp.where(slot == lane, returned, NONE), axis=1, keepdims=True)
    out_ref[...] = jnp.max(jnp.where(placed, by_slot, NONE), axis=0, keepdims=True)


def unpack(flip, returned, assignment):
    rows = assignment.shape[0]
    return pl.pallas_call(
        unpack_kernel,
        out_shape=jax.ShapeDtypeStruct((1, rows), jnp.float32),
        in_specs=[SMEM, VMEM] + [VMEM] * len(returned),
        out_specs=VMEM,
        name="unpack",
    )(flip, assignment.reshape(1, rows), *returned).reshape(-1)


def unit_of(values):
    values = values.astype(jnp.float32)
    scaled = values * lax.rsqrt(jnp.mean(values * values, axis=1, keepdims=True) + 1e-06)
    return (scaled * (1.0 / math.sqrt(values.shape[1]))).astype(jnp.bfloat16)


def best_of(own, own_clusters, others, other_clusters, same_rows=False):
    best = None
    for place, (rows, clusters) in enumerate(zip(others, other_clusters)):
        count = rows.shape[0]
        similar = lax.dot_general(
            rows, own, (((1,), (1,)), ((), ())), preferred_element_type=jnp.float32
        )
        down = jnp.broadcast_to(clusters, (count, count)).T[:, :1]
        kept = down == own_clusters
        if same_rows and place == 0:
            row = lax.broadcasted_iota(jnp.int32, similar.shape, 0)
            column = lax.broadcasted_iota(jnp.int32, similar.shape, 1)
            kept = kept & (row != column)
        found = jnp.max(jnp.where(kept, similar, NONE), axis=0, keepdims=True)
        best = found if best is None else jnp.maximum(best, found)
    return best


def block(refs):
    return jnp.concatenate([unit_of(ref[...]) for ref in refs], axis=0)


def early_kernel(
    mine_ref, x_refs, e_refs, c_refs, h_refs, ids_ref, x_ids_ref, c_ids_ref, e_ids_ref, h_ids_ref,
    best_ref, own_ref, far_ref,
):
    mine, c, h = unit_of(mine_ref[...]), block(c_refs), block(h_refs)
    own = jnp.concatenate([mine, block(x_refs), block(e_refs)], axis=0)
    own_ids = jnp.concatenate([ids_ref[...], x_ids_ref[...], e_ids_ref[:1, :]], axis=1)
    other_ids = [ids_ref[...], c_ids_ref[...], h_ids_ref[:1, :]]
    best_ref[...] = jnp.broadcast_to(best_of(own, own_ids, [mine, c, h], other_ids, True), best_ref.shape)
    own_ref[...] = own
    far_ref[...] = jnp.concatenate([mine, c, h], axis=0)


def early(mine, x, e, c, h, ids):
    rows, width = mine.shape
    return pl.pallas_call(
        early_kernel,
        out_shape=[
            jax.ShapeDtypeStruct((8, 3 * rows), jnp.float32),
            jax.ShapeDtypeStruct((3 * rows, width), jnp.bfloat16),
            jax.ShapeDtypeStruct((3 * rows, width), jnp.bfloat16),
        ],
        in_specs=(
            VMEM, [VMEM] * len(x), [VMEM] * len(e), [VMEM] * len(c), [VMEM] * len(h), *[VMEM] * len(ids)
        ),
        out_specs=[VMEM] * 3,
        compiler_params=LIMIT,
        name="early",
    )(mine, x, e, c, h, *ids)


def middle_kernel(
    best_ref, own_ref, near_ref, ch_refs, ids_ref, x_ids_ref, e_ids_ref, h_ids_ref,
    mine_out_ref, x_out_ref, e_out_ref, far_ref,
):
    ch = block(ch_refs)
    own_ids = jnp.concatenate([ids_ref[...], x_ids_ref[...], e_ids_ref[:1, :]], axis=1)
    best = best_of(own_ref[...], own_ids, [ch], [h_ids_ref[1:, :]])
    best = jnp.maximum(best, best_ref[:1, :])
    rows = ch.shape[0]
    for place, out_ref in enumerate((mine_out_ref, x_out_ref, e_out_ref)):
        out_ref[...] = jnp.broadcast_to(best[:, place * rows : (place + 1) * rows], out_ref.shape)
    far_ref[...] = jnp.concatenate([near_ref[...], ch], axis=0)


def middle(best, own, near, ch, ids):
    rows, width = own.shape[0] // 3, own.shape[1]
    return pl.pallas_call(
        middle_kernel,
        out_shape=[jax.ShapeDtypeStruct((8, rows), jnp.float32)] * 3
        + [jax.ShapeDtypeStruct((4 * rows, width), jnp.bfloat16)],
        in_specs=(VMEM, VMEM, VMEM, [VMEM] * len(ch), *[VMEM] * len(ids)),
        out_specs=[VMEM] * 4,
        compiler_params=LIMIT,
        name="middle",
    )(best, own, near, ch, *ids)


def late_kernel(far_ref, xe_refs, ids_ref, c_ids_ref, e_ids_ref, h_ids_ref, out_ref):
    xe = block(xe_refs)
    rows = xe.shape[0]
    others = [far_ref[place * rows : (place + 1) * rows] for place in range(4)]
    other_ids = [ids_ref[...], c_ids_ref[...], h_ids_ref[:1, :], h_ids_ref[1:, :]]
    out_ref[...] = jnp.broadcast_to(best_of(xe, e_ids_ref[1:, :], others, other_ids), out_ref.shape)


def late(far, xe, ids):
    return pl.pallas_call(
        late_kernel,
        out_shape=jax.ShapeDtypeStruct((8, far.shape[0] // 4), jnp.float32),
        in_specs=(VMEM, [VMEM] * len(xe), *[VMEM] * len(ids)),
        out_specs=VMEM,
        compiler_params=LIMIT,
        name="late",
    )(far, xe, *ids)


def square(embeddings, assignment):
    def swap(flip, array):
        return lax.ppermute(array, AXES, [(i, i ^ flip) for i in range(16)])

    rows = embeddings.shape[0]
    mine, ids = embeddings, assignment.reshape(1, rows)
    c = swap(SUB, mine)
    e = swap(LOW, mine)
    x = swap(SHARD, mine)
    far, _ = lax.optimization_barrier((mine, c))
    h = swap(HIGH, far)
    x_ids, c_ids = swap(SHARD, ids), swap(SUB, ids)
    e_ids = swap(LOW, jnp.concatenate([ids, x_ids]))
    h_ids = swap(HIGH, jnp.concatenate([ids, c_ids]))
    xe = swap(SHARD, e)
    h_then, _, _, _ = lax.optimization_barrier((h, h_ids, e_ids, x))
    ch = [swap(SUB, h_then[: rows // 2]), swap(SUB, h_then[rows // 2 :])]
    x, e, h, c, xe = [x], [e], [h], [c], [xe]
    best, own, near = early(mine, x, e, c, h, [ids, x_ids, c_ids, e_ids, h_ids])
    found, x_best, e_best, far = middle(best, own, near, ch, [ids, x_ids, e_ids, h_ids])
    x_best, e_best = swap(SHARD, x_best), swap(LOW, e_best)
    xe_best = swap(LOW | SHARD, late(far, xe, [ids, c_ids, e_ids, h_ids]))
    return jnp.maximum(jnp.maximum(found, x_best), jnp.maximum(e_best, xe_best))[0]


def shared_owner(embeddings, assignment):
    route, gather = AXES[:1], AXES[1:]
    owners = lax.axis_size(route)
    flip = jnp.zeros((1, 1), jnp.int32)
    (sent,) = pack(flip, embeddings, assignment, 1)
    got = lax.all_to_all(sent, route, split_axis=0, concat_axis=0, tiled=True)
    others = lax.all_gather(got, gather, axis=0, tiled=True)
    first = (lax.axis_index(gather) * SLOTS).astype(jnp.int32).reshape(1, 1)
    best = shared_best_of(got, others, first, owners)
    returned = lax.all_to_all(best, route, split_axis=0, concat_axis=0, tiled=True)
    return unpack(flip, [returned[i] for i in range(owners)], assignment)


def solution(mesh):
    placed = (
        P(("groups", "blk", "shard", "sub"), None),
        P(("groups", "blk", "shard", "sub"), None),
    )
    four_bits = [mesh.shape[axis] for axis in AXES] == [4, 2, 2]
    program = square if four_bits else shared_owner
    return jax.shard_map(
        program,
        mesh=mesh,
        in_specs=placed,
        out_specs=P(("groups", "blk", "shard", "sub")),
        check_vma=False,
    )
```

```python
import functools
import math

import jax
import jax.numpy as jnp
from jax import lax
from jax.experimental import pallas as pl
from jax.experimental.pallas import tpu as pltpu
from jax.sharding import PartitionSpec as P

CLUSTERS = 16
CAP = 16
SLOTS = CLUSTERS * CAP
LANES = 128
EMPTY = 4.0
NONE = -2.0
HIGH, LOW, SHARD, SUB = 8, 4, 2, 1
LIMIT = pltpu.CompilerParams(vmem_limit_bytes=12 << 20)
AXES = ("blk", "shard", "sub")

VMEM = pl.BlockSpec(memory_space=pltpu.VMEM)
SMEM = pl.BlockSpec(memory_space=pltpu.SMEM)


def placement(cluster, flip):
    rows = cluster.shape[1]
    label = lax.broadcasted_iota(jnp.int32, (CLUSTERS, rows), 0)
    member = (cluster == label).astype(jnp.float32)
    before = lax.broadcasted_iota(jnp.int32, (rows, rows), 0) < lax.broadcasted_iota(
        jnp.int32, (rows, rows), 1
    )
    earlier = jnp.dot(
        member.astype(jnp.bfloat16),
        before.astype(jnp.float32).astype(jnp.bfloat16),
        preferred_element_type=jnp.float32,
    )
    within = jnp.sum(earlier * member, axis=0, keepdims=True).astype(jnp.int32)
    target = (cluster ^ flip) * CAP + within
    return lax.broadcasted_iota(jnp.int32, (SLOTS, rows), 0) == target


def pack_kernel(flip_ref, rows_ref, cluster_ref, *out_refs):
    values = rows_ref[...].astype(jnp.float32)
    width = values.shape[1]
    scaled = values * lax.rsqrt(jnp.mean(values * values, axis=1, keepdims=True) + 1e-06)
    unit = (scaled * (1.0 / math.sqrt(width))).astype(jnp.bfloat16)
    placed = placement(cluster_ref[...], flip_ref[0, 0]).astype(jnp.float32)
    slots = jnp.dot(placed.astype(jnp.bfloat16), unit, preferred_element_type=jnp.float32)
    used = jnp.sum(placed, axis=1, keepdims=True)
    first = lax.broadcasted_iota(jnp.int32, slots.shape, 1) == 0
    slots = jnp.where(first & (used < 0.5), EMPTY, slots).astype(jnp.bfloat16)
    count = SLOTS // len(out_refs)
    for block, out_ref in enumerate(out_refs):
        out_ref[...] = slots[block * count : (block + 1) * count]


def pack(flip, embeddings, assignment, blocks):
    rows, width = embeddings.shape
    return pl.pallas_call(
        pack_kernel,
        out_shape=[jax.ShapeDtypeStruct((SLOTS // blocks, width), jnp.bfloat16)] * blocks,
        in_specs=[SMEM, VMEM, VMEM],
        out_specs=[VMEM] * blocks,
        name="pack",
    )(flip, embeddings, assignment.reshape(1, rows))


def shared_best_kernel(count, first_ref, slots_ref, others_ref, out_ref, best_ref):
    step = pl.program_id(0)
    slots, others = slots_ref[...], others_ref[...]
    similar = lax.dot_general(
        others, slots, (((1,), (1,)), ((), ())), preferred_element_type=jnp.float32
    )
    used = others[:, :1].astype(jnp.float32) < 2.0
    row = lax.broadcasted_iota(jnp.int32, similar.shape, 0)
    column = lax.broadcasted_iota(jnp.int32, similar.shape, 1)
    kept = used & (row + step * slots.shape[0] != column + first_ref[0, 0])
    kept = kept & (row % count // CAP == column % count // CAP)
    best = jnp.max(jnp.where(kept, similar, NONE), axis=0, keepdims=True)

    @pl.when(step == 0)
    def _():
        best_ref[...] = best

    @pl.when(step > 0)
    def _():
        best_ref[...] = jnp.maximum(best_ref[...], best)

    @pl.when(step == pl.num_programs(0) - 1)
    def _():
        for source in range(out_ref.shape[0]):
            piece = best_ref[:, source * count : (source + 1) * count]
            out_ref[source, :, :count] = jnp.broadcast_to(piece, (8, count))
            if count < LANES:
                out_ref[source, :, count:] = jnp.full((8, LANES - count), NONE)


def shared_best_of(slots, others, first, owners):
    size, width = slots.shape
    return pl.pallas_call(
        functools.partial(shared_best_kernel, size // owners),
        grid=(others.shape[0] // size,),
        out_shape=jax.ShapeDtypeStruct((owners, 8, LANES), jnp.float32),
        in_specs=[
            pl.BlockSpec((1, 1), lambda i: (0, 0), memory_space=pltpu.SMEM),
            pl.BlockSpec((size, width), lambda i: (0, 0)),
            pl.BlockSpec((size, width), lambda i: (i, 0)),
        ],
        out_specs=pl.BlockSpec((owners, 8, LANES), lambda i: (0, 0, 0)),
        scratch_shapes=[pltpu.VMEM((1, size), jnp.float32)],
        name="shared_best",
    )(first, slots, others)


def unpack_kernel(flip_ref, cluster_ref, *refs):
    returned_refs, out_ref = refs[:-1], refs[-1]
    count = SLOTS // len(returned_refs)
    placed = placement(cluster_ref[...], flip_ref[0, 0])
    returned = jnp.concatenate(
        [jnp.broadcast_to(ref[:1, :], (count, LANES)) for ref in returned_refs], axis=0
    )
    slot = lax.broadcasted_iota(jnp.int32, (SLOTS, LANES), 0) % count
    lane = lax.broadcasted_iota(jnp.int32, (SLOTS, LANES), 1)
    by_slot = jnp.max(jnp.where(slot == lane, returned, NONE), axis=1, keepdims=True)
    out_ref[...] = jnp.max(jnp.where(placed, by_slot, NONE), axis=0, keepdims=True)


def unpack(flip, returned, assignment):
    rows = assignment.shape[0]
    return pl.pallas_call(
        unpack_kernel,
        out_shape=jax.ShapeDtypeStruct((1, rows), jnp.float32),
        in_specs=[SMEM, VMEM] + [VMEM] * len(returned),
        out_specs=VMEM,
        name="unpack",
    )(flip, assignment.reshape(1, rows), *returned).reshape(-1)


def unit_of(values):
    values = values.astype(jnp.float32)
    scaled = values * lax.rsqrt(jnp.mean(values * values, axis=1, keepdims=True) + 1e-06)
    return (scaled * (1.0 / math.sqrt(values.shape[1]))).astype(jnp.bfloat16)


def best_of(own, own_clusters, others, other_clusters, same_rows=False):
    best = None
    for place, (rows, clusters) in enumerate(zip(others, other_clusters)):
        count = rows.shape[0]
        similar = lax.dot_general(
            rows, own, (((1,), (1,)), ((), ())), preferred_element_type=jnp.float32
        )
        down = jnp.broadcast_to(clusters, (count, count)).T[:, :1]
        kept = down == own_clusters
        if same_rows and place == 0:
            row = lax.broadcasted_iota(jnp.int32, similar.shape, 0)
            column = lax.broadcasted_iota(jnp.int32, similar.shape, 1)
            kept = kept & (row != column)
        found = jnp.max(jnp.where(kept, similar, NONE), axis=0, keepdims=True)
        best = found if best is None else jnp.maximum(best, found)
    return best


def block(refs):
    return jnp.concatenate([unit_of(ref[...]) for ref in refs], axis=0)


def early_kernel(mine_ref, x_refs, e_refs, c_refs, ids_ref, x_ids_ref, c_ids_ref, e_ids_ref, best_ref, own_ref, c_ref):
    mine, c = unit_of(mine_ref[...]), block(c_refs)
    own = jnp.concatenate([mine, block(x_refs), block(e_refs)], axis=0)
    own_ids = jnp.concatenate([ids_ref[...], x_ids_ref[...], e_ids_ref[:1, :]], axis=1)
    best = best_of(own, own_ids, [mine, c], [ids_ref[...], c_ids_ref[...]], True)
    best_ref[...] = jnp.broadcast_to(best, best_ref.shape)
    own_ref[...] = own
    c_ref[...] = c


def early(mine, x, e, c, ids):
    rows, width = mine.shape
    return pl.pallas_call(
        early_kernel,
        out_shape=[
            jax.ShapeDtypeStruct((8, 3 * rows), jnp.float32),
            jax.ShapeDtypeStruct((3 * rows, width), jnp.bfloat16),
            jax.ShapeDtypeStruct((rows, width), jnp.bfloat16),
        ],
        in_specs=(VMEM, [VMEM] * len(x), [VMEM] * len(e), [VMEM] * len(c), *[VMEM] * len(ids)),
        out_specs=[VMEM] * 3,
        compiler_params=LIMIT,
        name="early",
    )(mine, x, e, c, *ids)


def middle_kernel(
    best_ref, own_ref, c_ref, h_refs, ch_refs, ids_ref, x_ids_ref, c_ids_ref, e_ids_ref, h_ids_ref,
    mine_out_ref, x_out_ref, e_out_ref, far_ref,
):
    h, ch = block(h_refs), block(ch_refs)
    own_ids = jnp.concatenate([ids_ref[...], x_ids_ref[...], e_ids_ref[:1, :]], axis=1)
    best = best_of(own_ref[...], own_ids, [h, ch], [h_ids_ref[:1, :], h_ids_ref[1:, :]])
    best = jnp.maximum(best, best_ref[:1, :])
    rows = c_ref.shape[0]
    for place, out_ref in enumerate((mine_out_ref, x_out_ref, e_out_ref)):
        out_ref[...] = jnp.broadcast_to(best[:, place * rows : (place + 1) * rows], out_ref.shape)
    far_ref[...] = jnp.concatenate([own_ref[:rows], c_ref[...], h, ch], axis=0)


def middle(best, own, c, h, ch, ids):
    rows, width = c.shape
    return pl.pallas_call(
        middle_kernel,
        out_shape=[jax.ShapeDtypeStruct((8, rows), jnp.float32)] * 3
        + [jax.ShapeDtypeStruct((4 * rows, width), jnp.bfloat16)],
        in_specs=(VMEM, VMEM, VMEM, [VMEM] * len(h), [VMEM] * len(ch), *[VMEM] * len(ids)),
        out_specs=[VMEM] * 4,
        compiler_params=LIMIT,
        name="middle",
    )(best, own, c, h, ch, *ids)


def late_kernel(far_ref, xe_refs, ids_ref, c_ids_ref, e_ids_ref, h_ids_ref, out_ref):
    xe = block(xe_refs)
    rows = xe.shape[0]
    similar = lax.dot_general(
        far_ref[...], xe, (((1,), (1,)), ((), ())), preferred_element_type=jnp.float32
    )
    ids = [ids_ref[...], c_ids_ref[...], h_ids_ref[:1, :], h_ids_ref[1:, :]]
    down = jnp.concatenate([jnp.broadcast_to(row, (rows, rows)).T[:, :1] for row in ids], axis=0)
    best = jnp.max(jnp.where(down == e_ids_ref[1:, :], similar, NONE), axis=0, keepdims=True)
    out_ref[...] = jnp.broadcast_to(best, out_ref.shape)


def late(far, xe, ids):
    return pl.pallas_call(
        late_kernel,
        out_shape=jax.ShapeDtypeStruct((8, far.shape[0] // 4), jnp.float32),
        in_specs=(VMEM, [VMEM] * len(xe), *[VMEM] * len(ids)),
        out_specs=VMEM,
        compiler_params=LIMIT,
        name="late",
    )(far, xe, *ids)


def square(embeddings, assignment):
    def swap(flip, array):
        return lax.ppermute(array, AXES, [(i, i ^ flip) for i in range(16)])

    rows = embeddings.shape[0]
    mine, ids = embeddings, assignment.reshape(1, rows)
    c = swap(SUB, mine)
    e = swap(LOW, mine)
    x = swap(SHARD, mine)
    far, _ = lax.optimization_barrier((mine, c))
    h = swap(HIGH, far)
    x_ids, c_ids = swap(SHARD, ids), swap(SUB, ids)
    e_ids = swap(LOW, jnp.concatenate([ids, x_ids]))
    h_ids = swap(HIGH, jnp.concatenate([ids, c_ids]))
    xe = swap(SHARD, e)
    h_then, _, _, _ = lax.optimization_barrier((h, h_ids, e_ids, x))
    ch = [swap(SUB, h_then[: rows // 2]), swap(SUB, h_then[rows // 2 :])]
    x, e, h, c, xe = [x], [e], [h], [c], [xe]
    best, own, c = early(mine, x, e, c, [ids, x_ids, c_ids, e_ids])
    found, x_best, e_best, far = middle(best, own, c, h, ch, [ids, x_ids, c_ids, e_ids, h_ids])
    x_best, e_best = swap(SHARD, x_best), swap(LOW, e_best)
    xe_best = swap(LOW | SHARD, late(far, xe, [ids, c_ids, e_ids, h_ids]))
    return jnp.maximum(jnp.maximum(found, x_best), jnp.maximum(e_best, xe_best))[0]


def shared_owner(embeddings, assignment):
    route, gather = AXES[:1], AXES[1:]
    owners = lax.axis_size(route)
    flip = jnp.zeros((1, 1), jnp.int32)
    (sent,) = pack(flip, embeddings, assignment, 1)
    got = lax.all_to_all(sent, route, split_axis=0, concat_axis=0, tiled=True)
    others = lax.all_gather(got, gather, axis=0, tiled=True)
    first = (lax.axis_index(gather) * SLOTS).astype(jnp.int32).reshape(1, 1)
    best = shared_best_of(got, others, first, owners)
    returned = lax.all_to_all(best, route, split_axis=0, concat_axis=0, tiled=True)
    return unpack(flip, [returned[i] for i in range(owners)], assignment)


def solution(mesh):
    placed = (
        P(("groups", "blk", "shard", "sub"), None),
        P(("groups", "blk", "shard", "sub"), None),
    )
    four_bits = [mesh.shape[axis] for axis in AXES] == [4, 2, 2]
    program = square if four_bits else shared_owner
    return jax.shard_map(
        program,
        mesh=mesh,
        in_specs=placed,
        out_specs=P(("groups", "blk", "shard", "sub")),
        check_vma=False,
    )
```

```python
import functools
import math

import jax
import jax.numpy as jnp
from jax import lax
from jax.experimental import pallas as pl
from jax.experimental.pallas import tpu as pltpu
from jax.sharding import PartitionSpec as P

CLUSTERS = 16
CAP = 16
SLOTS = CLUSTERS * CAP
LANES = 128
EMPTY = 4.0
NONE = -2.0
HIGH, LOW, SHARD, SUB = 8, 4, 2, 1
LIMIT = pltpu.CompilerParams(vmem_limit_bytes=12 << 20)
AXES = ("blk", "shard", "sub")

VMEM = pl.BlockSpec(memory_space=pltpu.VMEM)
SMEM = pl.BlockSpec(memory_space=pltpu.SMEM)


def placement(cluster, flip):
    rows = cluster.shape[1]
    label = lax.broadcasted_iota(jnp.int32, (CLUSTERS, rows), 0)
    member = (cluster == label).astype(jnp.float32)
    before = lax.broadcasted_iota(jnp.int32, (rows, rows), 0) < lax.broadcasted_iota(
        jnp.int32, (rows, rows), 1
    )
    earlier = jnp.dot(
        member.astype(jnp.bfloat16),
        before.astype(jnp.float32).astype(jnp.bfloat16),
        preferred_element_type=jnp.float32,
    )
    within = jnp.sum(earlier * member, axis=0, keepdims=True).astype(jnp.int32)
    target = (cluster ^ flip) * CAP + within
    return lax.broadcasted_iota(jnp.int32, (SLOTS, rows), 0) == target


def pack_kernel(flip_ref, rows_ref, cluster_ref, *out_refs):
    values = rows_ref[...].astype(jnp.float32)
    width = values.shape[1]
    scaled = values * lax.rsqrt(jnp.mean(values * values, axis=1, keepdims=True) + 1e-06)
    unit = (scaled * (1.0 / math.sqrt(width))).astype(jnp.bfloat16)
    placed = placement(cluster_ref[...], flip_ref[0, 0]).astype(jnp.float32)
    slots = jnp.dot(placed.astype(jnp.bfloat16), unit, preferred_element_type=jnp.float32)
    used = jnp.sum(placed, axis=1, keepdims=True)
    first = lax.broadcasted_iota(jnp.int32, slots.shape, 1) == 0
    slots = jnp.where(first & (used < 0.5), EMPTY, slots).astype(jnp.bfloat16)
    count = SLOTS // len(out_refs)
    for block, out_ref in enumerate(out_refs):
        out_ref[...] = slots[block * count : (block + 1) * count]


def pack(flip, embeddings, assignment, blocks):
    rows, width = embeddings.shape
    return pl.pallas_call(
        pack_kernel,
        out_shape=[jax.ShapeDtypeStruct((SLOTS // blocks, width), jnp.bfloat16)] * blocks,
        in_specs=[SMEM, VMEM, VMEM],
        out_specs=[VMEM] * blocks,
        name="pack",
    )(flip, embeddings, assignment.reshape(1, rows))


def shared_best_kernel(count, first_ref, slots_ref, others_ref, out_ref, best_ref):
    step = pl.program_id(0)
    slots, others = slots_ref[...], others_ref[...]
    similar = lax.dot_general(
        others, slots, (((1,), (1,)), ((), ())), preferred_element_type=jnp.float32
    )
    used = others[:, :1].astype(jnp.float32) < 2.0
    row = lax.broadcasted_iota(jnp.int32, similar.shape, 0)
    column = lax.broadcasted_iota(jnp.int32, similar.shape, 1)
    kept = used & (row + step * slots.shape[0] != column + first_ref[0, 0])
    kept = kept & (row % count // CAP == column % count // CAP)
    best = jnp.max(jnp.where(kept, similar, NONE), axis=0, keepdims=True)

    @pl.when(step == 0)
    def _():
        best_ref[...] = best

    @pl.when(step > 0)
    def _():
        best_ref[...] = jnp.maximum(best_ref[...], best)

    @pl.when(step == pl.num_programs(0) - 1)
    def _():
        for source in range(out_ref.shape[0]):
            piece = best_ref[:, source * count : (source + 1) * count]
            out_ref[source, :, :count] = jnp.broadcast_to(piece, (8, count))
            if count < LANES:
                out_ref[source, :, count:] = jnp.full((8, LANES - count), NONE)


def shared_best_of(slots, others, first, owners):
    size, width = slots.shape
    return pl.pallas_call(
        functools.partial(shared_best_kernel, size // owners),
        grid=(others.shape[0] // size,),
        out_shape=jax.ShapeDtypeStruct((owners, 8, LANES), jnp.float32),
        in_specs=[
            pl.BlockSpec((1, 1), lambda i: (0, 0), memory_space=pltpu.SMEM),
            pl.BlockSpec((size, width), lambda i: (0, 0)),
            pl.BlockSpec((size, width), lambda i: (i, 0)),
        ],
        out_specs=pl.BlockSpec((owners, 8, LANES), lambda i: (0, 0, 0)),
        scratch_shapes=[pltpu.VMEM((1, size), jnp.float32)],
        name="shared_best",
    )(first, slots, others)


def unpack_kernel(flip_ref, cluster_ref, *refs):
    returned_refs, out_ref = refs[:-1], refs[-1]
    count = SLOTS // len(returned_refs)
    placed = placement(cluster_ref[...], flip_ref[0, 0])
    returned = jnp.concatenate(
        [jnp.broadcast_to(ref[:1, :], (count, LANES)) for ref in returned_refs], axis=0
    )
    slot = lax.broadcasted_iota(jnp.int32, (SLOTS, LANES), 0) % count
    lane = lax.broadcasted_iota(jnp.int32, (SLOTS, LANES), 1)
    by_slot = jnp.max(jnp.where(slot == lane, returned, NONE), axis=1, keepdims=True)
    out_ref[...] = jnp.max(jnp.where(placed, by_slot, NONE), axis=0, keepdims=True)


def unpack(flip, returned, assignment):
    rows = assignment.shape[0]
    return pl.pallas_call(
        unpack_kernel,
        out_shape=jax.ShapeDtypeStruct((1, rows), jnp.float32),
        in_specs=[SMEM, VMEM] + [VMEM] * len(returned),
        out_specs=VMEM,
        name="unpack",
    )(flip, assignment.reshape(1, rows), *returned).reshape(-1)


def unit_of(values):
    values = values.astype(jnp.float32)
    scaled = values * lax.rsqrt(jnp.mean(values * values, axis=1, keepdims=True) + 1e-06)
    return (scaled * (1.0 / math.sqrt(values.shape[1]))).astype(jnp.bfloat16)


def best_of(own, own_clusters, others, other_clusters, same_rows=False):
    best = None
    for place, (rows, clusters) in enumerate(zip(others, other_clusters)):
        count = rows.shape[0]
        similar = lax.dot_general(
            rows, own, (((1,), (1,)), ((), ())), preferred_element_type=jnp.float32
        )
        down = jnp.broadcast_to(clusters, (count, count)).T[:, :1]
        kept = down == own_clusters
        if same_rows and place == 0:
            row = lax.broadcasted_iota(jnp.int32, similar.shape, 0)
            column = lax.broadcasted_iota(jnp.int32, similar.shape, 1)
            kept = kept & (row != column)
        found = jnp.max(jnp.where(kept, similar, NONE), axis=0, keepdims=True)
        best = found if best is None else jnp.maximum(best, found)
    return best


def block(refs):
    return jnp.concatenate([unit_of(ref[...]) for ref in refs], axis=0)


def early_kernel(mine_ref, x_refs, e_refs, c_refs, ids_ref, x_ids_ref, c_ids_ref, e_ids_ref, best_ref, own_ref, c_ref):
    mine, c = unit_of(mine_ref[...]), block(c_refs)
    own = jnp.concatenate([mine, block(x_refs), block(e_refs)], axis=0)
    own_ids = jnp.concatenate([ids_ref[...], x_ids_ref[...], e_ids_ref[:1, :]], axis=1)
    best = best_of(own, own_ids, [mine, c], [ids_ref[...], c_ids_ref[...]], True)
    best_ref[...] = jnp.broadcast_to(best, best_ref.shape)
    own_ref[...] = own
    c_ref[...] = c


def early(mine, x, e, c, ids):
    rows, width = mine.shape
    return pl.pallas_call(
        early_kernel,
        out_shape=[
            jax.ShapeDtypeStruct((8, 3 * rows), jnp.float32),
            jax.ShapeDtypeStruct((3 * rows, width), jnp.bfloat16),
            jax.ShapeDtypeStruct((rows, width), jnp.bfloat16),
        ],
        in_specs=(VMEM, [VMEM] * len(x), [VMEM] * len(e), [VMEM] * len(c), *[VMEM] * len(ids)),
        out_specs=[VMEM] * 3,
        compiler_params=LIMIT,
        name="early",
    )(mine, x, e, c, *ids)


def middle_kernel(
    best_ref, own_ref, c_ref, h_refs, ch_refs, ids_ref, x_ids_ref, c_ids_ref, e_ids_ref, h_ids_ref,
    mine_out_ref, x_out_ref, e_out_ref, far_ref,
):
    h, ch = block(h_refs), block(ch_refs)
    own_ids = jnp.concatenate([ids_ref[...], x_ids_ref[...], e_ids_ref[:1, :]], axis=1)
    best = best_of(own_ref[...], own_ids, [h, ch], [h_ids_ref[:1, :], h_ids_ref[1:, :]])
    best = jnp.maximum(best, best_ref[:1, :])
    rows = c_ref.shape[0]
    for place, out_ref in enumerate((mine_out_ref, x_out_ref, e_out_ref)):
        out_ref[...] = jnp.broadcast_to(best[:, place * rows : (place + 1) * rows], out_ref.shape)
    far_ref[...] = jnp.concatenate([own_ref[:rows], c_ref[...], h, ch], axis=0)


def middle(best, own, c, h, ch, ids):
    rows, width = c.shape
    return pl.pallas_call(
        middle_kernel,
        out_shape=[jax.ShapeDtypeStruct((1, rows), jnp.float32)] * 3
        + [jax.ShapeDtypeStruct((4 * rows, width), jnp.bfloat16)],
        in_specs=(VMEM, VMEM, VMEM, [VMEM] * len(h), [VMEM] * len(ch), *[VMEM] * len(ids)),
        out_specs=[VMEM] * 4,
        compiler_params=LIMIT,
        name="middle",
    )(best, own, c, h, ch, *ids)


def late_kernel(far_ref, xe_refs, ids_ref, c_ids_ref, e_ids_ref, h_ids_ref, out_ref):
    xe = block(xe_refs)
    rows = xe.shape[0]
    others = [far_ref[place * rows : (place + 1) * rows] for place in range(4)]
    other_ids = [ids_ref[...], c_ids_ref[...], h_ids_ref[:1, :], h_ids_ref[1:, :]]
    out_ref[...] = jnp.broadcast_to(best_of(xe, e_ids_ref[1:, :], others, other_ids), out_ref.shape)


def late(far, xe, ids):
    return pl.pallas_call(
        late_kernel,
        out_shape=jax.ShapeDtypeStruct((1, far.shape[0] // 4), jnp.float32),
        in_specs=(VMEM, [VMEM] * len(xe), *[VMEM] * len(ids)),
        out_specs=VMEM,
        compiler_params=LIMIT,
        name="late",
    )(far, xe, *ids)


def square(embeddings, assignment):
    def swap(flip, array):
        return lax.ppermute(array, AXES, [(i, i ^ flip) for i in range(16)])

    rows = embeddings.shape[0]
    mine, ids = embeddings, assignment.reshape(1, rows)
    c = swap(SUB, mine)
    e = swap(LOW, mine)
    x = swap(SHARD, mine)
    far, _ = lax.optimization_barrier((mine, c))
    h = swap(HIGH, far)
    x_ids, c_ids = swap(SHARD, ids), swap(SUB, ids)
    e_ids = swap(LOW, jnp.concatenate([ids, x_ids]))
    h_ids = swap(HIGH, jnp.concatenate([ids, c_ids]))
    xe = swap(SHARD, e)
    h_then, _, _, _ = lax.optimization_barrier((h, h_ids, e_ids, x))
    ch = [swap(SUB, h_then[: rows // 2]), swap(SUB, h_then[rows // 2 :])]
    x, e, h, c, xe = [x], [e], [h], [c], [xe]
    best, own, c = early(mine, x, e, c, [ids, x_ids, c_ids, e_ids])
    found, x_best, e_best, far = middle(best, own, c, h, ch, [ids, x_ids, c_ids, e_ids, h_ids])
    x_best, e_best = swap(SHARD, x_best), swap(LOW, e_best)
    xe_best = swap(LOW | SHARD, late(far, xe, [ids, c_ids, e_ids, h_ids]))
    return jnp.maximum(jnp.maximum(found, x_best), jnp.maximum(e_best, xe_best))[0]


def shared_owner(embeddings, assignment):
    route, gather = AXES[:1], AXES[1:]
    owners = lax.axis_size(route)
    flip = jnp.zeros((1, 1), jnp.int32)
    (sent,) = pack(flip, embeddings, assignment, 1)
    got = lax.all_to_all(sent, route, split_axis=0, concat_axis=0, tiled=True)
    others = lax.all_gather(got, gather, axis=0, tiled=True)
    first = (lax.axis_index(gather) * SLOTS).astype(jnp.int32).reshape(1, 1)
    best = shared_best_of(got, others, first, owners)
    returned = lax.all_to_all(best, route, split_axis=0, concat_axis=0, tiled=True)
    return unpack(flip, [returned[i] for i in range(owners)], assignment)


def solution(mesh):
    placed = (
        P(("groups", "blk", "shard", "sub"), None),
        P(("groups", "blk", "shard", "sub"), None),
    )
    four_bits = [mesh.shape[axis] for axis in AXES] == [4, 2, 2]
    program = square if four_bits else shared_owner
    return jax.shard_map(
        program,
        mesh=mesh,
        in_specs=placed,
        out_specs=P(("groups", "blk", "shard", "sub")),
        check_vma=False,
    )
```
